32 devices in a mesh: inl: 8 (over y, x, core), xl: 4 (over z).
Axes of the slice: x: 2, y: 2, z: 4, core: 2. Of those that a mesh axis runs over, the one named last changes fastest.
Arguments:
- traces: bfloat16 [8192, 512], P(('inl', 'xl')), may hold values from -6 to 6
- trace_owner: int32 [8192, 1], P(('inl', 'xl')), may hold values from 0 to 31, as said below
- trace_cell: int32 [8192], P(('inl', 'xl')), may hold values from 0 to 1023, as said below
- acquired: int32 [8192], P(('inl', 'xl')), may hold values 0 or 1
- inline_dip: float32 [64, 512, 512], P('inl', 'xl'), may hold values from -1 to 1
- cross_dip: float32 [64, 512, 512], P('inl', 'xl'), may hold values from -1 to 1
Outputs:
- model: float32 [64, 512, 512], P('inl', 'xl')
- residual: float32 [64, 512, 512], P('inl', 'xl')
The draws below stay inside these ranges and needn't reach their ends.
Inputs may be any that keep to these rules, and one draw needn't show every extreme that they name: `trace_owner`: owners are numbered inline tile times n_xl plus crossline tile. Among the 256 traces of one device at most 16 name one owner, and some owner is named exactly 16 times by some device. `trace_cell`: bin within the owner's tile, crossline fastest; several traces may share a bin.
All inputs are finite; a program needn't handle non-finite values. No bound on the sum of `acquired` on one device may be relied on, other than what follows from the above.
Results may differ from the reference program's by a relative error of at most 0.0003.
Values may be sent and summed in bfloat16 or wider, within the bound.
No kernel may reach another device: no remote copies, remote signals or barrier semaphores. Data moves between devices by JAX's collectives and lax.ppermute only.
A program may use at most 128 MiB of HBM per device.

```python
import jax
import jax.numpy as jnp
from jax import lax

CI = 8
CX = 128
NT = 512
TR_DEV = 256
ITERS = 3
CAP = 16
NI = 64
NX = 512
TRACES = 8192
N_XL = 4
DEVICES = 32


def bins_of(key):
    slot_count = DEVICES * CAP
    slot_ids = jnp.arange(slot_count, dtype=jnp.int32)
    slot_owner = slot_ids // CAP
    tier_rank = jax.random.randint(jax.random.fold_in(key, 101), (DEVICES,), 0, 3)
    jitter = jax.random.randint(jax.random.fold_in(key, 102), (DEVICES, slot_count), 0, 4096)
    forced = jax.random.randint(jax.random.fold_in(key, 103), (DEVICES,), 0, DEVICES)
    forced_boost = jnp.where(slot_owner[None, :] == forced[:, None], 16384, 0)
    slot_score = tier_rank[slot_owner][None, :] * 2048 + jitter + forced_boost
    distinct = slot_score * slot_count + slot_ids[None, :]
    ranking = jnp.argsort(-distinct, axis=1)
    chosen = ranking[:, :TR_DEV]
    block_keys = jax.random.split(jax.random.fold_in(key, 104), DEVICES)

    def block_perm(block_key):
        return jax.random.permutation(block_key, TR_DEV)
    shuffle = jax.vmap(block_perm)(block_keys)
    chosen = jnp.take_along_axis(chosen, shuffle, axis=1)
    owner_ids = (chosen // CAP).reshape(TRACES).astype(jnp.int32)
    cell_ids = jax.random.randint(jax.random.fold_in(key, 105), (TRACES,), 0, CI * CX).astype(jnp.int32)
    return (owner_ids, cell_ids)


def keyed_rows(base_key, row_keys):

    def one_row(index):
        return jax.random.normal(jax.random.fold_in(base_key, index), (NT,), jnp.float32)
    return jax.vmap(one_row)(row_keys)


def draw_trace_owner(key, part):
    owner_ids, cell_ids = bins_of(key)
    return owner_ids[:, None]


def draw_trace_cell(key, part):
    owner_ids, cell_ids = bins_of(key)
    return cell_ids


def draw_traces(key, part):
    owner_ids, cell_ids = bins_of(key)
    key = jax.random.fold_in(key, 7)
    row_in = cell_ids // CX
    col_in = cell_ids % CX
    column_part = keyed_rows(jax.random.fold_in(key, 1), owner_ids * CX + col_in)
    row_part = keyed_rows(jax.random.fold_in(key, 2), owner_ids * CI + row_in)
    bin_part = keyed_rows(jax.random.fold_in(key, 3), owner_ids * (CI * CX) + cell_ids)
    trace_noise = jax.random.normal(jax.random.fold_in(key, 4), (TRACES, NT), jnp.float32)
    row_frac = row_in.astype(jnp.float32) / float(CI - 1)
    col_frac = col_in.astype(jnp.float32) / float(CX - 1)
    gain_curve = jnp.exp(0.8 * (2.0 * row_frac - 1.0) + 0.5 * (2.0 * col_frac - 1.0))
    sample_value = gain_curve[:, None] * (0.6 * (column_part + row_part + bin_part)) + 0.25 * trace_noise
    return (6.0 * jnp.tanh(sample_value / 6.0)).astype(jnp.bfloat16)


def plant(values, own_key, low, high):
    shape = values.shape
    index_at = [jax.random.randint(jax.random.fold_in(own_key, axis), (), 0, shape[axis]) for axis in range(len(shape))]
    values = values.at[tuple(index_at)].set(low)
    longest = shape.index(max(shape))
    index_at[longest] = (index_at[longest] + 1) % shape[longest]
    return values.at[tuple(index_at)].set(high)


def level_of(own_key, dims, cuts, low, top_value):
    factor_of = 1.0
    for position, shards_of in cuts:
        steps = jax.random.uniform(jax.random.fold_in(jax.random.fold_in(own_key, 6), position), (shards_of,), jnp.float32, low / len(cuts), top_value / len(cuts))
        factor_of = factor_of * jnp.repeat(jnp.exp(steps), dims[position] // shards_of).reshape((-1,) + (1,) * (len(dims) - 1 - position))
    return factor_of


def setup_inputs(seed: int = 0) -> dict:
    streams_of = jax.random.split(jax.random.key(seed), 7)
    traces = draw_traces(jax.random.fold_in(streams_of[6], 71), 0)
    trace_owner = draw_trace_owner(jax.random.fold_in(streams_of[6], 71), 0)
    trace_cell = draw_trace_cell(jax.random.fold_in(streams_of[6], 71), 0)
    acquired = plant((jax.random.randint(streams_of[3], (TRACES,), 0, 5) < 4).astype(jnp.int32), jax.random.fold_in(streams_of[3], 1), 0, 1)
    inline_dip = jnp.clip(jax.random.uniform(streams_of[4], (NI, NX, NT), jnp.float32, -1.0, 1.0) * level_of(streams_of[4], (NI, NX, NT), ((0, 8), (1, 4)), -0.4, 0.0), -1.0, 1.0)
    cross_dip = jnp.clip(jax.random.uniform(streams_of[5], (NI, NX, NT), jnp.float32, -1.0, 1.0) * level_of(streams_of[5], (NI, NX, NT), ((0, 8), (1, 4)), -0.4, 0.0), -1.0, 1.0)
    return dict(traces=traces, trace_owner=trace_owner, trace_cell=trace_cell, acquired=acquired, inline_dip=inline_dip, cross_dip=cross_dip)


reg_weight = 0.5


def time_earlier(field):
    return jnp.pad(field[:, :, :-1], ((0, 0), (0, 0), (1, 0)))


def time_later(field):
    return jnp.pad(field[:, :, 1:], ((0, 0), (0, 0), (0, 1)))


def lagrange(slope):
    return 0.5 * (slope * slope + slope), 1.0 - slope * slope, 0.5 * (slope * slope - slope)


def delay(field, slope):
    lower, centre, upper = lagrange(slope)
    return lower * time_earlier(field) + centre * field + upper * time_later(field)


def delay_adjoint(field, slope):
    lower, centre, upper = lagrange(slope)
    return time_earlier(upper * field) + centre * field + time_later(lower * field)


def following(field, axis):
    count = field.shape[axis]
    tail = lax.slice_in_dim(field, 1, count, axis=axis)
    return jnp.concatenate([tail, jnp.zeros_like(lax.slice_in_dim(field, 0, 1, axis=axis))], axis)


def preceding(field, axis):
    count = field.shape[axis]
    head = lax.slice_in_dim(field, 0, count - 1, axis=axis)
    return jnp.concatenate([jnp.zeros_like(lax.slice_in_dim(field, 0, 1, axis=axis)), head], axis)


def normal_apply(model, hits, inline_dip, cross_dip):
    first = following(model, 0) - delay(model, inline_dip)
    second = following(model, 1) - delay(model, cross_dip)
    smooth = preceding(first, 0) - delay_adjoint(first, inline_dip) + preceding(second, 1) - delay_adjoint(second, cross_dip)
    return hits * model + reg_weight * smooth


def reference(traces, trace_owner, trace_cell, acquired, inline_dip, cross_dip):
    owner = trace_owner[:, 0]
    inline_bin = (owner // N_XL) * CI + trace_cell // CX
    cross_bin = (owner % N_XL) * CX + trace_cell % CX
    flat_bin = (inline_bin * NX + cross_bin).astype(jnp.int32)
    live = (acquired > 0).astype(jnp.float32)
    data_sum = jax.ops.segment_sum(traces.astype(jnp.float32) * live[:, None], flat_bin, num_segments=NI * NX)
    data_sum = data_sum.reshape(NI, NX, NT)
    hits = jax.ops.segment_sum(live, flat_bin, num_segments=NI * NX).reshape(NI, NX, 1)
    model = jnp.zeros_like(data_sum)
    residual = data_sum
    direction = data_sum
    norm_now = jnp.sum(residual * residual)
    for sweep in range(ITERS):
        image = normal_apply(direction, hits, inline_dip, cross_dip)
        alpha = norm_now / jnp.sum(direction * image)
        model = model + alpha * direction
        residual = residual - alpha * image
        norm_next = jnp.sum(residual * residual)
        direction = residual + (norm_next / norm_now) * direction
        norm_now = norm_next
    return model, residual
```

```python
import functools

import jax
import jax.numpy as jnp
from jax import lax
from jax.experimental import pallas as pl
from jax.experimental.pallas import tpu as pltpu
from jax.sharding import PartitionSpec as P

ITERS = 3
LANES = 128
SUBLANES = 8

IN_VMEM = pl.BlockSpec(memory_space=pltpu.VMEM)
PARAMS = pltpu.CompilerParams(vmem_limit_bytes=16 << 20)


def shifted(value, axis, steps):
    count = lax.axis_size(axis)
    initial, last = (max(0, -steps), min(count, count - steps))
    return lax.ppermute(value, axis, [(source, source + steps) for source in range(initial, last)])


def iota(shape, dim):
    return lax.broadcasted_iota(jnp.int32, shape, dim)


def earlier(tiles):
    lane = iota(tiles[0].shape, 1)
    rolled = [pltpu.roll(tile, 1, 1) for tile in tiles]
    before = [jnp.zeros_like(tiles[0])] + rolled[:-1]
    return [jnp.where(lane == 0, edge, inner) for edge, inner in zip(before, rolled)]


def later(tiles):
    lane = iota(tiles[0].shape, 1)
    rolled = [pltpu.roll(tile, LANES - 1, 1) for tile in tiles]
    after = rolled[1:] + [jnp.zeros_like(tiles[0])]
    return [jnp.where(lane == LANES - 1, edge, inner) for edge, inner in zip(after, rolled)]


def stencil(v):
    em, ep = earlier(v), later(v)
    odd = [m - p for m, p in zip(em, ep)]
    even = [(m + p) - (c + c) for m, p, c in zip(em, ep, v)]
    return odd, even


def dip_part(p, odd, even):
    return [(0.5 * d) * (o + d * e) for d, o, e in zip(p, odd, even)]


def adjoint_terms(p, r):
    a = [(0.5 * d) * x for d, x in zip(p, r)]
    b = [d * x for d, x in zip(p, a)]
    return a, b


def adjoint_finish(r, a, b):
    up = later([x + y for x, y in zip(a, b)])
    down = earlier([y - x for x, y in zip(a, b)])
    return [(x + u) + (d - (y + y)) for x, u, d, y in zip(r, up, down, b)]


def load(ref, *index):
    count = ref.shape[-1] // LANES
    return [ref[(*index, slice(c * LANES, (c + 1) * LANES))] for c in range(count)]


def store(ref, tiles, *index):
    for c, tile in enumerate(tiles):
        ref[(*index, slice(c * LANES, (c + 1) * LANES))] = tile


def add(x, y):
    return [a + b for a, b in zip(x, y)]


def sub(x, y):
    return [a - b for a, b in zip(x, y)]


def dot(x, y):
    return functools.reduce(lambda s, t: s + t, [a * b for a, b in zip(x, y)])


def pack_kernel(capacity, owner_ref, cell_ref, live_ref, traces_ref, out_ref):
    held, samples = traces_ref.shape
    slots = out_ref.shape[0]
    spread = jnp.broadcast_to(owner_ref[...], (held, held))
    row, col = iota((held, held), 0), iota((held, held), 1)
    owner = jnp.sum(jnp.where(row == col, spread, 0), axis=0, keepdims=True)
    rank = jnp.sum(jnp.where((spread == owner) & (row < col), 1, 0), axis=0, keepdims=True)
    slot = jnp.where(live_ref[...] > 0, owner * capacity + rank, -1)
    chosen = (iota((slots, held), 0) == slot).astype(jnp.float32).astype(jnp.bfloat16)
    cell = cell_ref[...]
    kind = iota((LANES, held), 0)
    upper = (lax.shift_right_logical(cell, 6) + 1).astype(jnp.float32)
    lower = (cell & 63).astype(jnp.float32)
    codes = jnp.where(kind == 0, upper, jnp.where(kind == 1, lower, 0.0)).astype(jnp.bfloat16)
    rows = jnp.dot(chosen, traces_ref[...], preferred_element_type=jnp.float32)
    out_ref[:, :samples] = rows.astype(jnp.bfloat16)
    sent = lax.dot_general(chosen, codes, (((1,), (1,)), ((), ())), preferred_element_type=jnp.float32)
    out_ref[:, samples:] = sent.astype(jnp.bfloat16)


def bin_kernel(got_ref, p1_ref, p2_ref, b_ref, diag_ref, row0_ref, row7_ref, col0_ref, col7_ref):
    rows, cols, samples = b_ref.shape
    slots = got_ref.shape[0]
    kind = iota((SUBLANES, LANES), 1)
    weight = jnp.where(kind == 0, 64.0, jnp.where(kind == 1, 1.0, 0.0)).astype(jnp.bfloat16)
    value = lax.dot_general(
        weight, got_ref[:, samples:], (((1,), (1,)), ((), ())), preferred_element_type=jnp.float32
    )
    bin_of = value[:1].astype(jnp.int32) - 64
    not_first_row = (lax.axis_index("inl") > 0).astype(jnp.float32)
    not_first_col = (lax.axis_index("xl") > 0).astype(jnp.float32)
    ones = jnp.ones((slots, LANES), jnp.bfloat16)
    first_col = jnp.where(iota((cols, LANES), 0) == 0, not_first_col, 0.0)
    got = got_ref[:, :samples]
    for i in range(rows):
        place = (iota((cols, slots), 0) + i * cols == bin_of).astype(jnp.float32).astype(jnp.bfloat16)
        b_ref[i] = jnp.dot(place, got, preferred_element_type=jnp.float32)
        hits = jnp.dot(place, ones, preferred_element_type=jnp.float32)
        diag = 2.0 * hits + first_col
        diag_ref[i] = diag + not_first_row if i == 0 else diag
    write_edges(b_ref, p1_ref, p2_ref, row0_ref, row7_ref, col0_ref, col7_ref)


def write_edges(v_ref, p1_ref, p2_ref, row0_ref, row7_ref, col0_ref, col7_ref):
    rows, cols, _ = v_ref.shape
    last = rows - 1
    for x in range(0, cols, SUBLANES):
        at = slice(x, x + SUBLANES)
        store(row0_ref, load(v_ref, 0, at), at)
        v = load(v_ref, last, at)
        store(row7_ref, add(v, dip_part(load(p1_ref, last, at), *stencil(v))), at)
    for i in range(rows):
        store(col0_ref, load(v_ref, i, slice(0, 1)), slice(i, i + 1))
        at = slice(cols - SUBLANES, cols)
        v = load(v_ref, i, at)
        moved = add(v, dip_part(load(p2_ref, i, at), *stencil(v)))
        store(col7_ref, [t[SUBLANES - 1 :] for t in moved], slice(i, i + 1))


def apply_kernel(v_ref, p1_ref, p2_ref, diag_ref, out_ref, sums_ref, first_ref):
    rows, cols, samples = v_ref.shape
    tiles = samples // LANES
    sub_index = iota((SUBLANES, LANES), 0)
    zero = [jnp.zeros((SUBLANES, LANES), jnp.float32)] * tiles
    first_ref[...] = jnp.zeros_like(first_ref)

    def body(i, carry):
        vout, vv = carry
        after = jnp.where(i + 1 < rows, 1.0, 0.0)
        nxt = jnp.minimum(i + 1, rows - 1)
        v = load(v_ref, i, slice(0, SUBLANES))
        up = [pltpu.roll(t, SUBLANES - 1, 0) for t in v]
        down_before = zero
        for x in range(0, cols, SUBLANES):
            at = slice(x, x + SUBLANES)
            if x + SUBLANES < cols:
                v_ahead = load(v_ref, i, slice(x + SUBLANES, x + 2 * SUBLANES))
                up_ahead = [pltpu.roll(t, SUBLANES - 1, 0) for t in v_ahead]
            else:
                v_ahead, up_ahead = zero, zero
            right = [jnp.where(sub_index == SUBLANES - 1, b, a) for a, b in zip(up, up_ahead)]
            below = [after * t for t in load(v_ref, nxt, at)]
            p1, p2 = load(p1_ref, i, at), load(p2_ref, i, at)
            odd, even = stencil(v)
            first = sub(sub(below, v), dip_part(p1, odd, even))
            second = sub(sub(right, v), dip_part(p2, odd, even))
            a1, b1 = adjoint_terms(p1, first)
            a2, b2 = adjoint_terms(p2, second)
            moved = adjoint_finish(add(first, second), add(a1, a2), add(b1, b2))
            down = [pltpu.roll(t, 1, 0) for t in second]
            left = [jnp.where(sub_index == 0, b, a) for a, b in zip(down, down_before)]
            above = load(first_ref, at)
            store(first_ref, first, at)
            diag = diag_ref[i, at, :]
            out = [diag * c + ((f + s) - m) for c, f, s, m in zip(v, above, left, moved)]
            store(out_ref, out, i, at)
            vout = vout + dot(v, out)
            vv = vv + dot(v, v)
            v, up, down_before = v_ahead, up_ahead, down
        return vout, vv

    vout, vv = lax.fori_loop(0, rows, body, (zero[0], zero[0]))
    sums_ref[0] = vout
    sums_ref[1] = vv


def halo_corrections(out_ref, p1_ref, p2_ref, below_ref, above_ref, right_ref, left_ref):
    rows, cols, _ = out_ref.shape
    last = rows - 1
    sub_index = iota((SUBLANES, LANES), 0)
    for x in range(0, cols, SUBLANES):
        at = slice(x, x + SUBLANES)
        store(out_ref, sub(load(out_ref, 0, at), load(above_ref, at)), 0, at)
        r = load(below_ref, at)
        moved = adjoint_finish(r, *adjoint_terms(load(p1_ref, last, at), r))
        store(out_ref, sub(load(out_ref, last, at), moved), last, at)
    for i in range(rows):
        at = slice(0, SUBLANES)
        r = [jnp.where(sub_index == 0, t, 0.0) for t in load(left_ref, slice(i, i + 1))]
        store(out_ref, sub(load(out_ref, i, at), r), i, at)
        at = slice(cols - SUBLANES, cols)
        r = [jnp.where(sub_index == SUBLANES - 1, t, 0.0) for t in load(right_ref, slice(i, i + 1))]
        moved = adjoint_finish(r, *adjoint_terms(load(p2_ref, i, at), r))
        store(out_ref, sub(load(out_ref, i, at), moved), i, at)


def correct_kernel(
    image_ref, p1_ref, p2_ref, below_ref, above_ref, right_ref, left_ref, out_ref, *edge_refs
):
    halo_corrections(out_ref, p1_ref, p2_ref, below_ref, above_ref, right_ref, left_ref)
    if edge_refs:
        write_edges(out_ref, p1_ref, p2_ref, *edge_refs)


def moments_kernel(*refs):
    out_ref = refs[-1]
    m = []
    for step in range(ITERS):
        sums_ref, row7, below, col7, right = refs[5 * step : 5 * step + 5]
        across = jnp.zeros((SUBLANES, LANES), jnp.float32)
        for mine, theirs in ((row7, below), (col7, right)):
            for x in range(0, mine.shape[0], SUBLANES):
                at = slice(x, x + SUBLANES)
                across = across + dot(load(mine, at), load(theirs, at))
        m.append(sums_ref[1])
        m.append(sums_ref[0] - 2.0 * across)
    sub_index, lane = iota((SUBLANES, LANES), 0), iota((SUBLANES, LANES), 1)
    block = jnp.zeros((SUBLANES, LANES), jnp.float32)
    for k, part in enumerate(m):
        block = jnp.where(sub_index == k, jnp.sum(part, axis=0, keepdims=True), block)
    total = jnp.sum(block, axis=1, keepdims=True)
    line = jnp.sum(jnp.where(sub_index == lane, total, 0.0), axis=0, keepdims=True)
    out_ref[...] = jnp.broadcast_to(line[None], out_ref.shape)


def coefficients(m):
    zero = jnp.zeros_like(m[0])
    model = [zero] * ITERS
    residual = [zero + 1.0] + [zero] * ITERS
    direction = [zero + 1.0] + [zero] * (ITERS - 1)
    norm_now = m[0]

    def inner(x, y, power, count):
        total = zero
        for i in range(count):
            for j in range(count):
                total = total + x[i] * y[j] * m[i + j + power]
        return total

    for sweep in range(ITERS):
        alpha = norm_now / inner(direction, direction, 1, sweep + 1)
        model = [s + alpha * d for s, d in zip(model, direction)]
        residual = [residual[0]] + [r - alpha * d for r, d in zip(residual[1:], direction)]
        if sweep + 1 < ITERS:
            norm_next = inner(residual, residual, 0, sweep + 2)
            beta = norm_next / norm_now
            direction = [r + beta * d for r, d in zip(residual, direction)]
            norm_now = norm_next
    return model, residual


def finish_kernel(parts_ref, b_ref, v1_ref, v2_ref, v3_ref, model_ref, residual_ref):
    rows, cols, samples = b_ref.shape
    line = jnp.sum(parts_ref[...], axis=0)
    sub_index, lane = iota((SUBLANES, LANES), 0), iota((SUBLANES, LANES), 1)
    total = jnp.sum(jnp.where(sub_index == lane, line, 0.0), axis=1, keepdims=True)
    total = jnp.broadcast_to(total, (SUBLANES, LANES))
    m = [jnp.broadcast_to(total[k : k + 1], (SUBLANES, LANES)) for k in range(2 * ITERS)]
    model, residual = coefficients(m)

    def body(i, carry):
        for x in range(0, cols, SUBLANES):
            at = slice(x, x + SUBLANES)
            b, v1, v2, v3 = (load(ref, i, at) for ref in (b_ref, v1_ref, v2_ref, v3_ref))
            store(model_ref, [(2.0 * model[0]) * s + (2.0 * model[1]) * t + (2.0 * model[2]) * u for s, t, u in zip(b, v1, v2)], i, at)
            store(
                residual_ref,
                [residual[0] * s + residual[1] * t + residual[2] * u + residual[3] * w for s, t, u, w in zip(b, v1, v2, v3)],
                i, at,
            )
        return carry

    lax.fori_loop(0, rows, body, 0)


def f32(*shape):
    return pltpu.VMEM(shape, jnp.float32)


def call(kernel, outs, *args, name, scratch=(), aliases=None, cost=None, params=PARAMS):
    return pl.pallas_call(
        kernel,
        out_shape=outs,
        in_specs=[IN_VMEM] * len(args),
        out_specs=[IN_VMEM] * len(outs),
        scratch_shapes=list(scratch),
        input_output_aliases=aliases or {},
        compiler_params=params,
        cost_estimate=cost,
        name=name,
    )(*args)


def exchange(row0, row7, col0, col7):
    below = shifted(row0, "inl", -1)
    above = shifted(row7, "inl", 1)
    right = shifted(col0, "xl", -1)
    left = shifted(col7, "xl", 1)
    return below, above, right, left


def per_device(traces, trace_owner, trace_cell, acquired, inline_dip, cross_dip):
    rows, cols, samples = inline_dip.shape
    devices = lax.axis_size("inl") * lax.axis_size("xl")
    held = traces.shape[0]
    capacity = max(2, 2 * held // devices)
    slots = devices * capacity
    (sent,) = call(
        functools.partial(pack_kernel, capacity),
        [jax.ShapeDtypeStruct((slots, samples + LANES), jnp.bfloat16)],
        trace_owner, trace_cell[None], acquired[None], traces,
        name="pack",
    )
    got = lax.all_to_all(sent, ("inl", "xl"), split_axis=0, concat_axis=0, tiled=True)
    edge_shapes = [f32(cols, samples), f32(cols, samples), f32(rows, samples), f32(rows, samples)]
    tile = f32(rows, cols, samples)
    b, diag, *edges = call(
        bin_kernel, [tile, f32(rows, cols, LANES)] + edge_shapes, got, inline_dip, cross_dip, name="bin"
    )
    fields, products = [b], []
    cost = pl.CostEstimate(
        flops=60 * rows * cols * samples, bytes_accessed=16 * rows * cols * samples, transcendentals=0
    )
    for step in range(ITERS):
        halo = exchange(*edges)
        image, sums = call(
            apply_kernel,
            [tile, f32(2, SUBLANES, LANES)],
            fields[-1], inline_dip, cross_dip, diag,
            name="apply", scratch=[pltpu.VMEM((cols, samples), jnp.float32)], cost=cost,
        )
        products += [sums, edges[1], halo[0], edges[3], halo[2]]
        image, *edges = call(
            correct_kernel,
            [tile] + (edge_shapes if step + 1 < ITERS else []),
            image, inline_dip, cross_dip, *halo,
            name="correct", aliases={0: 0},
        )
        fields.append(image)
    (parts,) = call(moments_kernel, [jax.ShapeDtypeStruct((devices, 1, LANES), jnp.float32)], *products, name="moments")
    parts = lax.all_to_all(parts, ("inl", "xl"), split_axis=0, concat_axis=0, tiled=True)
    out = jax.ShapeDtypeStruct((rows, cols, samples), jnp.float32)
    return tuple(call(finish_kernel, [out, out], parts, *fields, name="finish"))


def solution(mesh):
    placed = (
        P(("inl", "xl"), None),
        P(("inl", "xl"), None),
        P(("inl", "xl")),
        P(("inl", "xl")),
        P("inl", "xl", None),
        P("inl", "xl", None),
    )
    return jax.shard_map(
        per_device,
        mesh=mesh,
        in_specs=placed,
        out_specs=(P("inl", "xl", None), P("inl", "xl", None)),
        check_vma=False,
    )
```

```python
import functools

import jax
import jax.numpy as jnp
from jax import lax
from jax.experimental import pallas as pl
from jax.experimental.pallas import tpu as pltpu
from jax.sharding import PartitionSpec as P

ITERS = 3
LANES = 128
SUBLANES = 8

SHIFT = 6.0
IN_VMEM = pl.BlockSpec(memory_space=pltpu.VMEM)
IN_HBM = pl.BlockSpec(memory_space=pltpu.HBM)
PARAMS = pltpu.CompilerParams(vmem_limit_bytes=16 << 20)


def shifted(value, axis, steps):
    count = lax.axis_size(axis)
    initial, last = (max(0, -steps), min(count, count - steps))
    return lax.ppermute(value, axis, [(source, source + steps) for source in range(initial, last)])


def iota(shape, dim):
    return lax.broadcasted_iota(jnp.int32, shape, dim)


def earlier(tiles):
    lane = iota(tiles[0].shape, 1)
    rolled = [pltpu.roll(tile, 1, 1) for tile in tiles]
    before = [jnp.zeros_like(tiles[0])] + rolled[:-1]
    return [jnp.where(lane == 0, edge, inner) for edge, inner in zip(before, rolled)]


def later(tiles):
    lane = iota(tiles[0].shape, 1)
    rolled = [pltpu.roll(tile, LANES - 1, 1) for tile in tiles]
    after = rolled[1:] + [jnp.zeros_like(tiles[0])]
    return [jnp.where(lane == LANES - 1, edge, inner) for edge, inner in zip(after, rolled)]


def stencil(v):
    em, ep = earlier(v), later(v)
    odd = [m - p for m, p in zip(em, ep)]
    even = [(m + p) - (c + c) for m, p, c in zip(em, ep, v)]
    return odd, even


def dip_part(p, odd, even):
    return [(0.5 * d) * (o + d * e) for d, o, e in zip(p, odd, even)]


def adjoint_terms(p, r):
    a = [(0.5 * d) * x for d, x in zip(p, r)]
    b = [d * x for d, x in zip(p, a)]
    return a, b


def adjoint_finish(r, a, b):
    up = later([x + y for x, y in zip(a, b)])
    down = earlier([y - x for x, y in zip(a, b)])
    return [(x + u) + (d - (y + y)) for x, u, d, y in zip(r, up, down, b)]


def load(ref, *index):
    count = ref.shape[-1] // LANES
    return [ref[(*index, slice(c * LANES, (c + 1) * LANES))] for c in range(count)]


def store(ref, tiles, *index):
    for c, tile in enumerate(tiles):
        ref[(*index, slice(c * LANES, (c + 1) * LANES))] = tile


def add(x, y):
    return [a + b for a, b in zip(x, y)]


def sub(x, y):
    return [a - b for a, b in zip(x, y)]


def dot(x, y):
    return functools.reduce(lambda s, t: s + t, [a * b for a, b in zip(x, y)])


def pack_kernel(capacity, owner_hbm, cell_hbm, live_hbm, traces_hbm, out_ref, owner_ref, cell_ref, live_ref, traces_ref, sems):
    held, samples = traces_ref.shape
    slots = out_ref.shape[0]
    pairs = ((owner_hbm, owner_ref), (cell_hbm, cell_ref), (live_hbm, live_ref), (traces_hbm, traces_ref))
    copies = [pltpu.make_async_copy(src, dst, sems.at[k]) for k, (src, dst) in enumerate(pairs)]
    for copy in copies:
        copy.start()
    for copy in copies[:3]:
        copy.wait()
    owner = owner_ref[...].astype(jnp.float32)
    row, col = iota((held, held), 0), iota((held, held), 1)
    owner_down = jnp.sum(jnp.where(row == col, owner, 0.0), axis=1, keepdims=True)
    earlier_same = (owner_down == owner) & (row < col)
    rank = jnp.sum(jnp.where(earlier_same, 1.0, 0.0), axis=0, keepdims=True)
    slot = jnp.where(live_ref[...] > 0, owner * capacity + rank, -1.0).astype(jnp.int32)
    chosen = (iota((slots, held), 0) == slot).astype(jnp.float32).astype(jnp.bfloat16)
    cell = cell_ref[...]
    kind = iota((LANES, held), 0)
    upper = (lax.shift_right_logical(cell, 6) + 1).astype(jnp.float32)
    lower = (cell & 63).astype(jnp.float32)
    codes = jnp.where(kind == 0, upper, jnp.where(kind == 1, lower, 0.0)).astype(jnp.bfloat16)
    sent = lax.dot_general(chosen, codes, (((1,), (1,)), ((), ())), preferred_element_type=jnp.float32)
    out_ref[:, samples:] = sent.astype(jnp.bfloat16)
    copies[3].wait()
    rows = jnp.dot(chosen, traces_ref[...], preferred_element_type=jnp.float32)
    out_ref[:, :samples] = rows.astype(jnp.bfloat16)


def bin_kernel(got_ref, p1_hbm, p2_hbm, b_ref, diag_ref, row0_ref, row7_ref, col0_ref, col7_ref, p1_ref, p2_ref, sems):
    rows, cols, samples = b_ref.shape
    slots = got_ref.shape[0]
    copies = (
        pltpu.make_async_copy(p1_hbm.at[rows - 1], p1_ref, sems.at[0]),
        pltpu.make_async_copy(p2_hbm.at[:, pl.ds(cols - SUBLANES, SUBLANES)], p2_ref, sems.at[1]),
    )
    for copy in copies:
        copy.start()
    kind = iota((SUBLANES, LANES), 1)
    weight = jnp.where(kind == 0, 64.0, jnp.where(kind == 1, 1.0, 0.0)).astype(jnp.bfloat16)
    value = lax.dot_general(
        weight, got_ref[:, samples:], (((1,), (1,)), ((), ())), preferred_element_type=jnp.float32
    )
    bin_of = value[:1].astype(jnp.int32) - 64
    not_first_row = (lax.axis_index("inl") > 0).astype(jnp.float32)
    not_first_col = (lax.axis_index("xl") > 0).astype(jnp.float32)
    ones = jnp.ones((slots, LANES), jnp.bfloat16)
    first_col = jnp.where(iota((cols, LANES), 0) == 0, not_first_col, 0.0) - SHIFT
    got = got_ref[:, :samples]
    for i in range(rows):
        place = (iota((cols, slots), 0) + i * cols == bin_of).astype(jnp.float32).astype(jnp.bfloat16)
        b_ref[i] = jnp.dot(place, got, preferred_element_type=jnp.float32)
        hits = jnp.dot(place, ones, preferred_element_type=jnp.float32)
        diag = 2.0 * hits + first_col
        diag_ref[i] = diag + not_first_row if i == 0 else diag
    for copy in copies:
        copy.wait()
    write_edges(
        b_ref, lambda at: load(p1_ref, at), lambda i: load(p2_ref, i, slice(None)),
        row0_ref, row7_ref, col0_ref, col7_ref,
    )


def write_edges(v_ref, p1_last_row, p2_last_cols, row0_ref, row7_ref, col0_ref, col7_ref):
    rows, cols, _ = v_ref.shape
    for x in range(0, cols, SUBLANES):
        at = slice(x, x + SUBLANES)
        store(row0_ref, load(v_ref, 0, at), at)
        v = load(v_ref, rows - 1, at)
        store(row7_ref, add(v, dip_part(p1_last_row(at), *stencil(v))), at)
    for i in range(rows):
        store(col0_ref, load(v_ref, i, slice(0, 1)), slice(i, i + 1))
        v = load(v_ref, i, slice(cols - SUBLANES, cols))
        moved = add(v, dip_part(p2_last_cols(i), *stencil(v)))
        store(col7_ref, [t[SUBLANES - 1 :] for t in moved], slice(i, i + 1))


def apply_kernel(v_ref, p1_ref, p2_ref, diag_ref, out_ref, sums_ref, first_ref):
    rows, cols, samples = v_ref.shape
    tiles = samples // LANES
    sub_index = iota((SUBLANES, LANES), 0)
    zero = [jnp.zeros((SUBLANES, LANES), jnp.float32)] * tiles
    first_ref[...] = jnp.zeros_like(first_ref)

    def row(i, sums, last):
        def fetch(x):
            at = slice(x, x + SUBLANES)
            v = load(v_ref, i, at)
            below = zero if last else load(v_ref, i + 1, at)
            lead = [pltpu.roll(t, SUBLANES - 1, 0) for t in v]
            return v, lead, below, load(p1_ref, i, at), load(p2_ref, i, at), load(first_ref, at), diag_ref[i, at, :]

        vout, vv = zero[0], zero[0]
        left_from = zero
        ahead = fetch(0)
        for x in range(0, cols, SUBLANES):
            at = slice(x, x + SUBLANES)
            v, lead, below, p1, p2, above, diag = ahead
            ahead = fetch(x + SUBLANES) if x + SUBLANES < cols else (zero, zero)
            right = [jnp.where(sub_index == SUBLANES - 1, b, a) for a, b in zip(lead, ahead[1])]
            odd, even = stencil(v)
            first = sub(sub(below, v), dip_part(p1, odd, even))
            second = sub(sub(right, v), dip_part(p2, odd, even))
            a1, b1 = adjoint_terms(p1, first)
            a2, b2 = adjoint_terms(p2, second)
            moved = adjoint_finish(add(first, second), add(a1, a2), add(b1, b2))
            down = [pltpu.roll(t, 1, 0) for t in second]
            left = [jnp.where(sub_index == 0, b, a) for a, b in zip(down, left_from)]
            left_from = down
            out = [diag * c + ((f + s) - m) for c, f, s, m in zip(v, above, left, moved)]
            vout = vout + dot(v, out)
            vv = vv + dot(v, v)
            store(first_ref, first, at)
            store(out_ref, out, i, at)
        return sums[0] + vout, sums[1] + vv

    sums = lax.fori_loop(0, rows - 1, lambda i, sums: row(i, sums, False), (zero[0], zero[0]))
    sums_ref[0], sums_ref[1] = row(rows - 1, sums, True)


def halo_corrections(out_ref, p1_ref, p2_ref, below_ref, above_ref, right_ref, left_ref):
    rows, cols, _ = out_ref.shape
    last = rows - 1
    sub_index = iota((SUBLANES, LANES), 0)
    for x in range(0, cols, SUBLANES):
        at = slice(x, x + SUBLANES)
        store(out_ref, sub(load(out_ref, 0, at), load(above_ref, at)), 0, at)
        r = load(below_ref, at)
        moved = adjoint_finish(r, *adjoint_terms(load(p1_ref, last, at), r))
        store(out_ref, sub(load(out_ref, last, at), moved), last, at)
    for i in range(rows):
        at = slice(0, SUBLANES)
        r = [jnp.where(sub_index == 0, t, 0.0) for t in load(left_ref, slice(i, i + 1))]
        store(out_ref, sub(load(out_ref, i, at), r), i, at)
        at = slice(cols - SUBLANES, cols)
        r = [jnp.where(sub_index == SUBLANES - 1, t, 0.0) for t in load(right_ref, slice(i, i + 1))]
        moved = adjoint_finish(r, *adjoint_terms(load(p2_ref, i, at), r))
        store(out_ref, sub(load(out_ref, i, at), moved), i, at)


def correct_kernel(
    image_ref, p1_ref, p2_ref, below_ref, above_ref, right_ref, left_ref, out_ref, *edge_refs
):
    halo_corrections(out_ref, p1_ref, p2_ref, below_ref, above_ref, right_ref, left_ref)
    if edge_refs:
        rows, cols, _ = out_ref.shape
        write_edges(
            out_ref,
            lambda at: load(p1_ref, rows - 1, at),
            lambda i: load(p2_ref, i, slice(cols - SUBLANES, cols)),
            *edge_refs,
        )


def moments_kernel(*refs):
    out_ref = refs[-1]
    m = []
    for step in range(ITERS):
        sums_ref, row7, below, col7, right = refs[5 * step : 5 * step + 5]
        across = jnp.zeros((SUBLANES, LANES), jnp.float32)
        for mine, theirs in ((row7, below), (col7, right)):
            for x in range(0, mine.shape[0], SUBLANES):
                at = slice(x, x + SUBLANES)
                across = across + dot(load(mine, at), load(theirs, at))
        m.append(sums_ref[1])
        m.append(sums_ref[0] - 2.0 * across)
    sub_index, lane = iota((SUBLANES, LANES), 0), iota((SUBLANES, LANES), 1)
    block = jnp.zeros((SUBLANES, LANES), jnp.float32)
    for k, part in enumerate(m):
        block = jnp.where(sub_index == k, jnp.sum(part, axis=0, keepdims=True), block)
    total = jnp.sum(block, axis=1, keepdims=True)
    line = jnp.sum(jnp.where(sub_index == lane, total, 0.0), axis=0, keepdims=True)
    out_ref[...] = jnp.broadcast_to(line[None], out_ref.shape)


def coefficients(m):
    zero = jnp.zeros_like(m[0])
    model = [zero] * ITERS
    residual = [zero + 1.0] + [zero] * ITERS
    direction = [zero + 1.0] + [zero] * (ITERS - 1)
    norm_now = m[0]

    def inner(x, y, count):
        total = zero
        for i in range(count):
            for j in range(len(y)):
                if i + j < len(m):
                    total = total + x[i] * y[j] * m[i + j]
        return total

    for sweep in range(ITERS):
        image = [SHIFT * d for d in direction] + [zero]
        image = [image[0]] + [s + d for s, d in zip(image[1:], direction)]
        alpha = norm_now / inner(direction, image[: sweep + 2], sweep + 1)
        model = [s + alpha * d for s, d in zip(model, direction)]
        residual = [r - alpha * d for r, d in zip(residual, image)]
        if sweep + 1 < ITERS:
            norm_next = inner(residual, residual[: sweep + 2], sweep + 2)
            beta = norm_next / norm_now
            direction = [r + beta * d for r, d in zip(residual, direction)]
            norm_now = norm_next
    return [2.0 * s for s in model] + residual


def finish_kernel(parts_ref, b_ref, v1_ref, v2_ref, v3_ref, model_ref, residual_ref, weight_ref):
    cols = b_ref.shape[1]
    i = pl.program_id(0)

    @pl.when(i == 0)
    def _():
        line = jnp.sum(parts_ref[...], axis=0)
        sub_index, lane = iota((SUBLANES, LANES), 0), iota((SUBLANES, LANES), 1)
        total = jnp.sum(jnp.where(sub_index == lane, line, 0.0), axis=1, keepdims=True)
        total = jnp.broadcast_to(total, (SUBLANES, LANES))
        m = [jnp.broadcast_to(total[k : k + 1], (SUBLANES, LANES)) for k in range(2 * ITERS)]
        for k, weight in enumerate(coefficients(m)):
            weight_ref[k] = weight

    weights = [weight_ref[k] for k in range(2 * ITERS + 1)]
    model, residual = weights[:ITERS], weights[ITERS:]
    for x in range(0, cols, SUBLANES):
        at = slice(x, x + SUBLANES)
        b, v1, v2, v3 = (load(ref, i, at) for ref in (b_ref, v1_ref, v2_ref, v3_ref))
        store(model_ref, [model[0] * s + model[1] * t + model[2] * u for s, t, u in zip(b, v1, v2)], 0, at)
        store(
            residual_ref,
            [(residual[0] * s + residual[1] * t) + (residual[2] * u + residual[3] * w) for s, t, u, w in zip(b, v1, v2, v3)],
            0, at,
        )


def f32(*shape):
    return pltpu.VMEM(shape, jnp.float32)


def call(kernel, outs, *args, name, scratch=(), aliases=None, cost=None, ins=None):
    return pl.pallas_call(
        kernel,
        out_shape=outs,
        in_specs=ins or [IN_VMEM] * len(args),
        out_specs=[IN_VMEM] * len(outs),
        scratch_shapes=list(scratch),
        input_output_aliases=aliases or {},
        compiler_params=PARAMS,
        cost_estimate=cost,
        name=name,
    )(*args)


def exchange(row0, row7, col0, col7):
    below = shifted(row0, "inl", -1)
    above = shifted(row7, "inl", 1)
    right = shifted(col0, "xl", -1)
    left = shifted(col7, "xl", 1)
    return below, above, right, left


def per_device(traces, trace_owner, trace_cell, acquired, inline_dip, cross_dip):
    rows, cols, samples = inline_dip.shape
    devices = lax.axis_size("inl") * lax.axis_size("xl")
    held = traces.shape[0]
    capacity = max(2, 2 * held // devices)
    slots = devices * capacity
    small = pltpu.VMEM((1, held), jnp.int32)
    (sent,) = call(
        functools.partial(pack_kernel, capacity),
        [jax.ShapeDtypeStruct((slots, samples + LANES), jnp.bfloat16)],
        trace_owner.reshape(1, held), trace_cell[None], acquired[None], traces,
        name="pack", ins=[IN_HBM] * 4,
        scratch=[small, small, small, pltpu.VMEM((held, samples), jnp.bfloat16), pltpu.SemaphoreType.DMA((4,))],
    )
    got = lax.all_to_all(sent, ("inl", "xl"), split_axis=0, concat_axis=0, tiled=True)
    edge_shapes = [f32(cols, samples), f32(cols, samples), f32(rows, samples), f32(rows, samples)]
    tile = f32(rows, cols, samples)
    b, diag, *edges = call(
        bin_kernel, [tile, f32(rows, cols, LANES)] + edge_shapes, got, inline_dip, cross_dip,
        name="bin", ins=[IN_VMEM, IN_HBM, IN_HBM],
        scratch=[
            pltpu.VMEM((cols, samples), jnp.float32),
            pltpu.VMEM((rows, SUBLANES, samples), jnp.float32),
            pltpu.SemaphoreType.DMA((2,)),
        ],
    )
    fields, products = [b], []
    cost = pl.CostEstimate(
        flops=60 * rows * cols * samples, bytes_accessed=16 * rows * cols * samples, transcendentals=0
    )
    for step in range(ITERS):
        halo = exchange(*edges)
        image, sums = call(
            apply_kernel,
            [tile, f32(2, SUBLANES, LANES)],
            fields[-1], inline_dip, cross_dip, diag,
            name="apply", scratch=[pltpu.VMEM((cols, samples), jnp.float32)], cost=cost,
        )
        products += [sums, edges[1], halo[0], edges[3], halo[2]]
        image, *edges = call(
            correct_kernel,
            [tile] + (edge_shapes if step + 1 < ITERS else []),
            image, inline_dip, cross_dip, *halo,
            name="correct", aliases={0: 0},
        )
        fields.append(image)
    (parts,) = call(moments_kernel, [f32(devices, 1, LANES)], *products, name="moments")
    parts = lax.all_to_all(parts, ("inl", "xl"), split_axis=0, concat_axis=0, tiled=True)
    out = jax.ShapeDtypeStruct((rows, cols, samples), jnp.float32)
    by_row = pl.BlockSpec((1, cols, samples), lambda i: (i, 0, 0))
    return tuple(
        pl.pallas_call(
            finish_kernel,
            grid=(rows,),
            out_shape=[out, out],
            in_specs=[IN_VMEM] * (ITERS + 2),
            out_specs=[by_row, by_row],
            scratch_shapes=[pltpu.VMEM((2 * ITERS + 1, SUBLANES, LANES), jnp.float32)],
            compiler_params=PARAMS,
            name="finish",
        )(parts, *fields)
    )


def solution(mesh):
    placed = (
        P(("inl", "xl"), None),
        P(("inl", "xl"), None),
        P(("inl", "xl")),
        P(("inl", "xl")),
        P("inl", "xl", None),
        P("inl", "xl", None),
    )
    return jax.shard_map(
        per_device,
        mesh=mesh,
        in_specs=placed,
        out_specs=(P("inl", "xl", None), P("inl", "xl", None)),
        check_vma=False,
    )
```

```python
import functools

import jax
import jax.numpy as jnp
from jax import lax
from jax.experimental import pallas as pl
from jax.experimental.pallas import tpu as pltpu
from jax.sharding import PartitionSpec as P

ITERS = 3
LANES = 128
SUBLANES = 8

SHIFT = 6.0
IN_VMEM = pl.BlockSpec(memory_space=pltpu.VMEM)
IN_HBM = pl.BlockSpec(memory_space=pltpu.HBM)
PARAMS = pltpu.CompilerParams(vmem_limit_bytes=16 << 20)


def shifted(value, axis, steps):
    count = lax.axis_size(axis)
    initial, last = (max(0, -steps), min(count, count - steps))
    return lax.ppermute(value, axis, [(source, source + steps) for source in range(initial, last)])


def iota(shape, dim):
    return lax.broadcasted_iota(jnp.int32, shape, dim)


def earlier(tiles):
    lane = iota(tiles[0].shape, 1)
    rolled = [pltpu.roll(tile, 1, 1) for tile in tiles]
    before = [jnp.zeros_like(tiles[0])] + rolled[:-1]
    return [jnp.where(lane == 0, edge, inner) for edge, inner in zip(before, rolled)]


def later(tiles):
    lane = iota(tiles[0].shape, 1)
    rolled = [pltpu.roll(tile, LANES - 1, 1) for tile in tiles]
    after = rolled[1:] + [jnp.zeros_like(tiles[0])]
    return [jnp.where(lane == LANES - 1, edge, inner) for edge, inner in zip(after, rolled)]


def stencil(v):
    em, ep = earlier(v), later(v)
    odd = [m - p for m, p in zip(em, ep)]
    even = [(m + p) - (c + c) for m, p, c in zip(em, ep, v)]
    return odd, even


def dip_part(p, odd, even):
    return [(0.5 * d) * (o + d * e) for d, o, e in zip(p, odd, even)]


def adjoint_terms(p, r):
    a = [(0.5 * d) * x for d, x in zip(p, r)]
    b = [d * x for d, x in zip(p, a)]
    return a, b


def adjoint_finish(r, a, b):
    up = later([x + y for x, y in zip(a, b)])
    down = earlier([y - x for x, y in zip(a, b)])
    return [(x + u) + (d - (y + y)) for x, u, d, y in zip(r, up, down, b)]


def load(ref, *index):
    count = ref.shape[-1] // LANES
    return [ref[(*index, slice(c * LANES, (c + 1) * LANES))] for c in range(count)]


def store(ref, tiles, *index):
    for c, tile in enumerate(tiles):
        ref[(*index, slice(c * LANES, (c + 1) * LANES))] = tile


def load_field(ref, i, at):
    return [ref[i, c, at, :] for c in range(ref.shape[1])]


def store_field(ref, tiles, i, at):
    for c, tile in enumerate(tiles):
        ref[i, c, at, :] = tile


def add(x, y):
    return [a + b for a, b in zip(x, y)]


def sub(x, y):
    return [a - b for a, b in zip(x, y)]


def dot(x, y):
    return functools.reduce(lambda s, t: s + t, [a * b for a, b in zip(x, y)])


def pack_kernel(capacity, owner_hbm, cell_hbm, live_hbm, traces_hbm, out_ref, owner_ref, cell_ref, live_ref, traces_ref, sems):
    held, samples = traces_ref.shape
    slots = out_ref.shape[0]
    pairs = ((owner_hbm, owner_ref), (cell_hbm, cell_ref), (live_hbm, live_ref), (traces_hbm, traces_ref))
    copies = [pltpu.make_async_copy(src, dst, sems.at[k]) for k, (src, dst) in enumerate(pairs)]
    for copy in copies:
        copy.start()
    for copy in copies[:3]:
        copy.wait()
    owner = owner_ref[...].astype(jnp.float32)
    row, col = iota((held, held), 0), iota((held, held), 1)
    owner_down = jnp.sum(jnp.where(row == col, owner, 0.0), axis=1, keepdims=True)
    earlier_same = (owner_down == owner) & (row < col)
    rank = jnp.sum(jnp.where(earlier_same, 1.0, 0.0), axis=0, keepdims=True)
    slot = jnp.where(live_ref[...] > 0, owner * capacity + rank, -1.0).astype(jnp.int32)
    chosen = (iota((slots, held), 0) == slot).astype(jnp.float32).astype(jnp.bfloat16)
    cell = cell_ref[...]
    kind = iota((LANES, held), 0)
    upper = (lax.shift_right_logical(cell, 6) + 1).astype(jnp.float32)
    lower = (cell & 63).astype(jnp.float32)
    codes = jnp.where(kind == 0, upper, jnp.where(kind == 1, lower, 0.0)).astype(jnp.bfloat16)
    sent = lax.dot_general(chosen, codes, (((1,), (1,)), ((), ())), preferred_element_type=jnp.float32)
    out_ref[:, samples:] = sent.astype(jnp.bfloat16)
    copies[3].wait()
    rows = jnp.dot(chosen, traces_ref[...], preferred_element_type=jnp.float32)
    out_ref[:, :samples] = rows.astype(jnp.bfloat16)


def bin_kernel(got_ref, p1_hbm, p2_hbm, b_ref, diag_ref, row0_ref, row7_ref, col0_ref, col7_ref, p1_ref, p2_ref, sems):
    rows, tiles, cols, _ = b_ref.shape
    samples = tiles * LANES
    slots = got_ref.shape[0]
    copies = (
        pltpu.make_async_copy(p1_hbm.at[rows - 1], p1_ref, sems.at[0]),
        pltpu.make_async_copy(p2_hbm.at[:, pl.ds(cols - SUBLANES, SUBLANES)], p2_ref, sems.at[1]),
    )
    for copy in copies:
        copy.start()
    kind = iota((SUBLANES, LANES), 1)
    weight = jnp.where(kind == 0, 64.0, jnp.where(kind == 1, 1.0, 0.0)).astype(jnp.bfloat16)
    value = lax.dot_general(
        weight, got_ref[:, samples:], (((1,), (1,)), ((), ())), preferred_element_type=jnp.float32
    )
    bin_of = value[:1].astype(jnp.int32) - 64
    not_first_row = (lax.axis_index("inl") > 0).astype(jnp.float32)
    not_first_col = (lax.axis_index("xl") > 0).astype(jnp.float32)
    ones = jnp.ones((slots, LANES), jnp.bfloat16)
    first_col = jnp.where(iota((cols, LANES), 0) == 0, not_first_col, 0.0) - SHIFT
    got = got_ref[:, :samples]
    for i in range(rows):
        place = (iota((cols, slots), 0) + i * cols == bin_of).astype(jnp.float32).astype(jnp.bfloat16)
        total = jnp.dot(place, got, preferred_element_type=jnp.float32)
        for c in range(tiles):
            b_ref[i, c] = total[:, c * LANES : (c + 1) * LANES]
        hits = jnp.dot(place, ones, preferred_element_type=jnp.float32)
        diag = 2.0 * hits + first_col
        diag_ref[i] = diag + not_first_row if i == 0 else diag
    for copy in copies:
        copy.wait()
    write_edges(
        b_ref, lambda at: load(p1_ref, at), lambda i: load(p2_ref, i, slice(None)),
        row0_ref, row7_ref, col0_ref, col7_ref,
    )


def write_edges(v_ref, p1_last_row, p2_last_cols, row0_ref, row7_ref, col0_ref, col7_ref):
    rows, _, cols, _ = v_ref.shape
    for x in range(0, cols, SUBLANES):
        at = slice(x, x + SUBLANES)
        store(row0_ref, load_field(v_ref, 0, at), at)
        v = load_field(v_ref, rows - 1, at)
        store(row7_ref, add(v, dip_part(p1_last_row(at), *stencil(v))), at)
    for i in range(rows):
        store(col0_ref, load_field(v_ref, i, slice(0, 1)), slice(i, i + 1))
        v = load_field(v_ref, i, slice(cols - SUBLANES, cols))
        moved = add(v, dip_part(p2_last_cols(i), *stencil(v)))
        store(col7_ref, [t[SUBLANES - 1 :] for t in moved], slice(i, i + 1))


def apply_kernel(v_ref, p1_ref, p2_ref, diag_ref, out_ref, sums_ref, first_ref, second_ref):
    rows, tiles, cols, _ = v_ref.shape
    sub_index = iota((SUBLANES, LANES), 0)
    zero = [jnp.zeros((SUBLANES, LANES), jnp.float32)] * tiles
    first_ref[...] = jnp.zeros_like(first_ref)
    for c in range(tiles):
        second_ref[c, :SUBLANES, :] = zero[0]

    def row(i, sums, last):
        vout, vv = zero[0], zero[0]
        for x in range(0, cols, SUBLANES):
            at = slice(x, x + SUBLANES)
            v = load_field(v_ref, i, at)
            if x + SUBLANES < cols:
                right = load_field(v_ref, i, slice(x + 1, x + 1 + SUBLANES))
            else:
                right = [jnp.where(sub_index == SUBLANES - 1, 0.0, pltpu.roll(t, SUBLANES - 1, 0)) for t in v]
            below = zero if last else load_field(v_ref, i + 1, at)
            p1, p2 = load(p1_ref, i, at), load(p2_ref, i, at)
            odd, even = stencil(v)
            first = sub(sub(below, v), dip_part(p1, odd, even))
            second = sub(sub(right, v), dip_part(p2, odd, even))
            for c in range(tiles):
                second_ref[c, x + SUBLANES : x + 2 * SUBLANES, :] = second[c]
            a1, b1 = adjoint_terms(p1, first)
            a2, b2 = adjoint_terms(p2, second)
            moved = adjoint_finish(add(first, second), add(a1, a2), add(b1, b2))
            left = [second_ref[c, x + SUBLANES - 1 : x + 2 * SUBLANES - 1, :] for c in range(tiles)]
            above = load(first_ref, at)
            store(first_ref, first, at)
            diag = diag_ref[i, at, :]
            out = [diag * c + ((f + s) - m) for c, f, s, m in zip(v, above, left, moved)]
            store_field(out_ref, out, i, at)
            vout = vout + dot(v, out)
            vv = vv + dot(v, v)
        return sums[0] + vout, sums[1] + vv

    sums = lax.fori_loop(0, rows - 1, lambda i, sums: row(i, sums, False), (zero[0], zero[0]))
    sums_ref[0], sums_ref[1] = row(rows - 1, sums, True)


def halo_corrections(out_ref, p1_ref, p2_ref, below_ref, above_ref, right_ref, left_ref):
    rows, _, cols, _ = out_ref.shape
    last = rows - 1
    sub_index = iota((SUBLANES, LANES), 0)
    for x in range(0, cols, SUBLANES):
        at = slice(x, x + SUBLANES)
        store_field(out_ref, sub(load_field(out_ref, 0, at), load(above_ref, at)), 0, at)
        r = load(below_ref, at)
        moved = adjoint_finish(r, *adjoint_terms(load(p1_ref, last, at), r))
        store_field(out_ref, sub(load_field(out_ref, last, at), moved), last, at)
    for i in range(rows):
        at = slice(0, SUBLANES)
        r = [jnp.where(sub_index == 0, t, 0.0) for t in load(left_ref, slice(i, i + 1))]
        store_field(out_ref, sub(load_field(out_ref, i, at), r), i, at)
        at = slice(cols - SUBLANES, cols)
        r = [jnp.where(sub_index == SUBLANES - 1, t, 0.0) for t in load(right_ref, slice(i, i + 1))]
        moved = adjoint_finish(r, *adjoint_terms(load(p2_ref, i, at), r))
        store_field(out_ref, sub(load_field(out_ref, i, at), moved), i, at)


def correct_kernel(
    image_ref, p1_ref, p2_ref, below_ref, above_ref, right_ref, left_ref, out_ref, *edge_refs
):
    halo_corrections(out_ref, p1_ref, p2_ref, below_ref, above_ref, right_ref, left_ref)
    rows, _, cols, _ = out_ref.shape
    write_edges(
        out_ref,
        lambda at: load(p1_ref, rows - 1, at),
        lambda i: load(p2_ref, i, slice(cols - SUBLANES, cols)),
        *edge_refs,
    )


def moments_kernel(image_ref, p1_ref, p2_ref, below_ref, above_ref, right_ref, left_ref, *refs):
    halo_corrections(refs[-2], p1_ref, p2_ref, below_ref, above_ref, right_ref, left_ref)
    out_ref = refs[-1]
    m = []
    for step in range(ITERS):
        sums_ref, row7, below, col7, right = refs[5 * step : 5 * step + 5]
        across = jnp.zeros((SUBLANES, LANES), jnp.float32)
        for mine, theirs in ((row7, below), (col7, right)):
            for x in range(0, mine.shape[0], SUBLANES):
                at = slice(x, x + SUBLANES)
                across = across + dot(load(mine, at), load(theirs, at))
        m.append(sums_ref[1])
        m.append(sums_ref[0] - 2.0 * across)
    sub_index, lane = iota((SUBLANES, LANES), 0), iota((SUBLANES, LANES), 1)
    block = jnp.zeros((SUBLANES, LANES), jnp.float32)
    for k, part in enumerate(m):
        block = jnp.where(sub_index == k, jnp.sum(part, axis=0, keepdims=True), block)
    total = jnp.sum(block, axis=1, keepdims=True)
    line = jnp.sum(jnp.where(sub_index == lane, total, 0.0), axis=0, keepdims=True)
    out_ref[...] = jnp.broadcast_to(line[None], out_ref.shape)


def coefficients(m):
    zero = jnp.zeros_like(m[0])
    model = [zero] * ITERS
    residual = [zero + 1.0] + [zero] * ITERS
    direction = [zero + 1.0] + [zero] * (ITERS - 1)
    norm_now = m[0]

    def inner(x, y, count):
        total = zero
        for i in range(count):
            for j in range(len(y)):
                if i + j < len(m):
                    total = total + x[i] * y[j] * m[i + j]
        return total

    for sweep in range(ITERS):
        image = [SHIFT * d for d in direction] + [zero]
        image = [image[0]] + [s + d for s, d in zip(image[1:], direction)]
        alpha = norm_now / inner(direction, image[: sweep + 2], sweep + 1)
        model = [s + alpha * d for s, d in zip(model, direction)]
        residual = [r - alpha * d for r, d in zip(residual, image)]
        if sweep + 1 < ITERS:
            norm_next = inner(residual, residual[: sweep + 2], sweep + 2)
            beta = norm_next / norm_now
            direction = [r + beta * d for r, d in zip(residual, direction)]
            norm_now = norm_next
    return [2.0 * s for s in model] + residual


def finish_kernel(parts_ref, b_ref, v1_ref, v2_ref, v3_ref, model_hbm, residual_hbm, model_ref, residual_ref, sems):
    rows, _, cols, _ = b_ref.shape
    line = jnp.sum(parts_ref[...], axis=0)
    sub_index, lane = iota((SUBLANES, LANES), 0), iota((SUBLANES, LANES), 1)
    total = jnp.sum(jnp.where(sub_index == lane, line, 0.0), axis=1, keepdims=True)
    total = jnp.broadcast_to(total, (SUBLANES, LANES))
    m = [jnp.broadcast_to(total[k : k + 1], (SUBLANES, LANES)) for k in range(2 * ITERS)]
    weights = coefficients(m)
    model, residual = weights[:ITERS], weights[ITERS:]

    def copies(i):
        return (
            pltpu.make_async_copy(model_ref.at[i], model_hbm.at[i], sems.at[0, i]),
            pltpu.make_async_copy(residual_ref.at[i], residual_hbm.at[i], sems.at[1, i]),
        )

    def body(i, carry):
        for x in range(0, cols, SUBLANES):
            at = slice(x, x + SUBLANES)
            b, v1, v2, v3 = (load_field(ref, i, at) for ref in (b_ref, v1_ref, v2_ref, v3_ref))
            store(model_ref, [model[0] * s + model[1] * t + model[2] * u for s, t, u in zip(b, v1, v2)], i, at)
            store(
                residual_ref,
                [(residual[0] * s + residual[1] * t) + (residual[2] * u + residual[3] * w) for s, t, u, w in zip(b, v1, v2, v3)],
                i, at,
            )
        for copy in copies(i):
            copy.start()
        return carry

    lax.fori_loop(0, rows, body, 0)
    for i in range(rows):
        for copy in copies(i):
            copy.wait()


def f32(*shape):
    return pltpu.VMEM(shape, jnp.float32)


def call(kernel, outs, *args, name, scratch=(), aliases=None, cost=None, ins=None, places=None):
    return pl.pallas_call(
        kernel,
        out_shape=outs,
        in_specs=ins or [IN_VMEM] * len(args),
        out_specs=places or [IN_VMEM] * len(outs),
        scratch_shapes=list(scratch),
        input_output_aliases=aliases or {},
        compiler_params=PARAMS,
        cost_estimate=cost,
        name=name,
    )(*args)


def in_hbm(array):
    return pltpu.with_memory_space_constraint(array, pltpu.HBM)


def exchange(row0, row7, col0, col7):
    below = shifted(row0, "inl", -1)
    above = shifted(row7, "inl", 1)
    right = shifted(col0, "xl", -1)
    left = shifted(col7, "xl", 1)
    return below, above, right, left


def per_device(traces, trace_owner, trace_cell, acquired, inline_dip, cross_dip):
    rows, cols, samples = inline_dip.shape
    devices = lax.axis_size("inl") * lax.axis_size("xl")
    held = traces.shape[0]
    capacity = max(2, 2 * held // devices)
    slots = devices * capacity
    small = pltpu.VMEM((1, held), jnp.int32)
    (sent,) = call(
        functools.partial(pack_kernel, capacity),
        [jax.ShapeDtypeStruct((slots, samples + LANES), jnp.bfloat16)],
        *(in_hbm(x) for x in (trace_owner.reshape(1, held), trace_cell[None], acquired[None], traces)),
        name="pack", ins=[IN_HBM] * 4,
        scratch=[small, small, small, pltpu.VMEM((held, samples), jnp.bfloat16), pltpu.SemaphoreType.DMA((4,))],
    )
    got = lax.all_to_all(sent, ("inl", "xl"), split_axis=0, concat_axis=0, tiled=True)
    edge_shapes = [f32(cols, samples), f32(cols, samples), f32(rows, samples), f32(rows, samples)]
    tile = f32(rows, samples // LANES, cols, LANES)
    b, diag, *edges = call(
        bin_kernel, [tile, f32(rows, cols, LANES)] + edge_shapes, got, in_hbm(inline_dip), in_hbm(cross_dip),
        name="bin", ins=[IN_VMEM, IN_HBM, IN_HBM],
        scratch=[
            pltpu.VMEM((cols, samples), jnp.float32),
            pltpu.VMEM((rows, SUBLANES, samples), jnp.float32),
            pltpu.SemaphoreType.DMA((2,)),
        ],
    )
    fields, products = [b], []
    cost = pl.CostEstimate(
        flops=60 * rows * cols * samples, bytes_accessed=16 * rows * cols * samples, transcendentals=0
    )
    for step in range(ITERS):
        halo = exchange(*edges)
        image, sums = call(
            apply_kernel,
            [tile, f32(2, SUBLANES, LANES)],
            fields[-1], inline_dip, cross_dip, diag,
            name="apply",
            scratch=[
                pltpu.VMEM((cols, samples), jnp.float32),
                pltpu.VMEM((samples // LANES, SUBLANES + cols, LANES), jnp.float32),
            ],
            cost=cost,
        )
        products += [sums, edges[1], halo[0], edges[3], halo[2]]
        if step + 1 < ITERS:
            image, *edges = call(
                correct_kernel, [tile] + edge_shapes, image, inline_dip, cross_dip, *halo,
                name="correct", aliases={0: 0},
            )
        else:
            image, parts = call(
                moments_kernel, [tile, f32(devices, 1, LANES)], image, inline_dip, cross_dip, *halo, *products,
                name="moments", aliases={0: 0},
            )
        fields.append(image)
    parts = lax.all_to_all(parts, ("inl", "xl"), split_axis=0, concat_axis=0, tiled=True)
    out = jax.ShapeDtypeStruct((rows, cols, samples), jnp.float32)
    return tuple(
        call(
            finish_kernel, [out, out], parts, *fields,
            name="finish", places=[pl.BlockSpec(memory_space=pl.ANY)] * 2,
            scratch=[
                pltpu.VMEM((rows, cols, samples), jnp.float32),
                pltpu.VMEM((rows, cols, samples), jnp.float32),
                pltpu.SemaphoreType.DMA((2, rows)),
            ],
        )
    )


def solution(mesh):
    placed = (
        P(("inl", "xl"), None),
        P(("inl", "xl"), None),
        P(("inl", "xl")),
        P(("inl", "xl")),
        P("inl", "xl", None),
        P("inl", "xl", None),
    )
    return jax.shard_map(
        per_device,
        mesh=mesh,
        in_specs=placed,
        out_specs=(P("inl", "xl", None), P("inl", "xl", None)),
        check_vma=False,
    )
```

```python
import functools

import jax
import jax.numpy as jnp
from jax import lax
from jax.experimental import pallas as pl
from jax.experimental.pallas import tpu as pltpu
from jax.sharding import PartitionSpec as P

ITERS = 3
LANES = 128
SUBLANES = 8

SHIFT = 6.0
IN_VMEM = pl.BlockSpec(memory_space=pltpu.VMEM)
IN_HBM = pl.BlockSpec(memory_space=pltpu.HBM)
PARAMS = pltpu.CompilerParams(vmem_limit_bytes=16 << 20)


def shifted(value, axis, steps):
    count = lax.axis_size(axis)
    initial, last = (max(0, -steps), min(count, count - steps))
    return lax.ppermute(value, axis, [(source, source + steps) for source in range(initial, last)])


def iota(shape, dim):
    return lax.broadcasted_iota(jnp.int32, shape, dim)


def earlier(tiles):
    lane = iota(tiles[0].shape, 1)
    rolled = [pltpu.roll(tile, 1, 1) for tile in tiles]
    before = [jnp.zeros_like(tiles[0])] + rolled[:-1]
    return [jnp.where(lane == 0, edge, inner) for edge, inner in zip(before, rolled)]


def later(tiles):
    lane = iota(tiles[0].shape, 1)
    rolled = [pltpu.roll(tile, LANES - 1, 1) for tile in tiles]
    after = rolled[1:] + [jnp.zeros_like(tiles[0])]
    return [jnp.where(lane == LANES - 1, edge, inner) for edge, inner in zip(after, rolled)]


def stencil(v):
    em, ep = earlier(v), later(v)
    odd = [m - p for m, p in zip(em, ep)]
    even = [(m + p) - (c + c) for m, p, c in zip(em, ep, v)]
    return odd, even


def dip_part(p, odd, even):
    return [(0.5 * d) * (o + d * e) for d, o, e in zip(p, odd, even)]


def adjoint_terms(p, r):
    a = [(0.5 * d) * x for d, x in zip(p, r)]
    b = [d * x for d, x in zip(p, a)]
    return a, b


def adjoint_finish(r, a, b):
    up = later([x + y for x, y in zip(a, b)])
    down = earlier([y - x for x, y in zip(a, b)])
    return [(x + u) + (d - (y + y)) for x, u, d, y in zip(r, up, down, b)]


def load(ref, *index):
    count = ref.shape[-1] // LANES
    return [ref[(*index, slice(c * LANES, (c + 1) * LANES))] for c in range(count)]


def store(ref, tiles, *index):
    for c, tile in enumerate(tiles):
        ref[(*index, slice(c * LANES, (c + 1) * LANES))] = tile


def load_tiles(ref, at):
    return [ref[c, at, :] for c in range(ref.shape[0])]


def load_field(ref, i, at):
    return [ref[i, c, at, :] for c in range(ref.shape[1])]


def store_field(ref, tiles, i, at):
    for c, tile in enumerate(tiles):
        ref[i, c, at, :] = tile


def add(x, y):
    return [a + b for a, b in zip(x, y)]


def sub(x, y):
    return [a - b for a, b in zip(x, y)]


def dot(x, y):
    return functools.reduce(lambda s, t: s + t, [a * b for a, b in zip(x, y)])


def pack_kernel(
    capacity, owner_hbm, cell_hbm, live_hbm, traces_hbm, p1_hbm, p2_hbm, out_ref, p1_last_ref, p2_last_ref,
    owner_ref, cell_ref, live_ref, traces_ref, sems,
):
    held, samples = traces_ref.shape
    slots = out_ref.shape[0]
    rows, cols, _ = p1_hbm.shape
    pairs = (
        (owner_hbm, owner_ref), (cell_hbm, cell_ref), (live_hbm, live_ref), (traces_hbm, traces_ref),
        (p1_hbm.at[rows - 1], p1_last_ref), (p2_hbm.at[:, pl.ds(cols - SUBLANES, SUBLANES)], p2_last_ref),
    )
    copies = [pltpu.make_async_copy(src, dst, sems.at[k]) for k, (src, dst) in enumerate(pairs)]
    for copy in copies:
        copy.start()
    for copy in copies[:3]:
        copy.wait()
    owner = owner_ref[...].astype(jnp.float32)
    row, col = iota((held, held), 0), iota((held, held), 1)
    owner_down = jnp.sum(jnp.where(row == col, owner, 0.0), axis=1, keepdims=True)
    earlier_same = (owner_down == owner) & (row < col)
    rank = jnp.sum(jnp.where(earlier_same, 1.0, 0.0), axis=0, keepdims=True)
    slot = jnp.where(live_ref[...] > 0, owner * capacity + rank, -1.0).astype(jnp.int32)
    chosen = (iota((slots, held), 0) == slot).astype(jnp.float32).astype(jnp.bfloat16)
    cell = cell_ref[...]
    kind = iota((LANES, held), 0)
    upper = (lax.shift_right_logical(cell, 6) + 1).astype(jnp.float32)
    lower = (cell & 63).astype(jnp.float32)
    codes = jnp.where(kind == 0, upper, jnp.where(kind == 1, lower, 0.0)).astype(jnp.bfloat16)
    sent = lax.dot_general(chosen, codes, (((1,), (1,)), ((), ())), preferred_element_type=jnp.float32)
    out_ref[:, samples:] = sent.astype(jnp.bfloat16)
    copies[3].wait()
    rows = jnp.dot(chosen, traces_ref[...], preferred_element_type=jnp.float32)
    out_ref[:, :samples] = rows.astype(jnp.bfloat16)
    for copy in copies[4:]:
        copy.wait()


def bin_kernel(got_ref, p1_ref, p2_ref, b_ref, diag_ref, row0_ref, row7_ref, ends_ref):
    rows, tiles, cols, _ = b_ref.shape
    samples = tiles * LANES
    slots = got_ref.shape[0]
    kind = iota((SUBLANES, LANES), 1)
    weight = jnp.where(kind == 0, 64.0, jnp.where(kind == 1, 1.0, 0.0)).astype(jnp.bfloat16)
    value = lax.dot_general(
        weight, got_ref[:, samples:], (((1,), (1,)), ((), ())), preferred_element_type=jnp.float32
    )
    bin_of = value[:1].astype(jnp.int32) - 64
    not_first_row = (lax.axis_index("inl") > 0).astype(jnp.float32)
    not_first_col = (lax.axis_index("xl") > 0).astype(jnp.float32)
    ones = jnp.ones((slots, LANES), jnp.bfloat16)
    first_col = jnp.where(iota((cols, LANES), 0) == 0, not_first_col, 0.0) - SHIFT
    got = got_ref[:, :samples]
    for i in range(rows):
        place = (iota((cols, slots), 0) + i * cols == bin_of).astype(jnp.float32).astype(jnp.bfloat16)
        total = jnp.dot(place, got, preferred_element_type=jnp.float32)
        for c in range(tiles):
            b_ref[i, c] = total[:, c * LANES : (c + 1) * LANES]
        hits = jnp.dot(place, ones, preferred_element_type=jnp.float32)
        diag = 2.0 * hits + first_col
        diag_ref[i] = diag + not_first_row if i == 0 else diag
    write_edges(
        b_ref, lambda at: load(p1_ref, at), lambda i: load(p2_ref, i, slice(None)), row0_ref, row7_ref, ends_ref
    )


def write_edges(v_ref, p1_last_row, p2_last_cols, row0_ref, row7_ref, ends_ref):
    rows, _, cols, _ = v_ref.shape
    for x in range(0, cols, SUBLANES):
        at = slice(x, x + SUBLANES)
        store(row0_ref, load_field(v_ref, 0, at), at)
        v = load_field(v_ref, rows - 1, at)
        store(row7_ref, add(v, dip_part(p1_last_row(at), *stencil(v))), at)
    for i in range(rows):
        store(ends_ref, load_field(v_ref, i, slice(0, 1)), 0, slice(i, i + 1))
        v = load_field(v_ref, i, slice(cols - SUBLANES, cols))
        moved = add(v, dip_part(p2_last_cols(i), *stencil(v)))
        store(ends_ref, [t[SUBLANES - 1 :] for t in moved], 1, slice(i, i + 1))


def apply_kernel(v_ref, p1_ref, p2_ref, diag_ref, out_ref, sums_ref, first_ref, second_ref):
    rows, tiles, cols, _ = v_ref.shape
    sub_index = iota((SUBLANES, LANES), 0)
    zero = [jnp.zeros((SUBLANES, LANES), jnp.float32)] * tiles
    first_ref[...] = jnp.zeros_like(first_ref)
    for c in range(tiles):
        second_ref[c, :SUBLANES, :] = zero[0]

    def row(i, sums, last):
        v_row, out_row, diag_row = v_ref.at[i], out_ref.at[i], diag_ref.at[i]
        p1_row, p2_row = p1_ref.at[i], p2_ref.at[i]
        below_row = None if last else v_ref.at[i + 1]
        vout, vv = zero[0], zero[0]
        for x in range(0, cols, SUBLANES):
            at = slice(x, x + SUBLANES)
            v = load_tiles(v_row, at)
            if x + SUBLANES < cols:
                right = load_tiles(v_row, slice(x + 1, x + 1 + SUBLANES))
            else:
                right = [jnp.where(sub_index == SUBLANES - 1, 0.0, pltpu.roll(t, SUBLANES - 1, 0)) for t in v]
            below = zero if last else load_tiles(below_row, at)
            p1, p2 = load(p1_row, at), load(p2_row, at)
            odd, even = stencil(v)
            first = sub(sub(below, v), dip_part(p1, odd, even))
            second = sub(sub(right, v), dip_part(p2, odd, even))
            for c in range(tiles):
                second_ref[c, x + SUBLANES : x + 2 * SUBLANES, :] = second[c]
            a1, b1 = adjoint_terms(p1, first)
            a2, b2 = adjoint_terms(p2, second)
            moved = adjoint_finish(add(first, second), add(a1, a2), add(b1, b2))
            left = [second_ref[c, x + SUBLANES - 1 : x + 2 * SUBLANES - 1, :] for c in range(tiles)]
            above = load(first_ref, at)
            store(first_ref, first, at)
            diag = diag_row[at, :]
            out = [diag * c + ((f + s) - m) for c, f, s, m in zip(v, above, left, moved)]
            for c in range(tiles):
                out_row[c, at, :] = out[c]
            vout = vout + dot(v, out)
            vv = vv + dot(v, v)
        return sums[0] + vout, sums[1] + vv

    sums = lax.fori_loop(0, rows - 1, lambda i, sums: row(i, sums, False), (zero[0], zero[0]))
    sums_ref[0], sums_ref[1] = row(rows - 1, sums, True)


def halo_corrections(out_ref, p1_ref, p2_ref, below_ref, above_ref, right_ref, left_ref):
    rows, _, cols, _ = out_ref.shape
    last = rows - 1
    sub_index = iota((SUBLANES, LANES), 0)
    for x in range(0, cols, SUBLANES):
        at = slice(x, x + SUBLANES)
        store_field(out_ref, sub(load_field(out_ref, 0, at), load(above_ref, at)), 0, at)
        r = load(below_ref, at)
        moved = adjoint_finish(r, *adjoint_terms(load(p1_ref, last, at), r))
        store_field(out_ref, sub(load_field(out_ref, last, at), moved), last, at)
    for i in range(rows):
        at = slice(0, SUBLANES)
        r = [jnp.where(sub_index == 0, t, 0.0) for t in load(left_ref, slice(i, i + 1))]
        store_field(out_ref, sub(load_field(out_ref, i, at), r), i, at)
        at = slice(cols - SUBLANES, cols)
        r = [jnp.where(sub_index == SUBLANES - 1, t, 0.0) for t in load(right_ref, slice(i, i + 1))]
        moved = adjoint_finish(r, *adjoint_terms(load(p2_ref, i, at), r))
        store_field(out_ref, sub(load_field(out_ref, i, at), moved), i, at)


def settle(image_ref, p1_ref, p2_ref, below_ref, above_ref, gathered_hbm, row7_ref, ends_ref, out_ref, side_ref, sems):
    here, count = lax.axis_index("xl"), lax.axis_size("xl")
    copies = (
        pltpu.make_async_copy(gathered_hbm.at[jnp.minimum(here + 1, count - 1), 0], side_ref.at[0], sems.at[0]),
        pltpu.make_async_copy(gathered_hbm.at[jnp.maximum(here - 1, 0), 1], side_ref.at[1], sems.at[1]),
    )
    for copy in copies:
        copy.start()
    across = jnp.zeros((SUBLANES, LANES), jnp.float32)
    for x in range(0, row7_ref.shape[0], SUBLANES):
        at = slice(x, x + SUBLANES)
        across = across + dot(load(row7_ref, at), load(below_ref, at))
    for copy in copies:
        copy.wait()
    side_ref[0] = jnp.where(here + 1 < count, side_ref[0], 0.0)
    side_ref[1] = jnp.where(here > 0, side_ref[1], 0.0)
    for x in range(0, ends_ref.shape[1], SUBLANES):
        at = slice(x, x + SUBLANES)
        across = across + dot(load(ends_ref, 1, at), load(side_ref, 0, at))
    halo_corrections(out_ref, p1_ref, p2_ref, below_ref, above_ref, side_ref.at[0], side_ref.at[1])
    return across


def correct_kernel(
    image_ref, p1_ref, p2_ref, below_ref, above_ref, gathered_hbm, row7_ref, ends_ref,
    out_ref, across_ref, next_row0_ref, next_row7_ref, next_ends_ref, side_ref, sems,
):
    across_ref[...] = settle(
        image_ref, p1_ref, p2_ref, below_ref, above_ref, gathered_hbm, row7_ref, ends_ref, out_ref, side_ref, sems
    )
    rows, _, cols, _ = out_ref.shape
    write_edges(
        out_ref,
        lambda at: load(p1_ref, rows - 1, at),
        lambda i: load(p2_ref, i, slice(cols - SUBLANES, cols)),
        next_row0_ref, next_row7_ref, next_ends_ref,
    )


def moments_kernel(
    image_ref, p1_ref, p2_ref, below_ref, above_ref, gathered_hbm, row7_ref, ends_ref, *refs
):
    sums_refs, across_refs = refs[:ITERS], refs[ITERS : 2 * ITERS - 1]
    out_ref, message_ref, side_ref, sems = refs[2 * ITERS - 1 :]
    final = settle(
        image_ref, p1_ref, p2_ref, below_ref, above_ref, gathered_hbm, row7_ref, ends_ref, out_ref, side_ref, sems
    )
    m = []
    for sums_ref, across in zip(sums_refs, [ref[...] for ref in across_refs] + [final]):
        m.append(sums_ref[1])
        m.append(sums_ref[0] - 2.0 * across)
    sub_index, lane = iota((SUBLANES, LANES), 0), iota((SUBLANES, LANES), 1)
    block = jnp.zeros((SUBLANES, LANES), jnp.float32)
    for k, part in enumerate(m):
        block = jnp.where(sub_index == k, jnp.sum(part, axis=0, keepdims=True), block)
    total = jnp.sum(block, axis=1, keepdims=True)
    line = jnp.sum(jnp.where(sub_index == lane, total, 0.0), axis=0, keepdims=True)
    message_ref[...] = jnp.broadcast_to(line, message_ref.shape)


def coefficients(m):
    zero = jnp.zeros_like(m[0])
    model = [zero] * ITERS
    residual = [zero + 1.0] + [zero] * ITERS
    direction = [zero + 1.0] + [zero] * (ITERS - 1)
    norm_now = m[0]

    def inner(x, y, count):
        total = zero
        for i in range(count):
            for j in range(len(y)):
                if i + j < len(m):
                    total = total + x[i] * y[j] * m[i + j]
        return total

    for sweep in range(ITERS):
        image = [SHIFT * d for d in direction] + [zero]
        image = [image[0]] + [s + d for s, d in zip(image[1:], direction)]
        alpha = norm_now / inner(direction, image[: sweep + 2], sweep + 1)
        model = [s + alpha * d for s, d in zip(model, direction)]
        residual = [r - alpha * d for r, d in zip(residual, image)]
        if sweep + 1 < ITERS:
            norm_next = inner(residual, residual[: sweep + 2], sweep + 2)
            beta = norm_next / norm_now
            direction = [r + beta * d for r, d in zip(residual, direction)]
            norm_now = norm_next
    return [2.0 * s for s in model] + residual


def finish_kernel(parts_ref, b_ref, v1_ref, v2_ref, v3_ref, model_hbm, residual_hbm, model_ref, residual_ref, sems):
    rows, _, cols, _ = b_ref.shape
    line = jnp.sum(parts_ref[...], axis=0)[:1]
    sub_index, lane = iota((SUBLANES, LANES), 0), iota((SUBLANES, LANES), 1)
    total = jnp.sum(jnp.where(sub_index == lane, line, 0.0), axis=1, keepdims=True)
    total = jnp.broadcast_to(total, (SUBLANES, LANES))
    m = [jnp.broadcast_to(total[k : k + 1], (SUBLANES, LANES)) for k in range(2 * ITERS)]
    weights = coefficients(m)
    model, residual = weights[:ITERS], weights[ITERS:]

    def copies(i):
        return (
            pltpu.make_async_copy(model_ref.at[i], model_hbm.at[i], sems.at[0, i]),
            pltpu.make_async_copy(residual_ref.at[i], residual_hbm.at[i], sems.at[1, i]),
        )

    def body(i, carry):
        for x in range(0, cols, SUBLANES):
            at = slice(x, x + SUBLANES)
            b, v1, v2, v3 = (load_field(ref, i, at) for ref in (b_ref, v1_ref, v2_ref, v3_ref))
            store(model_ref, [model[0] * s + model[1] * t + model[2] * u for s, t, u in zip(b, v1, v2)], i, at)
            store(
                residual_ref,
                [(residual[0] * s + residual[1] * t) + (residual[2] * u + residual[3] * w) for s, t, u, w in zip(b, v1, v2, v3)],
                i, at,
            )
        for copy in copies(i):
            copy.start()
        return carry

    lax.fori_loop(0, rows, body, 0)
    for i in range(rows):
        for copy in copies(i):
            copy.wait()


def f32(*shape):
    return pltpu.VMEM(shape, jnp.float32)


def call(kernel, outs, *args, name, scratch=(), aliases=None, cost=None, ins=None, places=None):
    return pl.pallas_call(
        kernel,
        out_shape=outs,
        in_specs=ins or [IN_VMEM] * len(args),
        out_specs=places or [IN_VMEM] * len(outs),
        scratch_shapes=list(scratch),
        input_output_aliases=aliases or {},
        compiler_params=PARAMS,
        cost_estimate=cost,
        name=name,
    )(*args)


def in_hbm(array):
    return pltpu.with_memory_space_constraint(array, pltpu.HBM)


def per_device(traces, trace_owner, trace_cell, acquired, inline_dip, cross_dip):
    rows, cols, samples = inline_dip.shape
    devices = lax.axis_size("inl") * lax.axis_size("xl")
    held = traces.shape[0]
    capacity = max(2, 2 * held // devices)
    slots = devices * capacity
    small = pltpu.VMEM((1, held), jnp.int32)
    inputs = (trace_owner.reshape(1, held), trace_cell[None], acquired[None], traces, inline_dip, cross_dip)
    sent, p1_last, p2_last = call(
        functools.partial(pack_kernel, capacity),
        [
            jax.ShapeDtypeStruct((slots, samples + LANES), jnp.bfloat16),
            f32(cols, samples),
            f32(rows, SUBLANES, samples),
        ],
        *(in_hbm(x) for x in inputs),
        name="pack", ins=[IN_HBM] * len(inputs),
        scratch=[small, small, small, pltpu.VMEM((held, samples), jnp.bfloat16), pltpu.SemaphoreType.DMA((6,))],
    )
    got = lax.all_to_all(sent, ("inl", "xl"), split_axis=0, concat_axis=0, tiled=True)
    edge_shapes = [f32(cols, samples), f32(cols, samples), jax.ShapeDtypeStruct((2, rows, samples), jnp.float32)]
    tile = f32(rows, samples // LANES, cols, LANES)
    b, diag, *edges = call(
        bin_kernel, [tile, f32(rows, cols, LANES)] + edge_shapes, got, p1_last, p2_last, name="bin"
    )
    fields, sums, products = [b], [], []
    cost = pl.CostEstimate(
        flops=60 * rows * cols * samples, bytes_accessed=16 * rows * cols * samples, transcendentals=0
    )
    side = [pltpu.VMEM((2, rows, samples), jnp.float32), pltpu.SemaphoreType.DMA((2,))]
    for step in range(ITERS):
        row0, row7, ends = edges
        gathered = lax.all_gather(ends, "xl")
        below = shifted(row0, "inl", -1)
        above = shifted(row7, "inl", 1)
        image, partial = call(
            apply_kernel,
            [tile, f32(2, SUBLANES, LANES)],
            fields[-1], inline_dip, cross_dip, diag,
            name="apply",
            scratch=[
                pltpu.VMEM((cols, samples), jnp.float32),
                pltpu.VMEM((samples // LANES, SUBLANES + cols, LANES), jnp.float32),
            ],
            cost=cost,
        )
        sums.append(partial)
        args = [image, inline_dip, cross_dip, below, above, in_hbm(gathered), row7, ends]
        places = [IN_VMEM] * 5 + [IN_HBM] + [IN_VMEM] * 2
        if step + 1 < ITERS:
            image, across, *edges = call(
                correct_kernel, [tile, f32(SUBLANES, LANES)] + edge_shapes, *args,
                name="correct", aliases={0: 0}, ins=places, scratch=side,
            )
            products.append(across)
        else:
            image, message = call(
                moments_kernel, [tile, jax.ShapeDtypeStruct((SUBLANES, LANES), jnp.float32)], *args, *sums, *products,
                name="moments", aliases={0: 0}, ins=places + [IN_VMEM] * (2 * ITERS - 1), scratch=side,
            )
        fields.append(image)
    parts = lax.all_gather(message, ("inl", "xl"))
    out = jax.ShapeDtypeStruct((rows, cols, samples), jnp.float32)
    return tuple(
        call(
            finish_kernel, [out, out], parts, *fields,
            name="finish", places=[pl.BlockSpec(memory_space=pl.ANY)] * 2,
            scratch=[
                pltpu.VMEM((rows, cols, samples), jnp.float32),
                pltpu.VMEM((rows, cols, samples), jnp.float32),
                pltpu.SemaphoreType.DMA((2, rows)),
            ],
        )
    )


def solution(mesh):
    placed = (
        P(("inl", "xl"), None),
        P(("inl", "xl"), None),
        P(("inl", "xl")),
        P(("inl", "xl")),
        P("inl", "xl", None),
        P("inl", "xl", None),
    )
    return jax.shard_map(
        per_device,
        mesh=mesh,
        in_specs=placed,
        out_specs=(P("inl", "xl", None), P("inl", "xl", None)),
        check_vma=False,
    )
```

```python
import functools

import jax
import jax.numpy as jnp
from jax import lax
from jax.experimental import pallas as pl
from jax.experimental.pallas import tpu as pltpu
from jax.sharding import PartitionSpec as P

ITERS = 3
LANES = 128
SUBLANES = 8
GROUP = 32

SHIFT = 6.0
IN_VMEM = pl.BlockSpec(memory_space=pltpu.VMEM)
IN_HBM = pl.BlockSpec(memory_space=pltpu.HBM)
PARAMS = pltpu.CompilerParams(vmem_limit_bytes=16 << 20)


def shifted(value, axis, steps):
    count = lax.axis_size(axis)
    initial, last = (max(0, -steps), min(count, count - steps))
    return lax.ppermute(value, axis, [(source, source + steps) for source in range(initial, last)])


def iota(shape, dim):
    return lax.broadcasted_iota(jnp.int32, shape, dim)


def earlier(tiles):
    lane = iota(tiles[0].shape, 1)
    rolled = [pltpu.roll(tile, 1, 1) for tile in tiles]
    before = [jnp.zeros_like(tiles[0])] + rolled[:-1]
    return [jnp.where(lane == 0, edge, inner) for edge, inner in zip(before, rolled)]


def later(tiles):
    lane = iota(tiles[0].shape, 1)
    rolled = [pltpu.roll(tile, LANES - 1, 1) for tile in tiles]
    after = rolled[1:] + [jnp.zeros_like(tiles[0])]
    return [jnp.where(lane == LANES - 1, edge, inner) for edge, inner in zip(after, rolled)]


def stencil(v):
    em, ep = earlier(v), later(v)
    odd = [m - p for m, p in zip(em, ep)]
    even = [(m + p) - (c + c) for m, p, c in zip(em, ep, v)]
    return odd, even


def dip_part(p, odd, even):
    return [(0.5 * d) * (o + d * e) for d, o, e in zip(p, odd, even)]


def adjoint_terms(p, r):
    a = [(0.5 * d) * x for d, x in zip(p, r)]
    b = [d * x for d, x in zip(p, a)]
    return a, b


def adjoint_finish(r, a, b):
    up = later([x + y for x, y in zip(a, b)])
    down = earlier([y - x for x, y in zip(a, b)])
    return [(x + u) + (d - (y + y)) for x, u, d, y in zip(r, up, down, b)]


def load(ref, *index):
    count = ref.shape[-1] // LANES
    return [ref[(*index, slice(c * LANES, (c + 1) * LANES))] for c in range(count)]


def store(ref, tiles, *index):
    for c, tile in enumerate(tiles):
        ref[(*index, slice(c * LANES, (c + 1) * LANES))] = tile


def load_tiles(ref, at):
    return [ref[c, at, :] for c in range(ref.shape[0])]


def load_field(ref, i, at):
    return [ref[i, c, at, :] for c in range(ref.shape[1])]


def store_field(ref, tiles, i, at):
    for c, tile in enumerate(tiles):
        ref[i, c, at, :] = tile


def add(x, y):
    return [a + b for a, b in zip(x, y)]


def sub(x, y):
    return [a - b for a, b in zip(x, y)]


def dot(x, y):
    return functools.reduce(lambda s, t: s + t, [a * b for a, b in zip(x, y)])


def pack_kernel(
    capacity, owner_hbm, cell_hbm, live_hbm, traces_hbm, p1_hbm, p2_hbm, out_ref, p1_last_ref, p2_last_ref,
    owner_ref, cell_ref, live_ref, traces_ref, sems,
):
    held, samples = traces_ref.shape
    slots = out_ref.shape[0]
    rows, cols, _ = p1_hbm.shape
    pairs = (
        (owner_hbm, owner_ref), (cell_hbm, cell_ref), (live_hbm, live_ref), (traces_hbm, traces_ref),
        (p1_hbm.at[rows - 1], p1_last_ref), (p2_hbm.at[:, pl.ds(cols - SUBLANES, SUBLANES)], p2_last_ref),
    )
    copies = [pltpu.make_async_copy(src, dst, sems.at[k]) for k, (src, dst) in enumerate(pairs)]
    for copy in copies:
        copy.start()
    for copy in copies[:3]:
        copy.wait()
    owner = owner_ref[...].astype(jnp.float32)
    row, col = iota((held, held), 0), iota((held, held), 1)
    owner_down = jnp.sum(jnp.where(row == col, owner, 0.0), axis=1, keepdims=True)
    earlier_same = (owner_down == owner) & (row < col)
    rank = jnp.sum(jnp.where(earlier_same, 1.0, 0.0), axis=0, keepdims=True)
    slot = jnp.where(live_ref[...] > 0, owner * capacity + rank, -1.0).astype(jnp.int32)
    chosen = (iota((slots, held), 0) == slot).astype(jnp.float32).astype(jnp.bfloat16)
    cell = cell_ref[...]
    kind = iota((LANES, held), 0)
    upper = (lax.shift_right_logical(cell, 6) + 1).astype(jnp.float32)
    lower = (cell & 63).astype(jnp.float32)
    codes = jnp.where(kind == 0, upper, jnp.where(kind == 1, lower, 0.0)).astype(jnp.bfloat16)
    sent = lax.dot_general(chosen, codes, (((1,), (1,)), ((), ())), preferred_element_type=jnp.float32)
    out_ref[:, samples:] = sent.astype(jnp.bfloat16)
    copies[3].wait()
    rows = jnp.dot(chosen, traces_ref[...], preferred_element_type=jnp.float32)
    out_ref[:, :samples] = rows.astype(jnp.bfloat16)
    for copy in copies[4:]:
        copy.wait()


def bin_kernel(got_ref, p1_ref, p2_ref, b_ref, diag_ref, *edge_refs):
    rows, tiles, cols, _ = b_ref.shape
    samples = tiles * LANES
    slots = got_ref.shape[0]
    kind = iota((SUBLANES, LANES), 1)
    weight = jnp.where(kind == 0, 64.0, jnp.where(kind == 1, 1.0, 0.0)).astype(jnp.bfloat16)
    value = lax.dot_general(
        weight, got_ref[:, samples:], (((1,), (1,)), ((), ())), preferred_element_type=jnp.float32
    )
    bin_of = value[:1].astype(jnp.int32) - 64
    not_first_row = (lax.axis_index("inl") > 0).astype(jnp.float32)
    not_first_col = (lax.axis_index("xl") > 0).astype(jnp.float32)
    ones = jnp.ones((slots, LANES), jnp.bfloat16)
    first_col = jnp.where(iota((cols, LANES), 0) == 0, not_first_col, 0.0) - SHIFT
    got = got_ref[:, :samples]
    for i in range(rows):
        place = (iota((cols, slots), 0) + i * cols == bin_of).astype(jnp.float32).astype(jnp.bfloat16)
        total = jnp.dot(place, got, preferred_element_type=jnp.float32)
        for c in range(tiles):
            b_ref[i, c] = total[:, c * LANES : (c + 1) * LANES]
        hits = jnp.dot(place, ones, preferred_element_type=jnp.float32)
        diag = 2.0 * hits + first_col
        diag_ref[i] = diag + not_first_row if i == 0 else diag
    write_edges(
        b_ref, lambda at: load(p1_ref, at), lambda i: load(p2_ref, i, slice(None)), *edge_refs
    )


def write_edges(v_ref, p1_last_row, p2_last_cols, row0_ref, row7_ref, col0_ref, col7_ref):
    rows, _, cols, _ = v_ref.shape
    for x in range(0, cols, SUBLANES):
        at = slice(x, x + SUBLANES)
        store(row0_ref, load_field(v_ref, 0, at), at)
        v = load_field(v_ref, rows - 1, at)
        store(row7_ref, add(v, dip_part(p1_last_row(at), *stencil(v))), at)
    for i in range(rows):
        store(col0_ref, load_field(v_ref, i, slice(0, 1)), slice(i, i + 1))
        v = load_field(v_ref, i, slice(cols - SUBLANES, cols))
        moved = add(v, dip_part(p2_last_cols(i), *stencil(v)))
        store(col7_ref, [t[SUBLANES - 1 :] for t in moved], slice(i, i + 1))


def apply_kernel(v_ref, p1_ref, p2_ref, diag_ref, out_ref, sums_ref, first_ref, second_ref):
    rows, tiles, cols, _ = v_ref.shape
    sub_index = iota((SUBLANES, LANES), 0)
    zero = [jnp.zeros((SUBLANES, LANES), jnp.float32)] * tiles
    first_ref[...] = jnp.zeros_like(first_ref)
    for i in range(rows):
        for c in range(tiles):
            second_ref[i, c, :SUBLANES, :] = zero[0]

    def body(i, sums, group, last):
        v_row, out_row, diag_row, second_row = v_ref.at[i], out_ref.at[i], diag_ref.at[i], second_ref.at[i]
        p1_row, p2_row = p1_ref.at[i], p2_ref.at[i]
        below_row = None if last else v_ref.at[i + 1]
        vout, vv = zero[0], zero[0]
        for x in range(group, group + GROUP, SUBLANES):
            at = slice(x, x + SUBLANES)
            v = load_tiles(v_row, at)
            if x + SUBLANES < cols:
                right = load_tiles(v_row, slice(x + 1, x + 1 + SUBLANES))
            else:
                right = [jnp.where(sub_index == SUBLANES - 1, 0.0, pltpu.roll(t, SUBLANES - 1, 0)) for t in v]
            below = zero if last else load_tiles(below_row, at)
            p1, p2 = load(p1_row, at), load(p2_row, at)
            odd, even = stencil(v)
            first = sub(sub(below, v), dip_part(p1, odd, even))
            second = sub(sub(right, v), dip_part(p2, odd, even))
            for c in range(tiles):
                second_row[c, x + SUBLANES : x + 2 * SUBLANES, :] = second[c]
            a1, b1 = adjoint_terms(p1, first)
            a2, b2 = adjoint_terms(p2, second)
            moved = adjoint_finish(add(first, second), add(a1, a2), add(b1, b2))
            left = [second_row[c, x + SUBLANES - 1 : x + 2 * SUBLANES - 1, :] for c in range(tiles)]
            above = load(first_ref, at)
            store(first_ref, first, at)
            diag = diag_row[at, :]
            out = [diag * c + ((f + s) - m) for c, f, s, m in zip(v, above, left, moved)]
            for c in range(tiles):
                out_row[c, at, :] = out[c]
            vout = vout + dot(v, out)
            vv = vv + dot(v, v)
        return sums[0] + vout, sums[1] + vv

    total = (zero[0], zero[0])
    for group in range(0, cols, GROUP):
        sums = lax.fori_loop(
            0, rows - 1, functools.partial(body, group=group, last=False), (zero[0], zero[0])
        )
        sums = body(rows - 1, sums, group, True)
        total = (total[0] + sums[0], total[1] + sums[1])
    sums_ref[0], sums_ref[1] = total


def halo_corrections(out_ref, p1_ref, p2_ref, below_ref, above_ref, right_ref, left_ref):
    rows, _, cols, _ = out_ref.shape
    last = rows - 1
    sub_index = iota((SUBLANES, LANES), 0)
    for x in range(0, cols, SUBLANES):
        at = slice(x, x + SUBLANES)
        store_field(out_ref, sub(load_field(out_ref, 0, at), load(above_ref, at)), 0, at)
        r = load(below_ref, at)
        moved = adjoint_finish(r, *adjoint_terms(load(p1_ref, last, at), r))
        store_field(out_ref, sub(load_field(out_ref, last, at), moved), last, at)
    for i in range(rows):
        at = slice(0, SUBLANES)
        r = [jnp.where(sub_index == 0, t, 0.0) for t in load(left_ref, slice(i, i + 1))]
        store_field(out_ref, sub(load_field(out_ref, i, at), r), i, at)
        at = slice(cols - SUBLANES, cols)
        r = [jnp.where(sub_index == SUBLANES - 1, t, 0.0) for t in load(right_ref, slice(i, i + 1))]
        moved = adjoint_finish(r, *adjoint_terms(load(p2_ref, i, at), r))
        store_field(out_ref, sub(load_field(out_ref, i, at), moved), i, at)


def settle(image_ref, p1_ref, p2_ref, below_ref, above_ref, right_ref, left_ref, row7_ref, col7_ref, out_ref):
    across = jnp.zeros((SUBLANES, LANES), jnp.float32)
    for mine, theirs in ((row7_ref, below_ref), (col7_ref, right_ref)):
        for x in range(0, mine.shape[0], SUBLANES):
            at = slice(x, x + SUBLANES)
            across = across + dot(load(mine, at), load(theirs, at))
    halo_corrections(out_ref, p1_ref, p2_ref, below_ref, above_ref, right_ref, left_ref)
    return across


def correct_kernel(
    image_ref, p1_ref, p2_ref, below_ref, above_ref, right_ref, left_ref, row7_ref, col7_ref,
    out_ref, across_ref, *edge_refs,
):
    across_ref[...] = settle(
        image_ref, p1_ref, p2_ref, below_ref, above_ref, right_ref, left_ref, row7_ref, col7_ref, out_ref
    )
    rows, _, cols, _ = out_ref.shape
    write_edges(
        out_ref,
        lambda at: load(p1_ref, rows - 1, at),
        lambda i: load(p2_ref, i, slice(cols - SUBLANES, cols)),
        *edge_refs,
    )


def moments_kernel(
    image_ref, p1_ref, p2_ref, below_ref, above_ref, right_ref, left_ref, row7_ref, col7_ref, *refs
):
    sums_refs, across_refs = refs[:ITERS], refs[ITERS : 2 * ITERS - 1]
    out_ref, message_ref = refs[2 * ITERS - 1 :]
    final = settle(
        image_ref, p1_ref, p2_ref, below_ref, above_ref, right_ref, left_ref, row7_ref, col7_ref, out_ref
    )
    m = []
    for sums_ref, across in zip(sums_refs, [ref[...] for ref in across_refs] + [final]):
        m.append(sums_ref[1])
        m.append(sums_ref[0] - 2.0 * across)
    sub_index, lane = iota((SUBLANES, LANES), 0), iota((SUBLANES, LANES), 1)
    block = jnp.zeros((SUBLANES, LANES), jnp.float32)
    for k, part in enumerate(m):
        block = jnp.where(sub_index == k, jnp.sum(part, axis=0, keepdims=True), block)
    total = jnp.sum(block, axis=1, keepdims=True)
    line = jnp.sum(jnp.where(sub_index == lane, total, 0.0), axis=0, keepdims=True)
    message_ref[...] = jnp.broadcast_to(line[None], message_ref.shape)


def coefficients(m):
    zero = jnp.zeros_like(m[0])
    model = [zero] * ITERS
    residual = [zero + 1.0] + [zero] * ITERS
    direction = [zero + 1.0] + [zero] * (ITERS - 1)
    norm_now = m[0]

    def inner(x, y, count):
        total = zero
        for i in range(count):
            for j in range(len(y)):
                if i + j < len(m):
                    total = total + x[i] * y[j] * m[i + j]
        return total

    for sweep in range(ITERS):
        image = [SHIFT * d for d in direction] + [zero]
        image = [image[0]] + [s + d for s, d in zip(image[1:], direction)]
        alpha = norm_now / inner(direction, image[: sweep + 2], sweep + 1)
        model = [s + alpha * d for s, d in zip(model, direction)]
        residual = [r - alpha * d for r, d in zip(residual, image)]
        if sweep + 1 < ITERS:
            norm_next = inner(residual, residual[: sweep + 2], sweep + 2)
            beta = norm_next / norm_now
            direction = [r + beta * d for r, d in zip(residual, direction)]
            norm_now = norm_next
    return [2.0 * s for s in model] + residual


def finish_kernel(parts_ref, b_ref, v1_ref, v2_ref, v3_ref, model_hbm, residual_hbm, model_ref, residual_ref, sems):
    rows, _, cols, _ = b_ref.shape
    line = jnp.sum(parts_ref[...], axis=0)
    sub_index, lane = iota((SUBLANES, LANES), 0), iota((SUBLANES, LANES), 1)
    total = jnp.sum(jnp.where(sub_index == lane, line, 0.0), axis=1, keepdims=True)
    total = jnp.broadcast_to(total, (SUBLANES, LANES))
    m = [jnp.broadcast_to(total[k : k + 1], (SUBLANES, LANES)) for k in range(2 * ITERS)]
    weights = coefficients(m)
    model, residual = weights[:ITERS], weights[ITERS:]

    def copies(i):
        return (
            pltpu.make_async_copy(model_ref.at[i], model_hbm.at[i], sems.at[0, i]),
            pltpu.make_async_copy(residual_ref.at[i], residual_hbm.at[i], sems.at[1, i]),
        )

    def body(i, carry):
        for x in range(0, cols, SUBLANES):
            at = slice(x, x + SUBLANES)
            b, v1, v2, v3 = (load_field(ref, i, at) for ref in (b_ref, v1_ref, v2_ref, v3_ref))
            store(model_ref, [model[0] * s + model[1] * t + model[2] * u for s, t, u in zip(b, v1, v2)], i, at)
            store(
                residual_ref,
                [(residual[0] * s + residual[1] * t) + (residual[2] * u + residual[3] * w) for s, t, u, w in zip(b, v1, v2, v3)],
                i, at,
            )
        for copy in copies(i):
            copy.start()
        return carry

    lax.fori_loop(0, rows, body, 0)
    for i in range(rows):
        for copy in copies(i):
            copy.wait()


def f32(*shape):
    return pltpu.VMEM(shape, jnp.float32)


def call(kernel, outs, *args, name, scratch=(), aliases=None, cost=None, ins=None, places=None):
    return pl.pallas_call(
        kernel,
        out_shape=outs,
        in_specs=ins or [IN_VMEM] * len(args),
        out_specs=places or [IN_VMEM] * len(outs),
        scratch_shapes=list(scratch),
        input_output_aliases=aliases or {},
        compiler_params=PARAMS,
        cost_estimate=cost,
        name=name,
    )(*args)


def in_hbm(array):
    return pltpu.with_memory_space_constraint(array, pltpu.HBM)


def per_device(traces, trace_owner, trace_cell, acquired, inline_dip, cross_dip):
    rows, cols, samples = inline_dip.shape
    devices = lax.axis_size("inl") * lax.axis_size("xl")
    held = traces.shape[0]
    capacity = max(2, 2 * held // devices)
    slots = devices * capacity
    small = pltpu.VMEM((1, held), jnp.int32)
    inputs = (trace_owner.reshape(1, held), trace_cell[None], acquired[None], traces, inline_dip, cross_dip)
    sent, p1_last, p2_last = call(
        functools.partial(pack_kernel, capacity),
        [
            jax.ShapeDtypeStruct((slots, samples + LANES), jnp.bfloat16),
            f32(cols, samples),
            f32(rows, SUBLANES, samples),
        ],
        *(in_hbm(x) for x in inputs),
        name="pack", ins=[IN_HBM] * len(inputs),
        scratch=[small, small, small, pltpu.VMEM((held, samples), jnp.bfloat16), pltpu.SemaphoreType.DMA((6,))],
    )
    got = lax.all_to_all(sent, ("inl", "xl"), split_axis=0, concat_axis=0, tiled=True)
    edge_shapes = [f32(cols, samples), f32(cols, samples), f32(rows, samples), f32(rows, samples)]
    tile = f32(rows, samples // LANES, cols, LANES)
    b, diag, *edges = call(
        bin_kernel, [tile, f32(rows, cols, LANES)] + edge_shapes, got, p1_last, p2_last, name="bin"
    )
    fields, sums, products = [b], [], []
    cost = pl.CostEstimate(
        flops=60 * rows * cols * samples, bytes_accessed=16 * rows * cols * samples, transcendentals=0
    )
    for step in range(ITERS):
        row0, row7, col0, col7 = edges
        below = shifted(row0, "inl", -1)
        above = shifted(row7, "inl", 1)
        right = shifted(col0, "xl", -1)
        left = shifted(col7, "xl", 1)
        image, partial = call(
            apply_kernel,
            [tile, f32(2, SUBLANES, LANES)],
            fields[-1], inline_dip, cross_dip, diag,
            name="apply",
            scratch=[
                pltpu.VMEM((cols, samples), jnp.float32),
                pltpu.VMEM((rows, samples // LANES, SUBLANES + cols, LANES), jnp.float32),
            ],
            cost=cost,
        )
        sums.append(partial)
        args = [image, inline_dip, cross_dip, below, above, right, left, row7, col7]
        if step + 1 < ITERS:
            image, across, *edges = call(
                correct_kernel, [tile, f32(SUBLANES, LANES)] + edge_shapes, *args, name="correct", aliases={0: 0}
            )
            products.append(across)
        else:
            image, message = call(
                moments_kernel, [tile, f32(devices, 1, LANES)], *args, *sums, *products,
                name="moments", aliases={0: 0},
            )
        fields.append(image)
    parts = lax.all_to_all(message, ("inl", "xl"), split_axis=0, concat_axis=0, tiled=True)
    out = jax.ShapeDtypeStruct((rows, cols, samples), jnp.float32)
    return tuple(
        call(
            finish_kernel, [out, out], parts, *fields,
            name="finish", places=[pl.BlockSpec(memory_space=pl.ANY)] * 2,
            scratch=[
                pltpu.VMEM((rows, cols, samples), jnp.float32),
                pltpu.VMEM((rows, cols, samples), jnp.float32),
                pltpu.SemaphoreType.DMA((2, rows)),
            ],
        )
    )


def solution(mesh):
    placed = (
        P(("inl", "xl"), None),
        P(("inl", "xl"), None),
        P(("inl", "xl")),
        P(("inl", "xl")),
        P("inl", "xl", None),
        P("inl", "xl", None),
    )
    return jax.shard_map(
        per_device,
        mesh=mesh,
        in_specs=placed,
        out_specs=(P("inl", "xl", None), P("inl", "xl", None)),
        check_vma=False,
    )
```

```python
import functools

import jax
import jax.numpy as jnp
from jax import lax
from jax.experimental import pallas as pl
from jax.experimental.pallas import tpu as pltpu
from jax.sharding import PartitionSpec as P

ITERS = 3
LANES = 128
SUBLANES = 8

SHIFT = 6.0
IN_VMEM = pl.BlockSpec(memory_space=pltpu.VMEM)
IN_HBM = pl.BlockSpec(memory_space=pltpu.HBM)
PARAMS = pltpu.CompilerParams(vmem_limit_bytes=16 << 20)


def shifted(value, axis, steps):
    count = lax.axis_size(axis)
    initial, last = (max(0, -steps), min(count, count - steps))
    return lax.ppermute(value, axis, [(source, source + steps) for source in range(initial, last)])


def iota(shape, dim):
    return lax.broadcasted_iota(jnp.int32, shape, dim)


def earlier(tiles):
    lane = iota(tiles[0].shape, 1)
    rolled = [pltpu.roll(tile, 1, 1) for tile in tiles]
    before = [jnp.zeros_like(tiles[0])] + rolled[:-1]
    return [jnp.where(lane == 0, edge, inner) for edge, inner in zip(before, rolled)]


def later(tiles):
    lane = iota(tiles[0].shape, 1)
    rolled = [pltpu.roll(tile, LANES - 1, 1) for tile in tiles]
    after = rolled[1:] + [jnp.zeros_like(tiles[0])]
    return [jnp.where(lane == LANES - 1, edge, inner) for edge, inner in zip(after, rolled)]


def stencil(v):
    em, ep = earlier(v), later(v)
    odd = [m - p for m, p in zip(em, ep)]
    even = [(m + p) - (c + c) for m, p, c in zip(em, ep, v)]
    return odd, even


def dip_part(p, odd, even):
    return [(0.5 * d) * (o + d * e) for d, o, e in zip(p, odd, even)]


def adjoint_terms(p, r):
    a = [(0.5 * d) * x for d, x in zip(p, r)]
    b = [d * x for d, x in zip(p, a)]
    return a, b


def adjoint_finish(r, a, b):
    up = later([x + y for x, y in zip(a, b)])
    down = earlier([y - x for x, y in zip(a, b)])
    return [(x + u) + (d - (y + y)) for x, u, d, y in zip(r, up, down, b)]


def load(ref, *index):
    count = ref.shape[-1] // LANES
    return [ref[(*index, slice(c * LANES, (c + 1) * LANES))] for c in range(count)]


def store(ref, tiles, *index):
    for c, tile in enumerate(tiles):
        ref[(*index, slice(c * LANES, (c + 1) * LANES))] = tile


def load_tiles(ref, at):
    return [ref[c, at, :] for c in range(ref.shape[0])]


def load_field(ref, i, at):
    return [ref[i, c, at, :] for c in range(ref.shape[1])]


def store_field(ref, tiles, i, at):
    for c, tile in enumerate(tiles):
        ref[i, c, at, :] = tile


def add(x, y):
    return [a + b for a, b in zip(x, y)]


def sub(x, y):
    return [a - b for a, b in zip(x, y)]


def dot(x, y):
    return functools.reduce(lambda s, t: s + t, [a * b for a, b in zip(x, y)])


def pack_kernel(
    capacity, owner_hbm, cell_hbm, live_hbm, traces_hbm, p1_hbm, p2_hbm, out_ref, p1_last_ref, p2_last_ref,
    owner_ref, cell_ref, live_ref, traces_ref, sems,
):
    held, samples = traces_ref.shape
    slots = out_ref.shape[0]
    rows, cols, _ = p1_hbm.shape
    pairs = (
        (owner_hbm, owner_ref), (cell_hbm, cell_ref), (live_hbm, live_ref), (traces_hbm, traces_ref),
        (p1_hbm.at[rows - 1], p1_last_ref), (p2_hbm.at[:, pl.ds(cols - SUBLANES, SUBLANES)], p2_last_ref),
    )
    copies = [pltpu.make_async_copy(src, dst, sems.at[k]) for k, (src, dst) in enumerate(pairs)]
    for copy in copies:
        copy.start()
    for copy in copies[:3]:
        copy.wait()
    owner = owner_ref[...].astype(jnp.float32)
    row, col = iota((held, held), 0), iota((held, held), 1)
    owner_down = jnp.sum(jnp.where(row == col, owner, 0.0), axis=1, keepdims=True)
    earlier_same = (owner_down == owner) & (row < col)
    rank = jnp.sum(jnp.where(earlier_same, 1.0, 0.0), axis=0, keepdims=True)
    slot = jnp.where(live_ref[...] > 0, owner * capacity + rank, -1.0).astype(jnp.int32)
    chosen = (iota((slots, held), 0) == slot).astype(jnp.float32).astype(jnp.bfloat16)
    cell = cell_ref[...]
    kind = iota((LANES, held), 0)
    upper = (lax.shift_right_logical(cell, 6) + 1).astype(jnp.float32)
    lower = (cell & 63).astype(jnp.float32)
    codes = jnp.where(kind == 0, upper, jnp.where(kind == 1, lower, 0.0)).astype(jnp.bfloat16)
    sent = lax.dot_general(chosen, codes, (((1,), (1,)), ((), ())), preferred_element_type=jnp.float32)
    out_ref[:, samples:] = sent.astype(jnp.bfloat16)
    copies[3].wait()
    rows = jnp.dot(chosen, traces_ref[...], preferred_element_type=jnp.float32)
    out_ref[:, :samples] = rows.astype(jnp.bfloat16)
    for copy in copies[4:]:
        copy.wait()


def bin_kernel(got_ref, p1_ref, p2_ref, b_ref, diag_ref, *edge_refs):
    rows, tiles, cols, _ = b_ref.shape
    samples = tiles * LANES
    slots = got_ref.shape[0]
    kind = iota((SUBLANES, LANES), 1)
    weight = jnp.where(kind == 0, 64.0, jnp.where(kind == 1, 1.0, 0.0)).astype(jnp.bfloat16)
    value = lax.dot_general(
        weight, got_ref[:, samples:], (((1,), (1,)), ((), ())), preferred_element_type=jnp.float32
    )
    bin_of = value[:1].astype(jnp.int32) - 64
    not_first_row = (lax.axis_index("inl") > 0).astype(jnp.float32)
    not_first_col = (lax.axis_index("xl") > 0).astype(jnp.float32)
    ones = jnp.ones((slots, LANES), jnp.bfloat16)
    first_col = jnp.where(iota((cols, LANES), 0) == 0, not_first_col, 0.0) - SHIFT
    got = got_ref[:, :samples]
    for i in range(rows):
        place = (iota((cols, slots), 0) + i * cols == bin_of).astype(jnp.float32).astype(jnp.bfloat16)
        total = jnp.dot(place, got, preferred_element_type=jnp.float32)
        for c in range(tiles):
            b_ref[i, c] = total[:, c * LANES : (c + 1) * LANES]
        hits = jnp.dot(place, ones, preferred_element_type=jnp.float32)
        diag = 2.0 * hits + first_col
        diag_ref[i] = diag + not_first_row if i == 0 else diag
    write_edges(
        b_ref, lambda at: load(p1_ref, at), lambda i: load(p2_ref, i, slice(None)), *edge_refs
    )


def write_edges(v_ref, p1_last_row, p2_last_cols, row0_ref, row7_ref, col0_ref, col7_ref):
    rows, _, cols, _ = v_ref.shape
    for x in range(0, cols, SUBLANES):
        at = slice(x, x + SUBLANES)
        store(row0_ref, load_field(v_ref, 0, at), at)
        v = load_field(v_ref, rows - 1, at)
        store(row7_ref, add(v, dip_part(p1_last_row(at), *stencil(v))), at)
    for i in range(rows):
        store(col0_ref, load_field(v_ref, i, slice(0, 1)), slice(i, i + 1))
        v = load_field(v_ref, i, slice(cols - SUBLANES, cols))
        moved = add(v, dip_part(p2_last_cols(i), *stencil(v)))
        store(col7_ref, [t[SUBLANES - 1 :] for t in moved], slice(i, i + 1))


def apply_kernel(v_ref, p1_ref, p2_ref, diag_ref, out_ref, sums_ref, second_ref):
    rows, tiles, cols, _ = v_ref.shape
    sub_index = iota((SUBLANES, LANES), 0)
    zero = [jnp.zeros((SUBLANES, LANES), jnp.float32)] * tiles
    for i in range(rows):
        for c in range(tiles):
            second_ref[i, c, :SUBLANES, :] = zero[0]

    def filters(i, x, v, shifted_v, above, below):
        at = slice(x, x + SUBLANES)
        v_row, second_row = v_ref.at[i], second_ref.at[i]
        odd, even = shifted_v
        p1, p2 = load(p1_ref.at[i], at), load(p2_ref.at[i], at)
        if x + SUBLANES < cols:
            right = load_tiles(v_row, slice(x + 1, x + 1 + SUBLANES))
        else:
            right = [jnp.where(sub_index == SUBLANES - 1, 0.0, pltpu.roll(t, SUBLANES - 1, 0)) for t in v]
        first = sub(sub(below, v), dip_part(p1, odd, even))
        second = sub(sub(right, v), dip_part(p2, odd, even))
        for c in range(tiles):
            second_row[c, x + SUBLANES : x + 2 * SUBLANES, :] = second[c]
        left = [second_row[c, x + SUBLANES - 1 : x + 2 * SUBLANES - 1, :] for c in range(tiles)]
        a1, b1 = adjoint_terms(p1, first)
        a2, b2 = adjoint_terms(p2, second)
        a, b = add(a1, a2), add(b1, b2)
        diag = diag_ref.at[i][at, :]
        rest = [
            (diag * c + (f + s)) - ((f1 + s1) - (y + y))
            for c, f, s, f1, s1, y in zip(v, above, left, first, second, b)
        ]
        return first, (rest, add(a, b), sub(b, a))

    def adjoint(i, x, pending):
        at = slice(x, x + SUBLANES)
        rest, up, down = pending
        out = [r - (u + d) for r, u, d in zip(rest, later(up), earlier(down))]
        out_row = out_ref.at[i]
        for c in range(tiles):
            out_row[c, at, :] = out[c]
        return dot(load_tiles(v_ref.at[i], at), out)

    vout, vv = zero[0], zero[0]
    for x in range(0, cols, SUBLANES):
        at = slice(x, x + SUBLANES)
        v = load_tiles(v_ref.at[0], at)
        below = load_tiles(v_ref.at[1], at)
        below_shifted = stencil(below)
        first, pending = filters(0, x, v, stencil(v), zero, below)

        def body(i, carry):
            v, shifted_v, first, pending, own, norm = carry
            below = load_tiles(v_ref.at[i + 1], at)
            below_shifted = stencil(below)
            first, fresh = filters(i, x, v, shifted_v, first, below)
            own = own + adjoint(i - 1, x, pending)
            return below, below_shifted, first, fresh, own, norm + dot(v, v)

        carry = (below, below_shifted, first, pending, zero[0], dot(v, v))
        v, shifted_v, first, pending, own, norm = lax.fori_loop(1, rows - 1, body, carry)
        first, fresh = filters(rows - 1, x, v, shifted_v, first, zero)
        own = own + adjoint(rows - 2, x, pending) + adjoint(rows - 1, x, fresh)
        vout, vv = vout + own, vv + (norm + dot(v, v))
    sums_ref[0], sums_ref[1] = vout, vv


def halo_corrections(out_ref, p1_ref, p2_ref, below_ref, above_ref, right_ref, left_ref):
    rows, _, cols, _ = out_ref.shape
    last = rows - 1
    sub_index = iota((SUBLANES, LANES), 0)
    for x in range(0, cols, SUBLANES):
        at = slice(x, x + SUBLANES)
        store_field(out_ref, sub(load_field(out_ref, 0, at), load(above_ref, at)), 0, at)
        r = load(below_ref, at)
        moved = adjoint_finish(r, *adjoint_terms(load(p1_ref, last, at), r))
        store_field(out_ref, sub(load_field(out_ref, last, at), moved), last, at)
    for i in range(rows):
        at = slice(0, SUBLANES)
        r = [jnp.where(sub_index == 0, t, 0.0) for t in load(left_ref, slice(i, i + 1))]
        store_field(out_ref, sub(load_field(out_ref, i, at), r), i, at)
        at = slice(cols - SUBLANES, cols)
        r = [jnp.where(sub_index == SUBLANES - 1, t, 0.0) for t in load(right_ref, slice(i, i + 1))]
        moved = adjoint_finish(r, *adjoint_terms(load(p2_ref, i, at), r))
        store_field(out_ref, sub(load_field(out_ref, i, at), moved), i, at)


def settle(image_ref, p1_ref, p2_ref, below_ref, above_ref, right_ref, left_ref, row7_ref, col7_ref, out_ref):
    across = jnp.zeros((SUBLANES, LANES), jnp.float32)
    for mine, theirs in ((row7_ref, below_ref), (col7_ref, right_ref)):
        for x in range(0, mine.shape[0], SUBLANES):
            at = slice(x, x + SUBLANES)
            across = across + dot(load(mine, at), load(theirs, at))
    halo_corrections(out_ref, p1_ref, p2_ref, below_ref, above_ref, right_ref, left_ref)
    return across


def correct_kernel(
    image_ref, p1_ref, p2_ref, below_ref, above_ref, right_ref, left_ref, row7_ref, col7_ref,
    out_ref, across_ref, *edge_refs,
):
    across_ref[...] = settle(
        image_ref, p1_ref, p2_ref, below_ref, above_ref, right_ref, left_ref, row7_ref, col7_ref, out_ref
    )
    rows, _, cols, _ = out_ref.shape
    write_edges(
        out_ref,
        lambda at: load(p1_ref, rows - 1, at),
        lambda i: load(p2_ref, i, slice(cols - SUBLANES, cols)),
        *edge_refs,
    )


def moments_kernel(
    image_ref, p1_ref, p2_ref, below_ref, above_ref, right_ref, left_ref, row7_ref, col7_ref, *refs
):
    sums_refs, across_refs = refs[:ITERS], refs[ITERS : 2 * ITERS - 1]
    out_ref, message_ref = refs[2 * ITERS - 1 :]
    final = settle(
        image_ref, p1_ref, p2_ref, below_ref, above_ref, right_ref, left_ref, row7_ref, col7_ref, out_ref
    )
    m = []
    for sums_ref, across in zip(sums_refs, [ref[...] for ref in across_refs] + [final]):
        m.append(sums_ref[1])
        m.append(sums_ref[0] - 2.0 * across)
    sub_index, lane = iota((SUBLANES, LANES), 0), iota((SUBLANES, LANES), 1)
    block = jnp.zeros((SUBLANES, LANES), jnp.float32)
    for k, part in enumerate(m):
        block = jnp.where(sub_index == k, jnp.sum(part, axis=0, keepdims=True), block)
    total = jnp.sum(block, axis=1, keepdims=True)
    line = jnp.sum(jnp.where(sub_index == lane, total, 0.0), axis=0, keepdims=True)
    message_ref[...] = jnp.broadcast_to(line[None], message_ref.shape)


def coefficients(m):
    zero = jnp.zeros_like(m[0])
    model = [zero] * ITERS
    residual = [zero + 1.0] + [zero] * ITERS
    direction = [zero + 1.0] + [zero] * (ITERS - 1)
    norm_now = m[0]

    def inner(x, y, count):
        total = zero
        for i in range(count):
            for j in range(len(y)):
                if i + j < len(m):
                    total = total + x[i] * y[j] * m[i + j]
        return total

    for sweep in range(ITERS):
        image = [SHIFT * d for d in direction] + [zero]
        image = [image[0]] + [s + d for s, d in zip(image[1:], direction)]
        alpha = norm_now / inner(direction, image[: sweep + 2], sweep + 1)
        model = [s + alpha * d for s, d in zip(model, direction)]
        residual = [r - alpha * d for r, d in zip(residual, image)]
        if sweep + 1 < ITERS:
            norm_next = inner(residual, residual[: sweep + 2], sweep + 2)
            beta = norm_next / norm_now
            direction = [r + beta * d for r, d in zip(residual, direction)]
            norm_now = norm_next
    return [2.0 * s for s in model] + residual


def finish_kernel(parts_ref, b_ref, v1_ref, v2_ref, v3_ref, model_hbm, residual_hbm, model_ref, residual_ref, sems):
    rows, _, cols, _ = b_ref.shape
    line = jnp.sum(parts_ref[...], axis=0)
    sub_index, lane = iota((SUBLANES, LANES), 0), iota((SUBLANES, LANES), 1)
    total = jnp.sum(jnp.where(sub_index == lane, line, 0.0), axis=1, keepdims=True)
    total = jnp.broadcast_to(total, (SUBLANES, LANES))
    m = [jnp.broadcast_to(total[k : k + 1], (SUBLANES, LANES)) for k in range(2 * ITERS)]
    weights = coefficients(m)
    model, residual = weights[:ITERS], weights[ITERS:]

    def copies(i):
        return (
            pltpu.make_async_copy(model_ref.at[i], model_hbm.at[i], sems.at[0, i]),
            pltpu.make_async_copy(residual_ref.at[i], residual_hbm.at[i], sems.at[1, i]),
        )

    def body(i, carry):
        for x in range(0, cols, SUBLANES):
            at = slice(x, x + SUBLANES)
            b, v1, v2, v3 = (load_field(ref, i, at) for ref in (b_ref, v1_ref, v2_ref, v3_ref))
            store(model_ref, [model[0] * s + model[1] * t + model[2] * u for s, t, u in zip(b, v1, v2)], i, at)
            store(
                residual_ref,
                [(residual[0] * s + residual[1] * t) + (residual[2] * u + residual[3] * w) for s, t, u, w in zip(b, v1, v2, v3)],
                i, at,
            )
        for copy in copies(i):
            copy.start()
        return carry

    lax.fori_loop(0, rows, body, 0)
    for i in range(rows):
        for copy in copies(i):
            copy.wait()


def f32(*shape):
    return pltpu.VMEM(shape, jnp.float32)


def call(kernel, outs, *args, name, scratch=(), aliases=None, cost=None, ins=None, places=None):
    return pl.pallas_call(
        kernel,
        out_shape=outs,
        in_specs=ins or [IN_VMEM] * len(args),
        out_specs=places or [IN_VMEM] * len(outs),
        scratch_shapes=list(scratch),
        input_output_aliases=aliases or {},
        compiler_params=PARAMS,
        cost_estimate=cost,
        name=name,
    )(*args)


def in_hbm(array):
    return pltpu.with_memory_space_constraint(array, pltpu.HBM)


def per_device(traces, trace_owner, trace_cell, acquired, inline_dip, cross_dip):
    rows, cols, samples = inline_dip.shape
    devices = lax.axis_size("inl") * lax.axis_size("xl")
    held = traces.shape[0]
    capacity = max(2, 2 * held // devices)
    slots = devices * capacity
    small = pltpu.VMEM((1, held), jnp.int32)
    inputs = (trace_owner.reshape(1, held), trace_cell[None], acquired[None], traces, inline_dip, cross_dip)
    sent, p1_last, p2_last = call(
        functools.partial(pack_kernel, capacity),
        [
            jax.ShapeDtypeStruct((slots, samples + LANES), jnp.bfloat16),
            f32(cols, samples),
            f32(rows, SUBLANES, samples),
        ],
        *(in_hbm(x) for x in inputs),
        name="pack", ins=[IN_HBM] * len(inputs),
        scratch=[small, small, small, pltpu.VMEM((held, samples), jnp.bfloat16), pltpu.SemaphoreType.DMA((6,))],
    )
    got = lax.all_to_all(sent, ("inl", "xl"), split_axis=0, concat_axis=0, tiled=True)
    edge_shapes = [f32(cols, samples), f32(cols, samples), f32(rows, samples), f32(rows, samples)]
    tile = f32(rows, samples // LANES, cols, LANES)
    b, diag, *edges = call(
        bin_kernel, [tile, f32(rows, cols, LANES)] + edge_shapes, got, p1_last, p2_last, name="bin"
    )
    fields, sums, products = [b], [], []
    cost = pl.CostEstimate(
        flops=60 * rows * cols * samples, bytes_accessed=16 * rows * cols * samples, transcendentals=0
    )
    for step in range(ITERS):
        row0, row7, col0, col7 = edges
        below = shifted(row0, "inl", -1)
        above = shifted(row7, "inl", 1)
        right = shifted(col0, "xl", -1)
        left = shifted(col7, "xl", 1)
        image, partial = call(
            apply_kernel,
            [tile, f32(2, SUBLANES, LANES)],
            fields[-1], inline_dip, cross_dip, diag,
            name="apply",
            scratch=[pltpu.VMEM((rows, samples // LANES, SUBLANES + cols, LANES), jnp.float32)],
            cost=cost,
        )
        sums.append(partial)
        args = [image, inline_dip, cross_dip, below, above, right, left, row7, col7]
        if step + 1 < ITERS:
            image, across, *edges = call(
                correct_kernel, [tile, f32(SUBLANES, LANES)] + edge_shapes, *args, name="correct", aliases={0: 0}
            )
            products.append(across)
        else:
            image, message = call(
                moments_kernel, [tile, f32(devices, 1, LANES)], *args, *sums, *products,
                name="moments", aliases={0: 0},
            )
        fields.append(image)
    parts = lax.all_to_all(message, ("inl", "xl"), split_axis=0, concat_axis=0, tiled=True)
    out = jax.ShapeDtypeStruct((rows, cols, samples), jnp.float32)
    return tuple(
        call(
            finish_kernel, [out, out], parts, *fields,
            name="finish", places=[pl.BlockSpec(memory_space=pl.ANY)] * 2,
            scratch=[
                pltpu.VMEM((rows, cols, samples), jnp.float32),
                pltpu.VMEM((rows, cols, samples), jnp.float32),
                pltpu.SemaphoreType.DMA((2, rows)),
            ],
        )
    )


def solution(mesh):
    placed = (
        P(("inl", "xl"), None),
        P(("inl", "xl"), None),
        P(("inl", "xl")),
        P(("inl", "xl")),
        P("inl", "xl", None),
        P("inl", "xl", None),
    )
    return jax.shard_map(
        per_device,
        mesh=mesh,
        in_specs=placed,
        out_specs=(P("inl", "xl", None), P("inl", "xl", None)),
        check_vma=False,
    )
```

```python
import functools

import jax
import jax.numpy as jnp
from jax import lax
from jax.experimental import pallas as pl
from jax.experimental.pallas import tpu as pltpu
from jax.sharding import PartitionSpec as P

ITERS = 3
LANES = 128
SUBLANES = 8
GROUP = 16

SHIFT = 6.0
IN_VMEM = pl.BlockSpec(memory_space=pltpu.VMEM)
IN_HBM = pl.BlockSpec(memory_space=pltpu.HBM)
PARAMS = pltpu.CompilerParams(vmem_limit_bytes=16 << 20)


def shifted(value, axis, steps):
    count = lax.axis_size(axis)
    initial, last = (max(0, -steps), min(count, count - steps))
    return lax.ppermute(value, axis, [(source, source + steps) for source in range(initial, last)])


def iota(shape, dim):
    return lax.broadcasted_iota(jnp.int32, shape, dim)


def earlier(tiles):
    lane = iota(tiles[0].shape, 1)
    rolled = [pltpu.roll(tile, 1, 1) for tile in tiles]
    before = [jnp.zeros_like(tiles[0])] + rolled[:-1]
    return [jnp.where(lane == 0, edge, inner) for edge, inner in zip(before, rolled)]


def later(tiles):
    lane = iota(tiles[0].shape, 1)
    rolled = [pltpu.roll(tile, LANES - 1, 1) for tile in tiles]
    after = rolled[1:] + [jnp.zeros_like(tiles[0])]
    return [jnp.where(lane == LANES - 1, edge, inner) for edge, inner in zip(after, rolled)]


def stencil(v):
    em, ep = earlier(v), later(v)
    odd = [m - p for m, p in zip(em, ep)]
    even = [(m + p) - (c + c) for m, p, c in zip(em, ep, v)]
    return odd, even


def dip_part(p, odd, even):
    return [(0.5 * d) * (o + d * e) for d, o, e in zip(p, odd, even)]


def adjoint_terms(p, r):
    a = [(0.5 * d) * x for d, x in zip(p, r)]
    b = [d * x for d, x in zip(p, a)]
    return a, b


def adjoint_finish(r, a, b):
    up = later([x + y for x, y in zip(a, b)])
    down = earlier([y - x for x, y in zip(a, b)])
    return [(x + u) + (d - (y + y)) for x, u, d, y in zip(r, up, down, b)]


def load(ref, *index):
    count = ref.shape[-1] // LANES
    return [ref[(*index, slice(c * LANES, (c + 1) * LANES))] for c in range(count)]


def store(ref, tiles, *index):
    for c, tile in enumerate(tiles):
        ref[(*index, slice(c * LANES, (c + 1) * LANES))] = tile


def load_tiles(ref, at):
    return [ref[c, at, :] for c in range(ref.shape[0])]


def load_field(ref, i, at):
    return [ref[i, c, at, :] for c in range(ref.shape[1])]


def store_field(ref, tiles, i, at):
    for c, tile in enumerate(tiles):
        ref[i, c, at, :] = tile


def add(x, y):
    return [a + b for a, b in zip(x, y)]


def sub(x, y):
    return [a - b for a, b in zip(x, y)]


def dot(x, y):
    return functools.reduce(lambda s, t: s + t, [a * b for a, b in zip(x, y)])


def pack_kernel(
    capacity, owner_hbm, cell_hbm, live_hbm, traces_hbm, p1_hbm, p2_hbm, out_ref, p1_last_ref, p2_last_ref,
    owner_ref, cell_ref, live_ref, traces_ref, sems,
):
    held, samples = traces_ref.shape
    slots = out_ref.shape[0]
    rows, cols, _ = p1_hbm.shape
    pairs = (
        (owner_hbm, owner_ref), (cell_hbm, cell_ref), (live_hbm, live_ref), (traces_hbm, traces_ref),
        (p1_hbm.at[rows - 1], p1_last_ref), (p2_hbm.at[:, pl.ds(cols - SUBLANES, SUBLANES)], p2_last_ref),
    )
    copies = [pltpu.make_async_copy(src, dst, sems.at[k]) for k, (src, dst) in enumerate(pairs)]
    for copy in copies:
        copy.start()
    for copy in copies[:3]:
        copy.wait()
    owner = owner_ref[...].astype(jnp.float32)
    row, col = iota((held, held), 0), iota((held, held), 1)
    owner_down = jnp.sum(jnp.where(row == col, owner, 0.0), axis=1, keepdims=True)
    earlier_same = (owner_down == owner) & (row < col)
    rank = jnp.sum(jnp.where(earlier_same, 1.0, 0.0), axis=0, keepdims=True)
    slot = jnp.where(live_ref[...] > 0, owner * capacity + rank, -1.0).astype(jnp.int32)
    chosen = (iota((slots, held), 0) == slot).astype(jnp.float32).astype(jnp.bfloat16)
    cell = cell_ref[...]
    kind = iota((LANES, held), 0)
    upper = (lax.shift_right_logical(cell, 6) + 1).astype(jnp.float32)
    lower = (cell & 63).astype(jnp.float32)
    codes = jnp.where(kind == 0, upper, jnp.where(kind == 1, lower, 0.0)).astype(jnp.bfloat16)
    sent = lax.dot_general(chosen, codes, (((1,), (1,)), ((), ())), preferred_element_type=jnp.float32)
    out_ref[:, samples:] = sent.astype(jnp.bfloat16)
    copies[3].wait()
    rows = jnp.dot(chosen, traces_ref[...], preferred_element_type=jnp.float32)
    out_ref[:, :samples] = rows.astype(jnp.bfloat16)
    for copy in copies[4:]:
        copy.wait()


def bin_kernel(got_ref, p1_ref, p2_ref, b_ref, diag_ref, *edge_refs):
    rows, tiles, cols, _ = b_ref.shape
    samples = tiles * LANES
    slots = got_ref.shape[0]
    kind = iota((SUBLANES, LANES), 1)
    weight = jnp.where(kind == 0, 64.0, jnp.where(kind == 1, 1.0, 0.0)).astype(jnp.bfloat16)
    value = lax.dot_general(
        weight, got_ref[:, samples:], (((1,), (1,)), ((), ())), preferred_element_type=jnp.float32
    )
    bin_of = value[:1].astype(jnp.int32) - 64
    not_first_row = (lax.axis_index("inl") > 0).astype(jnp.float32)
    not_first_col = (lax.axis_index("xl") > 0).astype(jnp.float32)
    ones = jnp.ones((slots, LANES), jnp.bfloat16)
    first_col = jnp.where(iota((cols, LANES), 0) == 0, not_first_col, 0.0) - SHIFT
    got = got_ref[:, :samples]
    for i in range(rows):
        place = (iota((cols, slots), 0) + i * cols == bin_of).astype(jnp.float32).astype(jnp.bfloat16)
        total = jnp.dot(place, got, preferred_element_type=jnp.float32)
        for c in range(tiles):
            b_ref[i, c] = total[:, c * LANES : (c + 1) * LANES]
        hits = jnp.dot(place, ones, preferred_element_type=jnp.float32)
        diag = 2.0 * hits + first_col
        diag_ref[i] = diag + not_first_row if i == 0 else diag
    write_edges(
        b_ref, lambda at: load(p1_ref, at), lambda i: load(p2_ref, i, slice(None)), *edge_refs
    )


def write_edges(v_ref, p1_last_row, p2_last_cols, row0_ref, row7_ref, col0_ref, col7_ref):
    rows, _, cols, _ = v_ref.shape
    for x in range(0, cols, SUBLANES):
        at = slice(x, x + SUBLANES)
        store(row0_ref, load_field(v_ref, 0, at), at)
        v = load_field(v_ref, rows - 1, at)
        store(row7_ref, add(v, dip_part(p1_last_row(at), *stencil(v))), at)
    for i in range(rows):
        store(col0_ref, load_field(v_ref, i, slice(0, 1)), slice(i, i + 1))
        v = load_field(v_ref, i, slice(cols - SUBLANES, cols))
        moved = add(v, dip_part(p2_last_cols(i), *stencil(v)))
        store(col7_ref, [t[SUBLANES - 1 :] for t in moved], slice(i, i + 1))


def apply_kernel(v_ref, p1_ref, p2_ref, diag_ref, out_ref, sums_ref, second_ref):
    rows, tiles, cols, _ = v_ref.shape
    sub_index = iota((SUBLANES, LANES), 0)
    zero = [jnp.zeros((SUBLANES, LANES), jnp.float32)] * tiles
    for i in range(rows):
        for c in range(tiles):
            second_ref[i, c, :SUBLANES, :] = zero[0]

    def filters(i, x, v, shifted_v, above, below):
        at = slice(x, x + SUBLANES)
        v_row, second_row = v_ref.at[i], second_ref.at[i]
        odd, even = shifted_v
        p1, p2 = load(p1_ref.at[i], at), load(p2_ref.at[i], at)
        if x + SUBLANES < cols:
            right = load_tiles(v_row, slice(x + 1, x + 1 + SUBLANES))
        else:
            right = [jnp.where(sub_index == SUBLANES - 1, 0.0, pltpu.roll(t, SUBLANES - 1, 0)) for t in v]
        first = sub(sub(below, v), dip_part(p1, odd, even))
        second = sub(sub(right, v), dip_part(p2, odd, even))
        for c in range(tiles):
            second_row[c, x + SUBLANES : x + 2 * SUBLANES, :] = second[c]
        left = [second_row[c, x + SUBLANES - 1 : x + 2 * SUBLANES - 1, :] for c in range(tiles)]
        a1, b1 = adjoint_terms(p1, first)
        a2, b2 = adjoint_terms(p2, second)
        a, b = add(a1, a2), add(b1, b2)
        diag = diag_ref.at[i][at, :]
        rest = [
            (diag * c + (f + s)) - ((f1 + s1) - (y + y))
            for c, f, s, f1, s1, y in zip(v, above, left, first, second, b)
        ]
        return first, (rest, add(a, b), sub(b, a))

    def adjoint(i, x, pending):
        at = slice(x, x + SUBLANES)
        rest, up, down = pending
        out = [r - (u + d) for r, u, d in zip(rest, later(up), earlier(down))]
        out_row = out_ref.at[i]
        for c in range(tiles):
            out_row[c, at, :] = out[c]
        return dot(load_tiles(v_ref.at[i], at), out)

    vout, vv = zero[0], zero[0]
    for x in range(0, cols, GROUP):
        chunks = range(x, x + GROUP, SUBLANES)

        def fetch(i):
            below = [load_tiles(v_ref.at[i], slice(k, k + SUBLANES)) for k in chunks]
            return below, [stencil(tiles_of) for tiles_of in below]

        def all_filters(i, v, shifted_v, first, below):
            done = [filters(i, k, *rest) for k, *rest in zip(chunks, v, shifted_v, first, below)]
            return [pair[0] for pair in done], [pair[1] for pair in done]

        def all_adjoint(i, own, pending):
            for k, waiting in zip(chunks, pending):
                own = own + adjoint(i, k, waiting)
            return own

        def norms(norm, v):
            for tiles_of in v:
                norm = norm + dot(tiles_of, tiles_of)
            return norm

        nothing = [zero] * len(chunks)
        v, shifted_v = fetch(0)
        below, below_shifted = fetch(1)
        first, pending = all_filters(0, v, shifted_v, nothing, below)

        def body(i, carry):
            v, shifted_v, first, pending, own, norm = carry
            below, below_shifted = fetch(i + 1)
            first, fresh = all_filters(i, v, shifted_v, first, below)
            own = all_adjoint(i - 1, own, pending)
            return below, below_shifted, first, fresh, own, norms(norm, v)

        carry = (below, below_shifted, first, pending, zero[0], norms(zero[0], v))
        v, shifted_v, first, pending, own, norm = lax.fori_loop(1, rows - 1, body, carry)
        first, fresh = all_filters(rows - 1, v, shifted_v, first, nothing)
        own = all_adjoint(rows - 1, all_adjoint(rows - 2, own, pending), fresh)
        vout, vv = vout + own, vv + norms(norm, v)
    sums_ref[0], sums_ref[1] = vout, vv


def halo_corrections(out_ref, p1_ref, p2_ref, below_ref, above_ref, right_ref, left_ref):
    rows, _, cols, _ = out_ref.shape
    last = rows - 1
    sub_index = iota((SUBLANES, LANES), 0)
    for x in range(0, cols, SUBLANES):
        at = slice(x, x + SUBLANES)
        store_field(out_ref, sub(load_field(out_ref, 0, at), load(above_ref, at)), 0, at)
        r = load(below_ref, at)
        moved = adjoint_finish(r, *adjoint_terms(load(p1_ref, last, at), r))
        store_field(out_ref, sub(load_field(out_ref, last, at), moved), last, at)
    for i in range(rows):
        at = slice(0, SUBLANES)
        r = [jnp.where(sub_index == 0, t, 0.0) for t in load(left_ref, slice(i, i + 1))]
        store_field(out_ref, sub(load_field(out_ref, i, at), r), i, at)
        at = slice(cols - SUBLANES, cols)
        r = [jnp.where(sub_index == SUBLANES - 1, t, 0.0) for t in load(right_ref, slice(i, i + 1))]
        moved = adjoint_finish(r, *adjoint_terms(load(p2_ref, i, at), r))
        store_field(out_ref, sub(load_field(out_ref, i, at), moved), i, at)


def settle(image_ref, p1_ref, p2_ref, below_ref, above_ref, right_ref, left_ref, row7_ref, col7_ref, out_ref):
    across = jnp.zeros((SUBLANES, LANES), jnp.float32)
    for mine, theirs in ((row7_ref, below_ref), (col7_ref, right_ref)):
        for x in range(0, mine.shape[0], SUBLANES):
            at = slice(x, x + SUBLANES)
            across = across + dot(load(mine, at), load(theirs, at))
    halo_corrections(out_ref, p1_ref, p2_ref, below_ref, above_ref, right_ref, left_ref)
    return across


def correct_kernel(
    image_ref, p1_ref, p2_ref, below_ref, above_ref, right_ref, left_ref, row7_ref, col7_ref,
    out_ref, across_ref, *edge_refs,
):
    across_ref[...] = settle(
        image_ref, p1_ref, p2_ref, below_ref, above_ref, right_ref, left_ref, row7_ref, col7_ref, out_ref
    )
    rows, _, cols, _ = out_ref.shape
    write_edges(
        out_ref,
        lambda at: load(p1_ref, rows - 1, at),
        lambda i: load(p2_ref, i, slice(cols - SUBLANES, cols)),
        *edge_refs,
    )


def moments_kernel(
    image_ref, p1_ref, p2_ref, below_ref, above_ref, right_ref, left_ref, row7_ref, col7_ref, *refs
):
    sums_refs, across_refs = refs[:ITERS], refs[ITERS : 2 * ITERS - 1]
    out_ref, message_ref = refs[2 * ITERS - 1 :]
    final = settle(
        image_ref, p1_ref, p2_ref, below_ref, above_ref, right_ref, left_ref, row7_ref, col7_ref, out_ref
    )
    m = []
    for sums_ref, across in zip(sums_refs, [ref[...] for ref in across_refs] + [final]):
        m.append(sums_ref[1])
        m.append(sums_ref[0] - 2.0 * across)
    sub_index, lane = iota((SUBLANES, LANES), 0), iota((SUBLANES, LANES), 1)
    block = jnp.zeros((SUBLANES, LANES), jnp.float32)
    for k, part in enumerate(m):
        block = jnp.where(sub_index == k, jnp.sum(part, axis=0, keepdims=True), block)
    total = jnp.sum(block, axis=1, keepdims=True)
    line = jnp.sum(jnp.where(sub_index == lane, total, 0.0), axis=0, keepdims=True)
    message_ref[...] = jnp.broadcast_to(line[None], message_ref.shape)


def coefficients(m):
    zero = jnp.zeros_like(m[0])
    model = [zero] * ITERS
    residual = [zero + 1.0] + [zero] * ITERS
    direction = [zero + 1.0] + [zero] * (ITERS - 1)
    norm_now = m[0]

    def inner(x, y, count):
        total = zero
        for i in range(count):
            for j in range(len(y)):
                if i + j < len(m):
                    total = total + x[i] * y[j] * m[i + j]
        return total

    for sweep in range(ITERS):
        image = [SHIFT * d for d in direction] + [zero]
        image = [image[0]] + [s + d for s, d in zip(image[1:], direction)]
        alpha = norm_now / inner(direction, image[: sweep + 2], sweep + 1)
        model = [s + alpha * d for s, d in zip(model, direction)]
        residual = [r - alpha * d for r, d in zip(residual, image)]
        if sweep + 1 < ITERS:
            norm_next = inner(residual, residual[: sweep + 2], sweep + 2)
            beta = norm_next / norm_now
            direction = [r + beta * d for r, d in zip(residual, direction)]
            norm_now = norm_next
    return [2.0 * s for s in model] + residual


def finish_kernel(parts_ref, b_ref, v1_ref, v2_ref, v3_ref, model_hbm, residual_hbm, model_ref, residual_ref, sems):
    rows, _, cols, _ = b_ref.shape
    line = jnp.sum(parts_ref[...], axis=0)
    sub_index, lane = iota((SUBLANES, LANES), 0), iota((SUBLANES, LANES), 1)
    total = jnp.sum(jnp.where(sub_index == lane, line, 0.0), axis=1, keepdims=True)
    total = jnp.broadcast_to(total, (SUBLANES, LANES))
    m = [jnp.broadcast_to(total[k : k + 1], (SUBLANES, LANES)) for k in range(2 * ITERS)]
    weights = coefficients(m)
    model, residual = weights[:ITERS], weights[ITERS:]

    def copies(i):
        return (
            pltpu.make_async_copy(model_ref.at[i], model_hbm.at[i], sems.at[0, i]),
            pltpu.make_async_copy(residual_ref.at[i], residual_hbm.at[i], sems.at[1, i]),
        )

    def body(i, carry):
        for x in range(0, cols, SUBLANES):
            at = slice(x, x + SUBLANES)
            b, v1, v2, v3 = (load_field(ref, i, at) for ref in (b_ref, v1_ref, v2_ref, v3_ref))
            store(model_ref, [model[0] * s + model[1] * t + model[2] * u for s, t, u in zip(b, v1, v2)], i, at)
            store(
                residual_ref,
                [(residual[0] * s + residual[1] * t) + (residual[2] * u + residual[3] * w) for s, t, u, w in zip(b, v1, v2, v3)],
                i, at,
            )
        for copy in copies(i):
            copy.start()
        return carry

    lax.fori_loop(0, rows, body, 0)
    for i in range(rows):
        for copy in copies(i):
            copy.wait()


def f32(*shape):
    return pltpu.VMEM(shape, jnp.float32)


def call(kernel, outs, *args, name, scratch=(), aliases=None, cost=None, ins=None, places=None):
    return pl.pallas_call(
        kernel,
        out_shape=outs,
        in_specs=ins or [IN_VMEM] * len(args),
        out_specs=places or [IN_VMEM] * len(outs),
        scratch_shapes=list(scratch),
        input_output_aliases=aliases or {},
        compiler_params=PARAMS,
        cost_estimate=cost,
        name=name,
    )(*args)


def in_hbm(array):
    return pltpu.with_memory_space_constraint(array, pltpu.HBM)


def per_device(traces, trace_owner, trace_cell, acquired, inline_dip, cross_dip):
    rows, cols, samples = inline_dip.shape
    devices = lax.axis_size("inl") * lax.axis_size("xl")
    held = traces.shape[0]
    capacity = max(2, 2 * held // devices)
    slots = devices * capacity
    small = pltpu.VMEM((1, held), jnp.int32)
    inputs = (trace_owner.reshape(1, held), trace_cell[None], acquired[None], traces, inline_dip, cross_dip)
    sent, p1_last, p2_last = call(
        functools.partial(pack_kernel, capacity),
        [
            jax.ShapeDtypeStruct((slots, samples + LANES), jnp.bfloat16),
            f32(cols, samples),
            f32(rows, SUBLANES, samples),
        ],
        *(in_hbm(x) for x in inputs),
        name="pack", ins=[IN_HBM] * len(inputs),
        scratch=[small, small, small, pltpu.VMEM((held, samples), jnp.bfloat16), pltpu.SemaphoreType.DMA((6,))],
    )
    got = lax.all_to_all(sent, ("inl", "xl"), split_axis=0, concat_axis=0, tiled=True)
    edge_shapes = [f32(cols, samples), f32(cols, samples), f32(rows, samples), f32(rows, samples)]
    tile = f32(rows, samples // LANES, cols, LANES)
    b, diag, *edges = call(
        bin_kernel, [tile, f32(rows, cols, LANES)] + edge_shapes, got, p1_last, p2_last, name="bin"
    )
    fields, sums, products = [b], [], []
    cost = pl.CostEstimate(
        flops=60 * rows * cols * samples, bytes_accessed=16 * rows * cols * samples, transcendentals=0
    )
    for step in range(ITERS):
        row0, row7, col0, col7 = edges
        below = shifted(row0, "inl", -1)
        above = shifted(row7, "inl", 1)
        right = shifted(col0, "xl", -1)
        left = shifted(col7, "xl", 1)
        image, partial = call(
            apply_kernel,
            [tile, f32(2, SUBLANES, LANES)],
            fields[-1], inline_dip, cross_dip, diag,
            name="apply",
            scratch=[pltpu.VMEM((rows, samples // LANES, SUBLANES + cols, LANES), jnp.float32)],
            cost=cost,
        )
        sums.append(partial)
        args = [image, inline_dip, cross_dip, below, above, right, left, row7, col7]
        if step + 1 < ITERS:
            image, across, *edges = call(
                correct_kernel, [tile, f32(SUBLANES, LANES)] + edge_shapes, *args, name="correct", aliases={0: 0}
            )
            products.append(across)
        else:
            image, message = call(
                moments_kernel, [tile, f32(devices, 1, LANES)], *args, *sums, *products,
                name="moments", aliases={0: 0},
            )
        fields.append(image)
    parts = lax.all_to_all(message, ("inl", "xl"), split_axis=0, concat_axis=0, tiled=True)
    out = jax.ShapeDtypeStruct((rows, cols, samples), jnp.float32)
    return tuple(
        call(
            finish_kernel, [out, out], parts, *fields,
            name="finish", places=[pl.BlockSpec(memory_space=pl.ANY)] * 2,
            scratch=[
                pltpu.VMEM((rows, cols, samples), jnp.float32),
                pltpu.VMEM((rows, cols, samples), jnp.float32),
                pltpu.SemaphoreType.DMA((2, rows)),
            ],
        )
    )


def solution(mesh):
    placed = (
        P(("inl", "xl"), None),
        P(("inl", "xl"), None),
        P(("inl", "xl")),
        P(("inl", "xl")),
        P("inl", "xl", None),
        P("inl", "xl", None),
    )
    return jax.shard_map(
        per_device,
        mesh=mesh,
        in_specs=placed,
        out_specs=(P("inl", "xl", None), P("inl", "xl", None)),
        check_vma=False,
    )
```

```python
import functools

import jax
import jax.numpy as jnp
from jax import lax
from jax.experimental import pallas as pl
from jax.experimental.pallas import tpu as pltpu
from jax.sharding import PartitionSpec as P

ITERS = 3
LANES = 128
SUBLANES = 8
GROUP = 32

SHIFT = 6.0
IN_VMEM = pl.BlockSpec(memory_space=pltpu.VMEM)
IN_HBM = pl.BlockSpec(memory_space=pltpu.HBM)
PARAMS = pltpu.CompilerParams(vmem_limit_bytes=16 << 20)


def shifted(value, axis, steps):
    count = lax.axis_size(axis)
    initial, last = (max(0, -steps), min(count, count - steps))
    return lax.ppermute(value, axis, [(source, source + steps) for source in range(initial, last)])


def iota(shape, dim):
    return lax.broadcasted_iota(jnp.int32, shape, dim)


def earlier(tiles):
    lane = iota(tiles[0].shape, 1)
    rolled = [pltpu.roll(tile, 1, 1) for tile in tiles]
    before = [jnp.zeros_like(tiles[0])] + rolled[:-1]
    return [jnp.where(lane == 0, edge, inner) for edge, inner in zip(before, rolled)]


def later(tiles):
    lane = iota(tiles[0].shape, 1)
    rolled = [pltpu.roll(tile, LANES - 1, 1) for tile in tiles]
    after = rolled[1:] + [jnp.zeros_like(tiles[0])]
    return [jnp.where(lane == LANES - 1, edge, inner) for edge, inner in zip(after, rolled)]


def stencil(v):
    em, ep = earlier(v), later(v)
    odd = [m - p for m, p in zip(em, ep)]
    even = [(m + p) - (c + c) for m, p, c in zip(em, ep, v)]
    return odd, even


def dip_part(p, odd, even):
    return [(0.5 * d) * (o + d * e) for d, o, e in zip(p, odd, even)]


def adjoint_terms(p, r):
    a = [(0.5 * d) * x for d, x in zip(p, r)]
    b = [d * x for d, x in zip(p, a)]
    return a, b


def adjoint_finish(r, a, b):
    up = later([x + y for x, y in zip(a, b)])
    down = earlier([y - x for x, y in zip(a, b)])
    return [(x + u) + (d - (y + y)) for x, u, d, y in zip(r, up, down, b)]


def load(ref, *index):
    count = ref.shape[-1] // LANES
    return [ref[(*index, slice(c * LANES, (c + 1) * LANES))] for c in range(count)]


def store(ref, tiles, *index):
    for c, tile in enumerate(tiles):
        ref[(*index, slice(c * LANES, (c + 1) * LANES))] = tile


def load_tiles(ref, at):
    return [ref[c, at, :] for c in range(ref.shape[0])]


def load_field(ref, i, at):
    return [ref[i, c, at, :] for c in range(ref.shape[1])]


def store_field(ref, tiles, i, at):
    for c, tile in enumerate(tiles):
        ref[i, c, at, :] = tile


def add(x, y):
    return [a + b for a, b in zip(x, y)]


def sub(x, y):
    return [a - b for a, b in zip(x, y)]


def dot(x, y):
    return functools.reduce(lambda s, t: s + t, [a * b for a, b in zip(x, y)])


def is_compact(capacity):
    return capacity % 16 == 0 and LANES % capacity == 0


def pack_kernel(
    capacity, owner_hbm, cell_hbm, live_hbm, traces_hbm, p1_hbm, p2_hbm, out_ref, p1_last_ref, p2_last_ref,
    owner_ref, cell_ref, live_ref, traces_ref, sems,
):
    held, samples = traces_ref.shape
    slots = lax.axis_size("inl") * lax.axis_size("xl") * capacity
    rows, cols, _ = p1_hbm.shape
    pairs = (
        (owner_hbm, owner_ref), (cell_hbm, cell_ref), (live_hbm, live_ref), (traces_hbm, traces_ref),
        (p1_hbm.at[rows - 1], p1_last_ref), (p2_hbm.at[:, pl.ds(cols - SUBLANES, SUBLANES)], p2_last_ref),
    )
    copies = [pltpu.make_async_copy(src, dst, sems.at[k]) for k, (src, dst) in enumerate(pairs)]
    for copy in copies:
        copy.start()
    for copy in copies[:3]:
        copy.wait()
    owner = owner_ref[...].astype(jnp.float32)
    row, col = iota((held, held), 0), iota((held, held), 1)
    owner_down = jnp.sum(jnp.where(row == col, owner, 0.0), axis=1, keepdims=True)
    earlier_same = (owner_down == owner) & (row < col)
    rank = jnp.sum(jnp.where(earlier_same, 1.0, 0.0), axis=0, keepdims=True)
    slot = jnp.where(live_ref[...] > 0, owner * capacity + rank, -1.0).astype(jnp.int32)
    chosen = (iota((slots, held), 0) == slot).astype(jnp.float32).astype(jnp.bfloat16)
    cell = cell_ref[...]
    kind = iota((LANES, held), 0)
    upper = (lax.shift_right_logical(cell, 6) + 1).astype(jnp.float32)
    lower = (cell & 63).astype(jnp.float32)
    codes = jnp.where(kind == 0, upper, jnp.where(kind == 1, lower, 0.0)).astype(jnp.bfloat16)
    if not is_compact(capacity):
        sent = lax.dot_general(chosen, codes, (((1,), (1,)), ((), ())), preferred_element_type=jnp.float32)
        out_ref[:, samples:] = sent.astype(jnp.bfloat16)
        copies[3].wait()
        packed = jnp.dot(chosen, traces_ref[...], preferred_element_type=jnp.float32)
        out_ref[:, :samples] = packed.astype(jnp.bfloat16)
    else:
        sent = lax.dot_general(codes[:16], chosen, (((1,), (1,)), ((), ())), preferred_element_type=jnp.float32)
        per = LANES // capacity
        here = lax.rem(lax.axis_index("inl") * lax.axis_size("xl") + lax.axis_index("xl"), per)
        mine = lax.div(iota((SUBLANES, LANES), 1), capacity) == here
        moves = [lax.rem(here - j + per, per) * capacity for j in range(per)]
        copies[3].wait()
        packed = jnp.dot(chosen, traces_ref[...], preferred_element_type=jnp.float32)
        for d in range(slots // capacity):
            at = slice(d * capacity, (d + 1) * capacity)
            tile = slice(d // per * LANES, (d // per + 1) * LANES)
            code = jnp.where(mine, pltpu.roll(sent[:SUBLANES, tile], moves[d % per], 1), 0.0)
            parts = [packed[at, c : c + LANES] for c in range(0, samples, LANES)]
            out_ref[d] = jnp.concatenate(parts + [code], axis=0).astype(jnp.bfloat16)
    for copy in copies[4:]:
        copy.wait()


def unpack(capacity, samples, got_ref):
    if not is_compact(capacity):
        kind = iota((SUBLANES, LANES), 1)
        weight = jnp.where(kind == 0, 64.0, jnp.where(kind == 1, 1.0, 0.0)).astype(jnp.bfloat16)
        value = lax.dot_general(
            weight, got_ref[:, samples:], (((1,), (1,)), ((), ())), preferred_element_type=jnp.float32
        )
        return got_ref[:, :samples], value[:1].astype(jnp.int32) - 64
    sources, per = got_ref.shape[0], LANES // capacity
    blocks = [got_ref[d].astype(jnp.float32) for d in range(sources)]
    tiles = samples // LANES
    values = []
    for first in range(0, sources, per):
        code = functools.reduce(lambda s, t: s + t, [blocks[d][tiles * capacity :] for d in range(first, first + per)])
        values.append(64.0 * code[:1] + code[1:2] - 64.0)
    columns = [
        jnp.concatenate([blocks[d][c * capacity : (c + 1) * capacity] for d in range(sources)], axis=0)
        for c in range(tiles)
    ]
    got = jnp.concatenate([column.astype(jnp.bfloat16) for column in columns], axis=1)
    return got, jnp.concatenate(values, axis=1).astype(jnp.int32)


def bin_kernel(capacity, got_ref, p1_ref, p2_ref, b_ref, diag_ref, *edge_refs):
    rows, tiles, cols, _ = b_ref.shape
    got, bin_of = unpack(capacity, tiles * LANES, got_ref)
    slots = got.shape[0]
    not_first_row = (lax.axis_index("inl") > 0).astype(jnp.float32)
    not_first_col = (lax.axis_index("xl") > 0).astype(jnp.float32)
    ones = jnp.ones((slots, LANES), jnp.bfloat16)
    first_col = jnp.where(iota((cols, LANES), 0) == 0, not_first_col, 0.0) - SHIFT
    for i in range(rows):
        place = (iota((cols, slots), 0) + i * cols == bin_of).astype(jnp.float32).astype(jnp.bfloat16)
        total = jnp.dot(place, got, preferred_element_type=jnp.float32)
        for c in range(tiles):
            b_ref[i, c] = total[:, c * LANES : (c + 1) * LANES]
        hits = jnp.dot(place, ones, preferred_element_type=jnp.float32)
        diag = 2.0 * hits + first_col
        diag_ref[i] = diag + not_first_row if i == 0 else diag
    write_edges(
        b_ref, lambda at: load(p1_ref, at), lambda i: load(p2_ref, i, slice(None)), *edge_refs
    )


def write_edges(v_ref, p1_last_row, p2_last_cols, row0_ref, row7_ref, col0_ref, col7_ref):
    rows, _, cols, _ = v_ref.shape
    for x in range(0, cols, SUBLANES):
        at = slice(x, x + SUBLANES)
        store(row0_ref, load_field(v_ref, 0, at), at)
        v = load_field(v_ref, rows - 1, at)
        store(row7_ref, add(v, dip_part(p1_last_row(at), *stencil(v))), at)
    for i in range(rows):
        store(col0_ref, load_field(v_ref, i, slice(0, 1)), slice(i, i + 1))
        v = load_field(v_ref, i, slice(cols - SUBLANES, cols))
        moved = add(v, dip_part(p2_last_cols(i), *stencil(v)))
        store(col7_ref, [t[SUBLANES - 1 :] for t in moved], slice(i, i + 1))


def apply_kernel(v_ref, p1_ref, p2_ref, diag_ref, out_ref, sums_ref, second_ref):
    rows, tiles, cols, _ = v_ref.shape
    sub_index = iota((SUBLANES, LANES), 0)
    zero = [jnp.zeros((SUBLANES, LANES), jnp.float32)] * tiles
    for i in range(rows):
        for c in range(tiles):
            second_ref[i, c, :SUBLANES, :] = zero[0]

    def filters(i, x, v, shifted_v, above, below):
        at = slice(x, x + SUBLANES)
        v_row, second_row = v_ref.at[i], second_ref.at[i]
        odd, even = shifted_v
        p1, p2 = load(p1_ref.at[i], at), load(p2_ref.at[i], at)
        if x + SUBLANES < cols:
            right = load_tiles(v_row, slice(x + 1, x + 1 + SUBLANES))
        else:
            right = [jnp.where(sub_index == SUBLANES - 1, 0.0, pltpu.roll(t, SUBLANES - 1, 0)) for t in v]
        first = sub(sub(below, v), dip_part(p1, odd, even))
        second = sub(sub(right, v), dip_part(p2, odd, even))
        for c in range(tiles):
            second_row[c, x + SUBLANES : x + 2 * SUBLANES, :] = second[c]
        left = [second_row[c, x + SUBLANES - 1 : x + 2 * SUBLANES - 1, :] for c in range(tiles)]
        a1, b1 = adjoint_terms(p1, first)
        a2, b2 = adjoint_terms(p2, second)
        a, b = add(a1, a2), add(b1, b2)
        diag = diag_ref.at[i][at, :]
        rest = [
            (diag * c + (f + s)) - ((f1 + s1) - (y + y))
            for c, f, s, f1, s1, y in zip(v, above, left, first, second, b)
        ]
        return first, (rest, add(a, b), sub(b, a))

    def adjoint(i, x, pending):
        at = slice(x, x + SUBLANES)
        rest, up, down = pending
        out = [r - (u + d) for r, u, d in zip(rest, later(up), earlier(down))]
        out_row = out_ref.at[i]
        for c in range(tiles):
            out_row[c, at, :] = out[c]
        return dot(load_tiles(v_ref.at[i], at), out)

    vout, vv = zero[0], zero[0]
    for x in range(0, cols, GROUP):
        chunks = range(x, x + GROUP, SUBLANES)

        def fetch(i):
            below = [load_tiles(v_ref.at[i], slice(k, k + SUBLANES)) for k in chunks]
            return below, [stencil(tiles_of) for tiles_of in below]

        def all_filters(i, v, shifted_v, first, below):
            done = [filters(i, k, *rest) for k, *rest in zip(chunks, v, shifted_v, first, below)]
            return [pair[0] for pair in done], [pair[1] for pair in done]

        def all_adjoint(i, own, pending):
            for k, waiting in zip(chunks, pending):
                own = own + adjoint(i, k, waiting)
            return own

        def norms(norm, v):
            for tiles_of in v:
                norm = norm + dot(tiles_of, tiles_of)
            return norm

        nothing = [zero] * len(chunks)
        v, shifted_v = fetch(0)
        below, below_shifted = fetch(1)
        first, pending = all_filters(0, v, shifted_v, nothing, below)

        def body(i, carry):
            v, shifted_v, first, pending, own, norm = carry
            below, below_shifted = fetch(i + 1)
            first, fresh = all_filters(i, v, shifted_v, first, below)
            own = all_adjoint(i - 1, own, pending)
            return below, below_shifted, first, fresh, own, norms(norm, v)

        carry = (below, below_shifted, first, pending, zero[0], norms(zero[0], v))
        v, shifted_v, first, pending, own, norm = lax.fori_loop(1, rows - 1, body, carry)
        first, fresh = all_filters(rows - 1, v, shifted_v, first, nothing)
        own = all_adjoint(rows - 1, all_adjoint(rows - 2, own, pending), fresh)
        vout, vv = vout + own, vv + norms(norm, v)
    sums_ref[0], sums_ref[1] = vout, vv


def halo_corrections(out_ref, p1_ref, p2_ref, below_ref, above_ref, right_ref, left_ref):
    rows, _, cols, _ = out_ref.shape
    last = rows - 1
    sub_index = iota((SUBLANES, LANES), 0)
    for x in range(0, cols, SUBLANES):
        at = slice(x, x + SUBLANES)
        store_field(out_ref, sub(load_field(out_ref, 0, at), load(above_ref, at)), 0, at)
        r = load(below_ref, at)
        moved = adjoint_finish(r, *adjoint_terms(load(p1_ref, last, at), r))
        store_field(out_ref, sub(load_field(out_ref, last, at), moved), last, at)
    for i in range(rows):
        at = slice(0, SUBLANES)
        r = [jnp.where(sub_index == 0, t, 0.0) for t in load(left_ref, slice(i, i + 1))]
        store_field(out_ref, sub(load_field(out_ref, i, at), r), i, at)
        at = slice(cols - SUBLANES, cols)
        r = [jnp.where(sub_index == SUBLANES - 1, t, 0.0) for t in load(right_ref, slice(i, i + 1))]
        moved = adjoint_finish(r, *adjoint_terms(load(p2_ref, i, at), r))
        store_field(out_ref, sub(load_field(out_ref, i, at), moved), i, at)


def settle(image_ref, p1_ref, p2_ref, below_ref, above_ref, right_ref, left_ref, row7_ref, col7_ref, out_ref):
    across = jnp.zeros((SUBLANES, LANES), jnp.float32)
    for mine, theirs in ((row7_ref, below_ref), (col7_ref, right_ref)):
        for x in range(0, mine.shape[0], SUBLANES):
            at = slice(x, x + SUBLANES)
            across = across + dot(load(mine, at), load(theirs, at))
    halo_corrections(out_ref, p1_ref, p2_ref, below_ref, above_ref, right_ref, left_ref)
    return across


def correct_kernel(
    image_ref, p1_ref, p2_ref, below_ref, above_ref, right_ref, left_ref, row7_ref, col7_ref,
    out_ref, across_ref, *edge_refs,
):
    across_ref[...] = settle(
        image_ref, p1_ref, p2_ref, below_ref, above_ref, right_ref, left_ref, row7_ref, col7_ref, out_ref
    )
    rows, _, cols, _ = out_ref.shape
    write_edges(
        out_ref,
        lambda at: load(p1_ref, rows - 1, at),
        lambda i: load(p2_ref, i, slice(cols - SUBLANES, cols)),
        *edge_refs,
    )


def moments_kernel(
    image_ref, p1_ref, p2_ref, below_ref, above_ref, right_ref, left_ref, row7_ref, col7_ref, *refs
):
    sums_refs, across_refs = refs[:ITERS], refs[ITERS : 2 * ITERS - 1]
    out_ref, message_ref = refs[2 * ITERS - 1 :]
    final = settle(
        image_ref, p1_ref, p2_ref, below_ref, above_ref, right_ref, left_ref, row7_ref, col7_ref, out_ref
    )
    m = []
    for sums_ref, across in zip(sums_refs, [ref[...] for ref in across_refs] + [final]):
        m.append(sums_ref[1])
        m.append(sums_ref[0] - 2.0 * across)
    sub_index, lane = iota((SUBLANES, LANES), 0), iota((SUBLANES, LANES), 1)
    block = jnp.zeros((SUBLANES, LANES), jnp.float32)
    for k, part in enumerate(m):
        block = jnp.where(sub_index == k, jnp.sum(part, axis=0, keepdims=True), block)
    total = jnp.sum(block, axis=1, keepdims=True)
    line = jnp.sum(jnp.where(sub_index == lane, total, 0.0), axis=0, keepdims=True)
    message_ref[...] = jnp.broadcast_to(line[None], message_ref.shape)


def coefficients(m):
    zero = jnp.zeros_like(m[0])
    model = [zero] * ITERS
    residual = [zero + 1.0] + [zero] * ITERS
    direction = [zero + 1.0] + [zero] * (ITERS - 1)
    norm_now = m[0]

    def inner(x, y, count):
        total = zero
        for i in range(count):
            for j in range(len(y)):
                if i + j < len(m):
                    total = total + x[i] * y[j] * m[i + j]
        return total

    for sweep in range(ITERS):
        image = [SHIFT * d for d in direction] + [zero]
        image = [image[0]] + [s + d for s, d in zip(image[1:], direction)]
        alpha = norm_now / inner(direction, image[: sweep + 2], sweep + 1)
        model = [s + alpha * d for s, d in zip(model, direction)]
        residual = [r - alpha * d for r, d in zip(residual, image)]
        if sweep + 1 < ITERS:
            norm_next = inner(residual, residual[: sweep + 2], sweep + 2)
            beta = norm_next / norm_now
            direction = [r + beta * d for r, d in zip(residual, direction)]
            norm_now = norm_next
    return [2.0 * s for s in model] + residual


def finish_kernel(parts_ref, b_ref, v1_ref, v2_ref, v3_ref, model_hbm, residual_hbm, model_ref, residual_ref, sems):
    rows, _, cols, _ = b_ref.shape
    line = jnp.sum(parts_ref[...], axis=0)
    sub_index, lane = iota((SUBLANES, LANES), 0), iota((SUBLANES, LANES), 1)
    total = jnp.sum(jnp.where(sub_index == lane, line, 0.0), axis=1, keepdims=True)
    total = jnp.broadcast_to(total, (SUBLANES, LANES))
    m = [jnp.broadcast_to(total[k : k + 1], (SUBLANES, LANES)) for k in range(2 * ITERS)]
    weights = coefficients(m)
    model, residual = weights[:ITERS], weights[ITERS:]

    def copies(i):
        return (
            pltpu.make_async_copy(model_ref.at[i], model_hbm.at[i], sems.at[0, i]),
            pltpu.make_async_copy(residual_ref.at[i], residual_hbm.at[i], sems.at[1, i]),
        )

    def body(i, carry):
        for x in range(0, cols, SUBLANES):
            at = slice(x, x + SUBLANES)
            b, v1, v2, v3 = (load_field(ref, i, at) for ref in (b_ref, v1_ref, v2_ref, v3_ref))
            store(model_ref, [model[0] * s + model[1] * t + model[2] * u for s, t, u in zip(b, v1, v2)], i, at)
            store(
                residual_ref,
                [(residual[0] * s + residual[1] * t) + (residual[2] * u + residual[3] * w) for s, t, u, w in zip(b, v1, v2, v3)],
                i, at,
            )
        for copy in copies(i):
            copy.start()
        return carry

    lax.fori_loop(0, rows, body, 0)
    for i in range(rows):
        for copy in copies(i):
            copy.wait()


def f32(*shape):
    return pltpu.VMEM(shape, jnp.float32)


def call(kernel, outs, *args, name, scratch=(), aliases=None, cost=None, ins=None, places=None):
    return pl.pallas_call(
        kernel,
        out_shape=outs,
        in_specs=ins or [IN_VMEM] * len(args),
        out_specs=places or [IN_VMEM] * len(outs),
        scratch_shapes=list(scratch),
        input_output_aliases=aliases or {},
        compiler_params=PARAMS,
        cost_estimate=cost,
        name=name,
    )(*args)


def in_hbm(array):
    return pltpu.with_memory_space_constraint(array, pltpu.HBM)


def per_device(traces, trace_owner, trace_cell, acquired, inline_dip, cross_dip):
    rows, cols, samples = inline_dip.shape
    devices = lax.axis_size("inl") * lax.axis_size("xl")
    held = traces.shape[0]
    capacity = max(2, 2 * held // devices)
    slots = devices * capacity
    message = (slots, samples + LANES)
    if is_compact(capacity):
        message = (devices, samples // LANES * capacity + SUBLANES, LANES)
    small = pltpu.VMEM((1, held), jnp.int32)
    inputs = (trace_owner.reshape(1, held), trace_cell[None], acquired[None], traces, inline_dip, cross_dip)
    sent, p1_last, p2_last = call(
        functools.partial(pack_kernel, capacity),
        [
            jax.ShapeDtypeStruct(message, jnp.bfloat16),
            f32(cols, samples),
            f32(rows, SUBLANES, samples),
        ],
        *(in_hbm(x) for x in inputs),
        name="pack", ins=[IN_HBM] * len(inputs),
        scratch=[small, small, small, pltpu.VMEM((held, samples), jnp.bfloat16), pltpu.SemaphoreType.DMA((6,))],
    )
    got = lax.all_to_all(sent, ("inl", "xl"), split_axis=0, concat_axis=0, tiled=True)
    edge_shapes = [f32(cols, samples), f32(cols, samples), f32(rows, samples), f32(rows, samples)]
    tile = f32(rows, samples // LANES, cols, LANES)
    b, diag, *edges = call(
        functools.partial(bin_kernel, capacity), [tile, f32(rows, cols, LANES)] + edge_shapes, got, p1_last, p2_last,
        name="bin",
    )
    fields, sums, products = [b], [], []
    cost = pl.CostEstimate(
        flops=60 * rows * cols * samples, bytes_accessed=16 * rows * cols * samples, transcendentals=0
    )
    for step in range(ITERS):
        row0, row7, col0, col7 = edges
        below = shifted(row0, "inl", -1)
        above = shifted(row7, "inl", 1)
        right = shifted(col0, "xl", -1)
        left = shifted(col7, "xl", 1)
        image, partial = call(
            apply_kernel,
            [tile, f32(2, SUBLANES, LANES)],
            fields[-1], inline_dip, cross_dip, diag,
            name="apply",
            scratch=[pltpu.VMEM((rows, samples // LANES, SUBLANES + cols, LANES), jnp.float32)],
            cost=cost,
        )
        sums.append(partial)
        args = [image, inline_dip, cross_dip, below, above, right, left, row7, col7]
        if step + 1 < ITERS:
            image, across, *edges = call(
                correct_kernel, [tile, f32(SUBLANES, LANES)] + edge_shapes, *args, name="correct", aliases={0: 0}
            )
            products.append(across)
        else:
            image, message = call(
                moments_kernel, [tile, f32(devices, 1, LANES)], *args, *sums, *products,
                name="moments", aliases={0: 0},
            )
        fields.append(image)
    parts = lax.all_to_all(message, ("inl", "xl"), split_axis=0, concat_axis=0, tiled=True)
    out = jax.ShapeDtypeStruct((rows, cols, samples), jnp.float32)
    return tuple(
        call(
            finish_kernel, [out, out], parts, *fields,
            name="finish", places=[pl.BlockSpec(memory_space=pl.ANY)] * 2,
            scratch=[
                pltpu.VMEM((rows, cols, samples), jnp.float32),
                pltpu.VMEM((rows, cols, samples), jnp.float32),
                pltpu.SemaphoreType.DMA((2, rows)),
            ],
        )
    )


def solution(mesh):
    placed = (
        P(("inl", "xl"), None),
        P(("inl", "xl"), None),
        P(("inl", "xl")),
        P(("inl", "xl")),
        P("inl", "xl", None),
        P("inl", "xl", None),
    )
    return jax.shard_map(
        per_device,
        mesh=mesh,
        in_specs=placed,
        out_specs=(P("inl", "xl", None), P("inl", "xl", None)),
        check_vma=False,
    )
```

```python
import functools

import jax
import jax.numpy as jnp
from jax import lax
from jax.experimental import pallas as pl
from jax.experimental.pallas import tpu as pltpu
from jax.sharding import PartitionSpec as P

ITERS = 3
LANES = 128
SUBLANES = 8
GROUP = 16

SHIFT = 6.0
IN_VMEM = pl.BlockSpec(memory_space=pltpu.VMEM)
IN_HBM = pl.BlockSpec(memory_space=pltpu.HBM)
PARAMS = pltpu.CompilerParams(vmem_limit_bytes=16 << 20)


def shifted(value, axis, steps):
    count = lax.axis_size(axis)
    initial, last = (max(0, -steps), min(count, count - steps))
    return lax.ppermute(value, axis, [(source, source + steps) for source in range(initial, last)])


def iota(shape, dim):
    return lax.broadcasted_iota(jnp.int32, shape, dim)


def earlier(tiles):
    lane = iota(tiles[0].shape, 1)
    rolled = [pltpu.roll(tile, 1, 1) for tile in tiles]
    before = [jnp.zeros_like(tiles[0])] + rolled[:-1]
    return [jnp.where(lane == 0, edge, inner) for edge, inner in zip(before, rolled)]


def later(tiles):
    lane = iota(tiles[0].shape, 1)
    rolled = [pltpu.roll(tile, LANES - 1, 1) for tile in tiles]
    after = rolled[1:] + [jnp.zeros_like(tiles[0])]
    return [jnp.where(lane == LANES - 1, edge, inner) for edge, inner in zip(after, rolled)]


def stencil(v):
    em, ep = earlier(v), later(v)
    odd = [m - p for m, p in zip(em, ep)]
    even = [(m + p) - (c + c) for m, p, c in zip(em, ep, v)]
    return odd, even


def dip_part(p, odd, even):
    return [(0.5 * d) * (o + d * e) for d, o, e in zip(p, odd, even)]


def adjoint_terms(p, r):
    a = [(0.5 * d) * x for d, x in zip(p, r)]
    b = [d * x for d, x in zip(p, a)]
    return a, b


def adjoint_finish(r, a, b):
    up = later([x + y for x, y in zip(a, b)])
    down = earlier([y - x for x, y in zip(a, b)])
    return [(x + u) + (d - (y + y)) for x, u, d, y in zip(r, up, down, b)]


def load(ref, *index):
    count = ref.shape[-1] // LANES
    return [ref[(*index, slice(c * LANES, (c + 1) * LANES))] for c in range(count)]


def store(ref, tiles, *index):
    for c, tile in enumerate(tiles):
        ref[(*index, slice(c * LANES, (c + 1) * LANES))] = tile


def load_tiles(ref, at):
    return [ref[c, at, :] for c in range(ref.shape[0])]


def load_field(ref, i, at):
    return [ref[i, c, at, :] for c in range(ref.shape[1])]


def store_field(ref, tiles, i, at):
    for c, tile in enumerate(tiles):
        ref[i, c, at, :] = tile


def add(x, y):
    return [a + b for a, b in zip(x, y)]


def sub(x, y):
    return [a - b for a, b in zip(x, y)]


def dot(x, y):
    return functools.reduce(lambda s, t: s + t, [a * b for a, b in zip(x, y)])


def is_compact(capacity):
    return capacity % 16 == 0 and LANES % capacity == 0


def pack_kernel(
    capacity, owner_hbm, cell_hbm, live_hbm, traces_hbm, p1_hbm, p2_hbm, out_ref, p1_last_ref, p2_last_ref,
    owner_ref, cell_ref, live_ref, traces_ref, sems,
):
    held, samples = traces_ref.shape
    slots = lax.axis_size("inl") * lax.axis_size("xl") * capacity
    rows, cols, _ = p1_hbm.shape
    pairs = (
        (owner_hbm, owner_ref), (cell_hbm, cell_ref), (live_hbm, live_ref), (traces_hbm, traces_ref),
        (p1_hbm.at[rows - 1], p1_last_ref), (p2_hbm.at[:, pl.ds(cols - SUBLANES, SUBLANES)], p2_last_ref),
    )
    copies = [pltpu.make_async_copy(src, dst, sems.at[k]) for k, (src, dst) in enumerate(pairs)]
    for copy in copies:
        copy.start()
    for copy in copies[:3]:
        copy.wait()
    owner = owner_ref[...].astype(jnp.float32)
    row, col = iota((held, held), 0), iota((held, held), 1)
    owner_down = jnp.sum(jnp.where(row == col, owner, 0.0), axis=1, keepdims=True)
    earlier_same = (owner_down == owner) & (row < col)
    rank = jnp.sum(jnp.where(earlier_same, 1.0, 0.0), axis=0, keepdims=True)
    slot = jnp.where(live_ref[...] > 0, owner * capacity + rank, -1.0).astype(jnp.int32)
    chosen = (iota((slots, held), 0) == slot).astype(jnp.float32).astype(jnp.bfloat16)
    cell = cell_ref[...]
    kind = iota((LANES, held), 0)
    upper = (lax.shift_right_logical(cell, 6) + 1).astype(jnp.float32)
    lower = (cell & 63).astype(jnp.float32)
    codes = jnp.where(kind == 0, upper, jnp.where(kind == 1, lower, 0.0)).astype(jnp.bfloat16)
    if not is_compact(capacity):
        sent = lax.dot_general(chosen, codes, (((1,), (1,)), ((), ())), preferred_element_type=jnp.float32)
        out_ref[:, samples:] = sent.astype(jnp.bfloat16)
        copies[3].wait()
        packed = jnp.dot(chosen, traces_ref[...], preferred_element_type=jnp.float32)
        out_ref[:, :samples] = packed.astype(jnp.bfloat16)
    else:
        sent = lax.dot_general(codes[:16], chosen, (((1,), (1,)), ((), ())), preferred_element_type=jnp.float32)
        per = LANES // capacity
        here = lax.rem(lax.axis_index("inl") * lax.axis_size("xl") + lax.axis_index("xl"), per)
        mine = lax.div(iota((SUBLANES, LANES), 1), capacity) == here
        moves = [lax.rem(here - j + per, per) * capacity for j in range(per)]
        copies[3].wait()
        packed = jnp.dot(chosen, traces_ref[...], preferred_element_type=jnp.float32)
        for d in range(slots // capacity):
            at = slice(d * capacity, (d + 1) * capacity)
            tile = slice(d // per * LANES, (d // per + 1) * LANES)
            code = jnp.where(mine, pltpu.roll(sent[:SUBLANES, tile], moves[d % per], 1), 0.0)
            parts = [packed[at, c : c + LANES] for c in range(0, samples, LANES)]
            out_ref[d] = jnp.concatenate(parts + [code], axis=0).astype(jnp.bfloat16)
    for copy in copies[4:]:
        copy.wait()


def unpack(capacity, samples, got_ref):
    if not is_compact(capacity):
        kind = iota((SUBLANES, LANES), 1)
        weight = jnp.where(kind == 0, 64.0, jnp.where(kind == 1, 1.0, 0.0)).astype(jnp.bfloat16)
        value = lax.dot_general(
            weight, got_ref[:, samples:], (((1,), (1,)), ((), ())), preferred_element_type=jnp.float32
        )
        return got_ref[:, :samples], value[:1].astype(jnp.int32) - 64
    sources, per = got_ref.shape[0], LANES // capacity
    blocks = [got_ref[d].astype(jnp.float32) for d in range(sources)]
    tiles = samples // LANES
    values = []
    for first in range(0, sources, per):
        code = functools.reduce(lambda s, t: s + t, [blocks[d][tiles * capacity :] for d in range(first, first + per)])
        values.append(64.0 * code[:1] + code[1:2] - 64.0)
    columns = [
        jnp.concatenate([blocks[d][c * capacity : (c + 1) * capacity] for d in range(sources)], axis=0)
        for c in range(tiles)
    ]
    got = jnp.concatenate([column.astype(jnp.bfloat16) for column in columns], axis=1)
    return got, jnp.concatenate(values, axis=1).astype(jnp.int32)


def bin_kernel(capacity, got_ref, p1_ref, p2_ref, b_ref, diag_ref, *edge_refs):
    rows, tiles, cols, _ = b_ref.shape
    got, bin_of = unpack(capacity, tiles * LANES, got_ref)
    slots = got.shape[0]
    not_first_row = (lax.axis_index("inl") > 0).astype(jnp.float32)
    not_first_col = (lax.axis_index("xl") > 0).astype(jnp.float32)
    ones = jnp.ones((slots, LANES), jnp.bfloat16)
    first_col = jnp.where(iota((cols, LANES), 0) == 0, not_first_col, 0.0) - SHIFT
    for i in range(rows):
        place = (iota((cols, slots), 0) + i * cols == bin_of).astype(jnp.float32).astype(jnp.bfloat16)
        total = jnp.dot(place, got, preferred_element_type=jnp.float32)
        for c in range(tiles):
            b_ref[i, c] = total[:, c * LANES : (c + 1) * LANES]
        hits = jnp.dot(place, ones, preferred_element_type=jnp.float32)
        diag = 2.0 * hits + first_col
        diag_ref[i] = diag + not_first_row if i == 0 else diag
    write_edges(
        b_ref, lambda at: load(p1_ref, at), lambda i: load(p2_ref, i, slice(None)), *edge_refs
    )


def write_edges(v_ref, p1_last_row, p2_last_cols, row0_ref, row7_ref, col0_ref, col7_ref):
    rows, _, cols, _ = v_ref.shape
    for x in range(0, cols, SUBLANES):
        at = slice(x, x + SUBLANES)
        store(row0_ref, load_field(v_ref, 0, at), at)
        v = load_field(v_ref, rows - 1, at)
        store(row7_ref, add(v, dip_part(p1_last_row(at), *stencil(v))), at)
    for i in range(rows):
        store(col0_ref, load_field(v_ref, i, slice(0, 1)), slice(i, i + 1))
        v = load_field(v_ref, i, slice(cols - SUBLANES, cols))
        moved = add(v, dip_part(p2_last_cols(i), *stencil(v)))
        store(col7_ref, [t[SUBLANES - 1 :] for t in moved], slice(i, i + 1))


def apply_kernel(v_ref, p1_ref, p2_ref, diag_ref, out_ref, sums_ref, edge_ref):
    rows, tiles, cols, _ = v_ref.shape
    sub_index = iota((SUBLANES, LANES), 0)
    zero = [jnp.zeros((SUBLANES, LANES), jnp.float32)] * tiles
    edge_ref[...] = jnp.zeros_like(edge_ref)

    def roll_tiles(values, steps):
        return [pltpu.roll(t, steps, 0) for t in values]

    def filters(i, x, v, right, shifted_v, above, below, down_before):
        at = slice(x, x + SUBLANES)
        odd, even = shifted_v
        p1, p2 = load(p1_ref.at[i], at), load(p2_ref.at[i], at)
        first = sub(sub(below, v), dip_part(p1, odd, even))
        second = sub(sub(right, v), dip_part(p2, odd, even))
        down = roll_tiles(second, 1)
        left = [jnp.where(sub_index == 0, e, t) for e, t in zip(down_before, down)]
        a1, b1 = adjoint_terms(p1, first)
        a2, b2 = adjoint_terms(p2, second)
        a, b = add(a1, a2), add(b1, b2)
        diag = diag_ref.at[i][at, :]
        rest = [
            (diag * c + (f + s)) - ((f1 + s1) - (y + y))
            for c, f, s, f1, s1, y in zip(v, above, left, first, second, b)
        ]
        return first, (rest, add(a, b), sub(b, a)), down

    def adjoint(i, x, pending):
        at = slice(x, x + SUBLANES)
        rest, up, down = pending
        out = [r - (u + d) for r, u, d in zip(rest, later(up), earlier(down))]
        out_row = out_ref.at[i]
        for c in range(tiles):
            out_row[c, at, :] = out[c]
        return dot(load_tiles(v_ref.at[i], at), out)

    vout, vv = zero[0], zero[0]
    for x in range(0, cols, GROUP):
        chunks = range(x, x + GROUP, SUBLANES)

        def fetch(i):
            below = [load_tiles(v_ref.at[i], slice(k, k + SUBLANES)) for k in chunks]
            return below, [stencil(tiles_of) for tiles_of in below]

        def all_filters(i, v, shifted_v, first, below):
            leads = [roll_tiles(tiles_of, SUBLANES - 1) for tiles_of in v]
            if x + GROUP < cols:
                following = load_tiles(v_ref.at[i], slice(x + GROUP, x + GROUP + SUBLANES))
                leads.append(roll_tiles(following, SUBLANES - 1))
            else:
                leads.append(zero)
            edge_row = edge_ref.at[i]
            down = load_tiles(edge_row, slice(None))
            firsts, pending = [], []
            for n, k in enumerate(chunks):
                right = [jnp.where(sub_index == SUBLANES - 1, e, t) for e, t in zip(leads[n + 1], leads[n])]
                made, waiting, down = filters(i, k, v[n], right, shifted_v[n], first[n], below[n], down)
                firsts.append(made)
                pending.append(waiting)
            for c in range(tiles):
                edge_row[c, :, :] = down[c]
            return firsts, pending

        def all_adjoint(i, own, pending):
            for k, waiting in zip(chunks, pending):
                own = own + adjoint(i, k, waiting)
            return own

        def norms(norm, v):
            for tiles_of in v:
                norm = norm + dot(tiles_of, tiles_of)
            return norm

        nothing = [zero] * len(chunks)
        v, shifted_v = fetch(0)
        below, below_shifted = fetch(1)
        first, pending = all_filters(0, v, shifted_v, nothing, below)

        def body(i, carry):
            v, shifted_v, first, pending, own, norm = carry
            below, below_shifted = fetch(i + 1)
            first, fresh = all_filters(i, v, shifted_v, first, below)
            own = all_adjoint(i - 1, own, pending)
            return below, below_shifted, first, fresh, own, norms(norm, v)

        carry = (below, below_shifted, first, pending, zero[0], norms(zero[0], v))
        v, shifted_v, first, pending, own, norm = lax.fori_loop(1, rows - 1, body, carry)
        first, fresh = all_filters(rows - 1, v, shifted_v, first, nothing)
        own = all_adjoint(rows - 1, all_adjoint(rows - 2, own, pending), fresh)
        vout, vv = vout + own, vv + norms(norm, v)
    sums_ref[0], sums_ref[1] = vout, vv


def halo_corrections(out_ref, p1_ref, p2_ref, below_ref, above_ref, right_ref, left_ref):
    rows, _, cols, _ = out_ref.shape
    last = rows - 1
    sub_index = iota((SUBLANES, LANES), 0)
    for x in range(0, cols, SUBLANES):
        at = slice(x, x + SUBLANES)
        store_field(out_ref, sub(load_field(out_ref, 0, at), load(above_ref, at)), 0, at)
        r = load(below_ref, at)
        moved = adjoint_finish(r, *adjoint_terms(load(p1_ref, last, at), r))
        store_field(out_ref, sub(load_field(out_ref, last, at), moved), last, at)
    for i in range(rows):
        at = slice(0, SUBLANES)
        r = [jnp.where(sub_index == 0, t, 0.0) for t in load(left_ref, slice(i, i + 1))]
        store_field(out_ref, sub(load_field(out_ref, i, at), r), i, at)
        at = slice(cols - SUBLANES, cols)
        r = [jnp.where(sub_index == SUBLANES - 1, t, 0.0) for t in load(right_ref, slice(i, i + 1))]
        moved = adjoint_finish(r, *adjoint_terms(load(p2_ref, i, at), r))
        store_field(out_ref, sub(load_field(out_ref, i, at), moved), i, at)


def settle(image_ref, p1_ref, p2_ref, below_ref, above_ref, right_ref, left_ref, row7_ref, col7_ref, out_ref):
    across = jnp.zeros((SUBLANES, LANES), jnp.float32)
    for mine, theirs in ((row7_ref, below_ref), (col7_ref, right_ref)):
        for x in range(0, mine.shape[0], SUBLANES):
            at = slice(x, x + SUBLANES)
            across = across + dot(load(mine, at), load(theirs, at))
    halo_corrections(out_ref, p1_ref, p2_ref, below_ref, above_ref, right_ref, left_ref)
    return across


def correct_kernel(
    image_ref, p1_ref, p2_ref, below_ref, above_ref, right_ref, left_ref, row7_ref, col7_ref,
    out_ref, across_ref, *edge_refs,
):
    across_ref[...] = settle(
        image_ref, p1_ref, p2_ref, below_ref, above_ref, right_ref, left_ref, row7_ref, col7_ref, out_ref
    )
    rows, _, cols, _ = out_ref.shape
    write_edges(
        out_ref,
        lambda at: load(p1_ref, rows - 1, at),
        lambda i: load(p2_ref, i, slice(cols - SUBLANES, cols)),
        *edge_refs,
    )


def moments_kernel(
    image_ref, p1_ref, p2_ref, below_ref, above_ref, right_ref, left_ref, row7_ref, col7_ref, *refs
):
    sums_refs, across_refs = refs[:ITERS], refs[ITERS : 2 * ITERS - 1]
    out_ref, message_ref = refs[2 * ITERS - 1 :]
    final = settle(
        image_ref, p1_ref, p2_ref, below_ref, above_ref, right_ref, left_ref, row7_ref, col7_ref, out_ref
    )
    m = []
    for sums_ref, across in zip(sums_refs, [ref[...] for ref in across_refs] + [final]):
        m.append(sums_ref[1])
        m.append(sums_ref[0] - 2.0 * across)
    sub_index, lane = iota((SUBLANES, LANES), 0), iota((SUBLANES, LANES), 1)
    block = jnp.zeros((SUBLANES, LANES), jnp.float32)
    for k, part in enumerate(m):
        block = jnp.where(sub_index == k, jnp.sum(part, axis=0, keepdims=True), block)
    total = jnp.sum(block, axis=1, keepdims=True)
    line = jnp.sum(jnp.where(sub_index == lane, total, 0.0), axis=0, keepdims=True)
    message_ref[...] = jnp.broadcast_to(line[None], message_ref.shape)


def coefficients(m):
    zero = jnp.zeros_like(m[0])
    model = [zero] * ITERS
    residual = [zero + 1.0] + [zero] * ITERS
    direction = [zero + 1.0] + [zero] * (ITERS - 1)
    norm_now = m[0]

    def inner(x, y, count):
        total = zero
        for i in range(count):
            for j in range(len(y)):
                if i + j < len(m):
                    total = total + x[i] * y[j] * m[i + j]
        return total

    for sweep in range(ITERS):
        image = [SHIFT * d for d in direction] + [zero]
        image = [image[0]] + [s + d for s, d in zip(image[1:], direction)]
        alpha = norm_now / inner(direction, image[: sweep + 2], sweep + 1)
        model = [s + alpha * d for s, d in zip(model, direction)]
        residual = [r - alpha * d for r, d in zip(residual, image)]
        if sweep + 1 < ITERS:
            norm_next = inner(residual, residual[: sweep + 2], sweep + 2)
            beta = norm_next / norm_now
            direction = [r + beta * d for r, d in zip(residual, direction)]
            norm_now = norm_next
    return [2.0 * s for s in model] + residual


def finish_kernel(parts_ref, b_ref, v1_ref, v2_ref, v3_ref, model_hbm, residual_hbm, model_ref, residual_ref, sems):
    rows, _, cols, _ = b_ref.shape
    line = jnp.sum(parts_ref[...], axis=0)
    sub_index, lane = iota((SUBLANES, LANES), 0), iota((SUBLANES, LANES), 1)
    total = jnp.sum(jnp.where(sub_index == lane, line, 0.0), axis=1, keepdims=True)
    total = jnp.broadcast_to(total, (SUBLANES, LANES))
    m = [jnp.broadcast_to(total[k : k + 1], (SUBLANES, LANES)) for k in range(2 * ITERS)]
    weights = coefficients(m)
    model, residual = weights[:ITERS], weights[ITERS:]

    def copies(i):
        return (
            pltpu.make_async_copy(model_ref.at[i], model_hbm.at[i], sems.at[0, i]),
            pltpu.make_async_copy(residual_ref.at[i], residual_hbm.at[i], sems.at[1, i]),
        )

    def body(i, carry):
        for x in range(0, cols, SUBLANES):
            at = slice(x, x + SUBLANES)
            b, v1, v2, v3 = (load_field(ref, i, at) for ref in (b_ref, v1_ref, v2_ref, v3_ref))
            store(model_ref, [model[0] * s + model[1] * t + model[2] * u for s, t, u in zip(b, v1, v2)], i, at)
            store(
                residual_ref,
                [(residual[0] * s + residual[1] * t) + (residual[2] * u + residual[3] * w) for s, t, u, w in zip(b, v1, v2, v3)],
                i, at,
            )
        for copy in copies(i):
            copy.start()
        return carry

    lax.fori_loop(0, rows, body, 0)
    for i in range(rows):
        for copy in copies(i):
            copy.wait()


def f32(*shape):
    return pltpu.VMEM(shape, jnp.float32)


def call(kernel, outs, *args, name, scratch=(), aliases=None, cost=None, ins=None, places=None):
    return pl.pallas_call(
        kernel,
        out_shape=outs,
        in_specs=ins or [IN_VMEM] * len(args),
        out_specs=places or [IN_VMEM] * len(outs),
        scratch_shapes=list(scratch),
        input_output_aliases=aliases or {},
        compiler_params=PARAMS,
        cost_estimate=cost,
        name=name,
    )(*args)


def in_hbm(array):
    return pltpu.with_memory_space_constraint(array, pltpu.HBM)


def per_device(traces, trace_owner, trace_cell, acquired, inline_dip, cross_dip):
    rows, cols, samples = inline_dip.shape
    devices = lax.axis_size("inl") * lax.axis_size("xl")
    held = traces.shape[0]
    capacity = max(2, 2 * held // devices)
    slots = devices * capacity
    message = (slots, samples + LANES)
    if is_compact(capacity):
        message = (devices, samples // LANES * capacity + SUBLANES, LANES)
    small = pltpu.VMEM((1, held), jnp.int32)
    inputs = (trace_owner.reshape(1, held), trace_cell[None], acquired[None], traces, inline_dip, cross_dip)
    sent, p1_last, p2_last = call(
        functools.partial(pack_kernel, capacity),
        [
            jax.ShapeDtypeStruct(message, jnp.bfloat16),
            f32(cols, samples),
            f32(rows, SUBLANES, samples),
        ],
        *(in_hbm(x) for x in inputs),
        name="pack", ins=[IN_HBM] * len(inputs),
        scratch=[small, small, small, pltpu.VMEM((held, samples), jnp.bfloat16), pltpu.SemaphoreType.DMA((6,))],
    )
    got = lax.all_to_all(sent, ("inl", "xl"), split_axis=0, concat_axis=0, tiled=True)
    edge_shapes = [f32(cols, samples), f32(cols, samples), f32(rows, samples), f32(rows, samples)]
    tile = f32(rows, samples // LANES, cols, LANES)
    b, diag, *edges = call(
        functools.partial(bin_kernel, capacity), [tile, f32(rows, cols, LANES)] + edge_shapes, got, p1_last, p2_last,
        name="bin",
    )
    fields, sums, products = [b], [], []
    cost = pl.CostEstimate(
        flops=60 * rows * cols * samples, bytes_accessed=16 * rows * cols * samples, transcendentals=0
    )
    for step in range(ITERS):
        row0, row7, col0, col7 = edges
        below = shifted(row0, "inl", -1)
        above = shifted(row7, "inl", 1)
        right = shifted(col0, "xl", -1)
        left = shifted(col7, "xl", 1)
        image, partial = call(
            apply_kernel,
            [tile, f32(2, SUBLANES, LANES)],
            fields[-1], inline_dip, cross_dip, diag,
            name="apply",
            scratch=[pltpu.VMEM((rows, samples // LANES, SUBLANES, LANES), jnp.float32)],
            cost=cost,
        )
        sums.append(partial)
        args = [image, inline_dip, cross_dip, below, above, right, left, row7, col7]
        if step + 1 < ITERS:
            image, across, *edges = call(
                correct_kernel, [tile, f32(SUBLANES, LANES)] + edge_shapes, *args, name="correct", aliases={0: 0}
            )
            products.append(across)
        else:
            image, message = call(
                moments_kernel, [tile, f32(devices, 1, LANES)], *args, *sums, *products,
                name="moments", aliases={0: 0},
            )
        fields.append(image)
    parts = lax.all_to_all(message, ("inl", "xl"), split_axis=0, concat_axis=0, tiled=True)
    out = jax.ShapeDtypeStruct((rows, cols, samples), jnp.float32)
    return tuple(
        call(
            finish_kernel, [out, out], parts, *fields,
            name="finish", places=[pl.BlockSpec(memory_space=pl.ANY)] * 2,
            scratch=[
                pltpu.VMEM((rows, cols, samples), jnp.float32),
                pltpu.VMEM((rows, cols, samples), jnp.float32),
                pltpu.SemaphoreType.DMA((2, rows)),
            ],
        )
    )


def solution(mesh):
    placed = (
        P(("inl", "xl"), None),
        P(("inl", "xl"), None),
        P(("inl", "xl")),
        P(("inl", "xl")),
        P("inl", "xl", None),
        P("inl", "xl", None),
    )
    return jax.shard_map(
        per_device,
        mesh=mesh,
        in_specs=placed,
        out_specs=(P("inl", "xl", None), P("inl", "xl", None)),
        check_vma=False,
    )
```

```python
import functools

import jax
import jax.numpy as jnp
from jax import lax
from jax.experimental import pallas as pl
from jax.experimental.pallas import tpu as pltpu
from jax.sharding import PartitionSpec as P

ITERS = 3
LANES = 128
SUBLANES = 8
GROUP = 16

SHIFT = 6.0
IN_VMEM = pl.BlockSpec(memory_space=pltpu.VMEM)
IN_HBM = pl.BlockSpec(memory_space=pltpu.HBM)
PARAMS = pltpu.CompilerParams(vmem_limit_bytes=16 << 20)


def shifted(value, axis, steps):
    count = lax.axis_size(axis)
    initial, last = (max(0, -steps), min(count, count - steps))
    return lax.ppermute(value, axis, [(source, source + steps) for source in range(initial, last)])


def iota(shape, dim):
    return lax.broadcasted_iota(jnp.int32, shape, dim)


def earlier(tiles):
    lane = iota(tiles[0].shape, 1)
    rolled = [pltpu.roll(tile, 1, 1) for tile in tiles]
    before = [jnp.zeros_like(tiles[0])] + rolled[:-1]
    return [jnp.where(lane == 0, edge, inner) for edge, inner in zip(before, rolled)]


def later(tiles):
    lane = iota(tiles[0].shape, 1)
    rolled = [pltpu.roll(tile, LANES - 1, 1) for tile in tiles]
    after = rolled[1:] + [jnp.zeros_like(tiles[0])]
    return [jnp.where(lane == LANES - 1, edge, inner) for edge, inner in zip(after, rolled)]


def stencil(v):
    em, ep = earlier(v), later(v)
    odd = [0.5 * (m - p) for m, p in zip(em, ep)]
    even = [0.5 * (m + p) - c for m, p, c in zip(em, ep, v)]
    return odd, even


def dip_part(p, odd, even):
    return [d * (o + d * e) for d, o, e in zip(p, odd, even)]


def adjoint_terms(p, r):
    a = [d * x for d, x in zip(p, r)]
    b = [d * x for d, x in zip(p, a)]
    return a, b


def adjoint_finish(r, a, b):
    up = later([x + y for x, y in zip(a, b)])
    down = earlier([y - x for x, y in zip(a, b)])
    return [(x - y) + 0.5 * (u + d) for x, u, d, y in zip(r, up, down, b)]


def load(ref, *index):
    count = ref.shape[-1] // LANES
    return [ref[(*index, slice(c * LANES, (c + 1) * LANES))] for c in range(count)]


def store(ref, tiles, *index):
    for c, tile in enumerate(tiles):
        ref[(*index, slice(c * LANES, (c + 1) * LANES))] = tile


def load_tiles(ref, at):
    return [ref[c, at, :] for c in range(ref.shape[0])]


def load_field(ref, i, at):
    return [ref[i, c, at, :] for c in range(ref.shape[1])]


def store_field(ref, tiles, i, at):
    for c, tile in enumerate(tiles):
        ref[i, c, at, :] = tile


def add(x, y):
    return [a + b for a, b in zip(x, y)]


def sub(x, y):
    return [a - b for a, b in zip(x, y)]


def dot(x, y):
    return functools.reduce(lambda s, t: s + t, [a * b for a, b in zip(x, y)])


def is_compact(capacity):
    return capacity % 16 == 0 and LANES % capacity == 0


def pack_kernel(
    capacity, owner_hbm, cell_hbm, live_hbm, traces_hbm, p1_hbm, p2_hbm, out_ref, p1_last_ref, p2_last_ref,
    owner_ref, cell_ref, live_ref, traces_ref, sems,
):
    held, samples = traces_ref.shape
    slots = lax.axis_size("inl") * lax.axis_size("xl") * capacity
    rows, cols, _ = p1_hbm.shape
    pairs = (
        (owner_hbm, owner_ref), (cell_hbm, cell_ref), (live_hbm, live_ref), (traces_hbm, traces_ref),
        (p1_hbm.at[rows - 1], p1_last_ref), (p2_hbm.at[:, pl.ds(cols - SUBLANES, SUBLANES)], p2_last_ref),
    )
    copies = [pltpu.make_async_copy(src, dst, sems.at[k]) for k, (src, dst) in enumerate(pairs)]
    for copy in copies:
        copy.start()
    for copy in copies[:3]:
        copy.wait()
    owner = owner_ref[...].astype(jnp.float32)
    row, col = iota((held, held), 0), iota((held, held), 1)
    owner_down = jnp.sum(jnp.where(row == col, owner, 0.0), axis=1, keepdims=True)
    earlier_same = (owner_down == owner) & (row < col)
    rank = jnp.sum(jnp.where(earlier_same, 1.0, 0.0), axis=0, keepdims=True)
    slot = jnp.where(live_ref[...] > 0, owner * capacity + rank, -1.0).astype(jnp.int32)
    chosen = (iota((slots, held), 0) == slot).astype(jnp.float32).astype(jnp.bfloat16)
    cell = cell_ref[...]
    kind = iota((LANES, held), 0)
    upper = (lax.shift_right_logical(cell, 6) + 1).astype(jnp.float32)
    lower = (cell & 63).astype(jnp.float32)
    codes = jnp.where(kind == 0, upper, jnp.where(kind == 1, lower, 0.0)).astype(jnp.bfloat16)
    if not is_compact(capacity):
        sent = lax.dot_general(chosen, codes, (((1,), (1,)), ((), ())), preferred_element_type=jnp.float32)
        out_ref[:, samples:] = sent.astype(jnp.bfloat16)
        copies[3].wait()
        packed = jnp.dot(chosen, traces_ref[...], preferred_element_type=jnp.float32)
        out_ref[:, :samples] = packed.astype(jnp.bfloat16)
    else:
        sent = lax.dot_general(codes[:16], chosen, (((1,), (1,)), ((), ())), preferred_element_type=jnp.float32)
        per = LANES // capacity
        here = lax.rem(lax.axis_index("inl") * lax.axis_size("xl") + lax.axis_index("xl"), per)
        mine = lax.div(iota((SUBLANES, LANES), 1), capacity) == here
        moves = [lax.rem(here - j + per, per) * capacity for j in range(per)]
        copies[3].wait()
        packed = jnp.dot(chosen, traces_ref[...], preferred_element_type=jnp.float32)
        for d in range(slots // capacity):
            at = slice(d * capacity, (d + 1) * capacity)
            tile = slice(d // per * LANES, (d // per + 1) * LANES)
            code = jnp.where(mine, pltpu.roll(sent[:SUBLANES, tile], moves[d % per], 1), 0.0)
            parts = [packed[at, c : c + LANES] for c in range(0, samples, LANES)]
            out_ref[d] = jnp.concatenate(parts + [code], axis=0).astype(jnp.bfloat16)
    for copy in copies[4:]:
        copy.wait()


def unpack(capacity, samples, got_ref):
    if not is_compact(capacity):
        kind = iota((SUBLANES, LANES), 1)
        weight = jnp.where(kind == 0, 64.0, jnp.where(kind == 1, 1.0, 0.0)).astype(jnp.bfloat16)
        value = lax.dot_general(
            weight, got_ref[:, samples:], (((1,), (1,)), ((), ())), preferred_element_type=jnp.float32
        )
        return got_ref[:, :samples], value[:1].astype(jnp.int32) - 64
    sources, per = got_ref.shape[0], LANES // capacity
    blocks = [got_ref[d].astype(jnp.float32) for d in range(sources)]
    tiles = samples // LANES
    values = []
    for first in range(0, sources, per):
        code = functools.reduce(lambda s, t: s + t, [blocks[d][tiles * capacity :] for d in range(first, first + per)])
        values.append(64.0 * code[:1] + code[1:2] - 64.0)
    columns = [
        jnp.concatenate([blocks[d][c * capacity : (c + 1) * capacity] for d in range(sources)], axis=0)
        for c in range(tiles)
    ]
    got = jnp.concatenate([column.astype(jnp.bfloat16) for column in columns], axis=1)
    return got, jnp.concatenate(values, axis=1).astype(jnp.int32)


def bin_kernel(capacity, got_ref, p1_ref, p2_ref, b_ref, diag_ref, *edge_refs):
    rows, tiles, cols, _ = b_ref.shape
    got, bin_of = unpack(capacity, tiles * LANES, got_ref)
    slots = got.shape[0]
    not_first_row = (lax.axis_index("inl") > 0).astype(jnp.float32)
    not_first_col = (lax.axis_index("xl") > 0).astype(jnp.float32)
    ones = jnp.ones((slots, LANES), jnp.bfloat16)
    first_col = jnp.where(iota((cols, LANES), 0) == 0, not_first_col, 0.0) - SHIFT
    for i in range(rows):
        place = (iota((cols, slots), 0) + i * cols == bin_of).astype(jnp.float32).astype(jnp.bfloat16)
        total = jnp.dot(place, got, preferred_element_type=jnp.float32)
        for c in range(tiles):
            b_ref[i, c] = total[:, c * LANES : (c + 1) * LANES]
        hits = jnp.dot(place, ones, preferred_element_type=jnp.float32)
        diag = 2.0 * hits + first_col
        diag_ref[i] = diag + not_first_row if i == 0 else diag
    write_edges(
        b_ref, lambda at: load(p1_ref, at), lambda i: load(p2_ref, i, slice(None)), *edge_refs
    )


def write_edges(v_ref, p1_last_row, p2_last_cols, row0_ref, row7_ref, col0_ref, col7_ref):
    rows, _, cols, _ = v_ref.shape
    for x in range(0, cols, SUBLANES):
        at = slice(x, x + SUBLANES)
        store(row0_ref, load_field(v_ref, 0, at), at)
        v = load_field(v_ref, rows - 1, at)
        store(row7_ref, add(v, dip_part(p1_last_row(at), *stencil(v))), at)
    for i in range(rows):
        store(col0_ref, load_field(v_ref, i, slice(0, 1)), slice(i, i + 1))
        v = load_field(v_ref, i, slice(cols - SUBLANES, cols))
        moved = add(v, dip_part(p2_last_cols(i), *stencil(v)))
        store(col7_ref, [t[SUBLANES - 1 :] for t in moved], slice(i, i + 1))


def apply_kernel(v_ref, p1_ref, p2_ref, diag_ref, out_ref, sums_ref, edge_ref):
    rows, tiles, cols, _ = v_ref.shape
    sub_index = iota((SUBLANES, LANES), 0)
    zero = [jnp.zeros((SUBLANES, LANES), jnp.float32)] * tiles
    edge_ref[...] = jnp.zeros_like(edge_ref)

    def roll_tiles(values, steps):
        return [pltpu.roll(t, steps, 0) for t in values]

    def filters(i, x, v, right, shifted_v, above, below, down_before):
        at = slice(x, x + SUBLANES)
        odd, even = shifted_v
        p1, p2 = load(p1_ref.at[i], at), load(p2_ref.at[i], at)
        first = sub(sub(below, v), dip_part(p1, odd, even))
        second = sub(sub(right, v), dip_part(p2, odd, even))
        down = roll_tiles(second, 1)
        left = [jnp.where(sub_index == 0, e, t) for e, t in zip(down_before, down)]
        a1, b1 = adjoint_terms(p1, first)
        a2, b2 = adjoint_terms(p2, second)
        a, b = add(a1, a2), add(b1, b2)
        diag = diag_ref.at[i][at, :]
        rest = [
            (diag * c + (f + s)) - ((f1 + s1) - y)
            for c, f, s, f1, s1, y in zip(v, above, left, first, second, b)
        ]
        return first, (rest, add(a, b), sub(b, a)), down

    def adjoint(i, x, pending):
        at = slice(x, x + SUBLANES)
        rest, up, down = pending
        out = [r - 0.5 * (u + d) for r, u, d in zip(rest, later(up), earlier(down))]
        out_row = out_ref.at[i]
        for c in range(tiles):
            out_row[c, at, :] = out[c]
        return dot(load_tiles(v_ref.at[i], at), out)

    vout, vv = zero[0], zero[0]
    for x in range(0, cols, GROUP):
        chunks = range(x, x + GROUP, SUBLANES)

        def fetch(i):
            below = [load_tiles(v_ref.at[i], slice(k, k + SUBLANES)) for k in chunks]
            return below, [stencil(tiles_of) for tiles_of in below]

        def all_filters(i, v, shifted_v, first, below):
            leads = [roll_tiles(tiles_of, SUBLANES - 1) for tiles_of in v]
            if x + GROUP < cols:
                following = load_tiles(v_ref.at[i], slice(x + GROUP, x + GROUP + SUBLANES))
                leads.append(roll_tiles(following, SUBLANES - 1))
            else:
                leads.append(zero)
            edge_row = edge_ref.at[i]
            down = load_tiles(edge_row, slice(None))
            firsts, pending = [], []
            for n, k in enumerate(chunks):
                right = [jnp.where(sub_index == SUBLANES - 1, e, t) for e, t in zip(leads[n + 1], leads[n])]
                made, waiting, down = filters(i, k, v[n], right, shifted_v[n], first[n], below[n], down)
                firsts.append(made)
                pending.append(waiting)
            for c in range(tiles):
                edge_row[c, :, :] = down[c]
            return firsts, pending

        def all_adjoint(i, own, pending):
            for k, waiting in zip(chunks, pending):
                own = own + adjoint(i, k, waiting)
            return own

        def norms(norm, v):
            for tiles_of in v:
                norm = norm + dot(tiles_of, tiles_of)
            return norm

        nothing = [zero] * len(chunks)
        v, shifted_v = fetch(0)
        below, below_shifted = fetch(1)
        first, pending = all_filters(0, v, shifted_v, nothing, below)

        def body(i, carry):
            v, shifted_v, first, pending, own, norm = carry
            below, below_shifted = fetch(i + 1)
            first, fresh = all_filters(i, v, shifted_v, first, below)
            own = all_adjoint(i - 1, own, pending)
            return below, below_shifted, first, fresh, own, norms(norm, v)

        carry = (below, below_shifted, first, pending, zero[0], norms(zero[0], v))
        v, shifted_v, first, pending, own, norm = lax.fori_loop(1, rows - 1, body, carry)
        first, fresh = all_filters(rows - 1, v, shifted_v, first, nothing)
        own = all_adjoint(rows - 1, all_adjoint(rows - 2, own, pending), fresh)
        vout, vv = vout + own, vv + norms(norm, v)
    sums_ref[0], sums_ref[1] = vout, vv


def halo_corrections(out_ref, p1_ref, p2_ref, below_ref, above_ref, right_ref, left_ref):
    rows, _, cols, _ = out_ref.shape
    last = rows - 1
    sub_index = iota((SUBLANES, LANES), 0)
    for x in range(0, cols, SUBLANES):
        at = slice(x, x + SUBLANES)
        store_field(out_ref, sub(load_field(out_ref, 0, at), load(above_ref, at)), 0, at)
        r = load(below_ref, at)
        moved = adjoint_finish(r, *adjoint_terms(load(p1_ref, last, at), r))
        store_field(out_ref, sub(load_field(out_ref, last, at), moved), last, at)
    for i in range(rows):
        at = slice(0, SUBLANES)
        r = [jnp.where(sub_index == 0, t, 0.0) for t in load(left_ref, slice(i, i + 1))]
        store_field(out_ref, sub(load_field(out_ref, i, at), r), i, at)
        at = slice(cols - SUBLANES, cols)
        r = [jnp.where(sub_index == SUBLANES - 1, t, 0.0) for t in load(right_ref, slice(i, i + 1))]
        moved = adjoint_finish(r, *adjoint_terms(load(p2_ref, i, at), r))
        store_field(out_ref, sub(load_field(out_ref, i, at), moved), i, at)


def settle(image_ref, p1_ref, p2_ref, below_ref, above_ref, right_ref, left_ref, row7_ref, col7_ref, out_ref):
    across = jnp.zeros((SUBLANES, LANES), jnp.float32)
    for mine, theirs in ((row7_ref, below_ref), (col7_ref, right_ref)):
        for x in range(0, mine.shape[0], SUBLANES):
            at = slice(x, x + SUBLANES)
            across = across + dot(load(mine, at), load(theirs, at))
    halo_corrections(out_ref, p1_ref, p2_ref, below_ref, above_ref, right_ref, left_ref)
    return across


def correct_kernel(
    image_ref, p1_ref, p2_ref, below_ref, above_ref, right_ref, left_ref, row7_ref, col7_ref,
    out_ref, across_ref, *edge_refs,
):
    across_ref[...] = settle(
        image_ref, p1_ref, p2_ref, below_ref, above_ref, right_ref, left_ref, row7_ref, col7_ref, out_ref
    )
    rows, _, cols, _ = out_ref.shape
    write_edges(
        out_ref,
        lambda at: load(p1_ref, rows - 1, at),
        lambda i: load(p2_ref, i, slice(cols - SUBLANES, cols)),
        *edge_refs,
    )


def moments_kernel(
    image_ref, p1_ref, p2_ref, below_ref, above_ref, right_ref, left_ref, row7_ref, col7_ref, *refs
):
    sums_refs, across_refs = refs[:ITERS], refs[ITERS : 2 * ITERS - 1]
    out_ref, message_ref = refs[2 * ITERS - 1 :]
    final = settle(
        image_ref, p1_ref, p2_ref, below_ref, above_ref, right_ref, left_ref, row7_ref, col7_ref, out_ref
    )
    m = []
    for sums_ref, across in zip(sums_refs, [ref[...] for ref in across_refs] + [final]):
        m.append(sums_ref[1])
        m.append(sums_ref[0] - 2.0 * across)
    sub_index, lane = iota((SUBLANES, LANES), 0), iota((SUBLANES, LANES), 1)
    block = jnp.zeros((SUBLANES, LANES), jnp.float32)
    for k, part in enumerate(m):
        block = jnp.where(sub_index == k, jnp.sum(part, axis=0, keepdims=True), block)
    total = jnp.sum(block, axis=1, keepdims=True)
    line = jnp.sum(jnp.where(sub_index == lane, total, 0.0), axis=0, keepdims=True)
    message_ref[...] = jnp.broadcast_to(line[None], message_ref.shape)


def coefficients(m):
    zero = jnp.zeros_like(m[0])
    model = [zero] * ITERS
    residual = [zero + 1.0] + [zero] * ITERS
    direction = [zero + 1.0] + [zero] * (ITERS - 1)
    norm_now = m[0]

    def inner(x, y, count):
        total = zero
        for i in range(count):
            for j in range(len(y)):
                if i + j < len(m):
                    total = total + x[i] * y[j] * m[i + j]
        return total

    for sweep in range(ITERS):
        image = [SHIFT * d for d in direction] + [zero]
        image = [image[0]] + [s + d for s, d in zip(image[1:], direction)]
        alpha = norm_now / inner(direction, image[: sweep + 2], sweep + 1)
        model = [s + alpha * d for s, d in zip(model, direction)]
        residual = [r - alpha * d for r, d in zip(residual, image)]
        if sweep + 1 < ITERS:
            norm_next = inner(residual, residual[: sweep + 2], sweep + 2)
            beta = norm_next / norm_now
            direction = [r + beta * d for r, d in zip(residual, direction)]
            norm_now = norm_next
    return [2.0 * s for s in model] + residual


def finish_kernel(parts_ref, b_ref, v1_ref, v2_ref, v3_ref, model_hbm, residual_hbm, model_ref, residual_ref, sems):
    rows, _, cols, _ = b_ref.shape
    line = jnp.sum(parts_ref[...], axis=0)
    sub_index, lane = iota((SUBLANES, LANES), 0), iota((SUBLANES, LANES), 1)
    total = jnp.sum(jnp.where(sub_index == lane, line, 0.0), axis=1, keepdims=True)
    total = jnp.broadcast_to(total, (SUBLANES, LANES))
    m = [jnp.broadcast_to(total[k : k + 1], (SUBLANES, LANES)) for k in range(2 * ITERS)]
    weights = coefficients(m)
    model, residual = weights[:ITERS], weights[ITERS:]

    def copies(i):
        return (
            pltpu.make_async_copy(model_ref.at[i], model_hbm.at[i], sems.at[0, i]),
            pltpu.make_async_copy(residual_ref.at[i], residual_hbm.at[i], sems.at[1, i]),
        )

    def body(i, carry):
        for x in range(0, cols, SUBLANES):
            at = slice(x, x + SUBLANES)
            b, v1, v2, v3 = (load_field(ref, i, at) for ref in (b_ref, v1_ref, v2_ref, v3_ref))
            store(model_ref, [model[0] * s + model[1] * t + model[2] * u for s, t, u in zip(b, v1, v2)], i, at)
            store(
                residual_ref,
                [(residual[0] * s + residual[1] * t) + (residual[2] * u + residual[3] * w) for s, t, u, w in zip(b, v1, v2, v3)],
                i, at,
            )
        for copy in copies(i):
            copy.start()
        return carry

    lax.fori_loop(0, rows, body, 0)
    for i in range(rows):
        for copy in copies(i):
            copy.wait()


def f32(*shape):
    return pltpu.VMEM(shape, jnp.float32)


def call(kernel, outs, *args, name, scratch=(), aliases=None, cost=None, ins=None, places=None):
    return pl.pallas_call(
        kernel,
        out_shape=outs,
        in_specs=ins or [IN_VMEM] * len(args),
        out_specs=places or [IN_VMEM] * len(outs),
        scratch_shapes=list(scratch),
        input_output_aliases=aliases or {},
        compiler_params=PARAMS,
        cost_estimate=cost,
        name=name,
    )(*args)


def in_hbm(array):
    return pltpu.with_memory_space_constraint(array, pltpu.HBM)


def per_device(traces, trace_owner, trace_cell, acquired, inline_dip, cross_dip):
    rows, cols, samples = inline_dip.shape
    devices = lax.axis_size("inl") * lax.axis_size("xl")
    held = traces.shape[0]
    capacity = max(2, 2 * held // devices)
    slots = devices * capacity
    message = (slots, samples + LANES)
    if is_compact(capacity):
        message = (devices, samples // LANES * capacity + SUBLANES, LANES)
    small = pltpu.VMEM((1, held), jnp.int32)
    inputs = (trace_owner.reshape(1, held), trace_cell[None], acquired[None], traces, inline_dip, cross_dip)
    sent, p1_last, p2_last = call(
        functools.partial(pack_kernel, capacity),
        [
            jax.ShapeDtypeStruct(message, jnp.bfloat16),
            f32(cols, samples),
            f32(rows, SUBLANES, samples),
        ],
        *(in_hbm(x) for x in inputs),
        name="pack", ins=[IN_HBM] * len(inputs),
        scratch=[small, small, small, pltpu.VMEM((held, samples), jnp.bfloat16), pltpu.SemaphoreType.DMA((6,))],
    )
    got = lax.all_to_all(sent, ("inl", "xl"), split_axis=0, concat_axis=0, tiled=True)
    edge_shapes = [f32(cols, samples), f32(cols, samples), f32(rows, samples), f32(rows, samples)]
    tile = f32(rows, samples // LANES, cols, LANES)
    b, diag, *edges = call(
        functools.partial(bin_kernel, capacity), [tile, f32(rows, cols, LANES)] + edge_shapes, got, p1_last, p2_last,
        name="bin",
    )
    fields, sums, products = [b], [], []
    cost = pl.CostEstimate(
        flops=60 * rows * cols * samples, bytes_accessed=16 * rows * cols * samples, transcendentals=0
    )
    for step in range(ITERS):
        row0, row7, col0, col7 = edges
        below = shifted(row0, "inl", -1)
        above = shifted(row7, "inl", 1)
        right = shifted(col0, "xl", -1)
        left = shifted(col7, "xl", 1)
        image, partial = call(
            apply_kernel,
            [tile, f32(2, SUBLANES, LANES)],
            fields[-1], inline_dip, cross_dip, diag,
            name="apply",
            scratch=[pltpu.VMEM((rows, samples // LANES, SUBLANES, LANES), jnp.float32)],
            cost=cost,
        )
        sums.append(partial)
        args = [image, inline_dip, cross_dip, below, above, right, left, row7, col7]
        if step + 1 < ITERS:
            image, across, *edges = call(
                correct_kernel, [tile, f32(SUBLANES, LANES)] + edge_shapes, *args, name="correct", aliases={0: 0}
            )
            products.append(across)
        else:
            image, message = call(
                moments_kernel, [tile, f32(devices, 1, LANES)], *args, *sums, *products,
                name="moments", aliases={0: 0},
            )
        fields.append(image)
    parts = lax.all_to_all(message, ("inl", "xl"), split_axis=0, concat_axis=0, tiled=True)
    out = jax.ShapeDtypeStruct((rows, cols, samples), jnp.float32)
    return tuple(
        call(
            finish_kernel, [out, out], parts, *fields,
            name="finish", places=[pl.BlockSpec(memory_space=pl.ANY)] * 2,
            scratch=[
                pltpu.VMEM((rows, cols, samples), jnp.float32),
                pltpu.VMEM((rows, cols, samples), jnp.float32),
                pltpu.SemaphoreType.DMA((2, rows)),
            ],
        )
    )


def solution(mesh):
    placed = (
        P(("inl", "xl"), None),
        P(("inl", "xl"), None),
        P(("inl", "xl")),
        P(("inl", "xl")),
        P("inl", "xl", None),
        P("inl", "xl", None),
    )
    return jax.shard_map(
        per_device,
        mesh=mesh,
        in_specs=placed,
        out_specs=(P("inl", "xl", None), P("inl", "xl", None)),
        check_vma=False,
    )
```

```python
import functools

import jax
import jax.numpy as jnp
from jax import lax
from jax.experimental import pallas as pl
from jax.experimental.pallas import tpu as pltpu
from jax.sharding import PartitionSpec as P

ITERS = 3
LANES = 128
SUBLANES = 8
GROUP = 32

SHIFT = 6.0
IN_VMEM = pl.BlockSpec(memory_space=pltpu.VMEM)
IN_HBM = pl.BlockSpec(memory_space=pltpu.HBM)
PARAMS = pltpu.CompilerParams(vmem_limit_bytes=16 << 20)


def shifted(value, axis, steps):
    count = lax.axis_size(axis)
    initial, last = (max(0, -steps), min(count, count - steps))
    return lax.ppermute(value, axis, [(source, source + steps) for source in range(initial, last)])


def iota(shape, dim):
    return lax.broadcasted_iota(jnp.int32, shape, dim)


def earlier(tiles):
    lane = iota(tiles[0].shape, 1)
    rolled = [pltpu.roll(tile, 1, 1) for tile in tiles]
    before = [jnp.zeros_like(tiles[0])] + rolled[:-1]
    return [jnp.where(lane == 0, edge, inner) for edge, inner in zip(before, rolled)]


def later(tiles):
    lane = iota(tiles[0].shape, 1)
    rolled = [pltpu.roll(tile, LANES - 1, 1) for tile in tiles]
    after = rolled[1:] + [jnp.zeros_like(tiles[0])]
    return [jnp.where(lane == LANES - 1, edge, inner) for edge, inner in zip(after, rolled)]


def stencil(v):
    em, ep = earlier(v), later(v)
    odd = [m - p for m, p in zip(em, ep)]
    even = [(m + p) - (c + c) for m, p, c in zip(em, ep, v)]
    return odd, even


def dip_part(p, odd, even):
    return [(0.5 * d) * (o + d * e) for d, o, e in zip(p, odd, even)]


def adjoint_terms(p, r):
    a = [(0.5 * d) * x for d, x in zip(p, r)]
    b = [d * x for d, x in zip(p, a)]
    return a, b


def adjoint_finish(r, a, b):
    up = later([x + y for x, y in zip(a, b)])
    down = earlier([y - x for x, y in zip(a, b)])
    return [(x + u) + (d - (y + y)) for x, u, d, y in zip(r, up, down, b)]


def load(ref, *index):
    count = ref.shape[-1] // LANES
    return [ref[(*index, slice(c * LANES, (c + 1) * LANES))] for c in range(count)]


def store(ref, tiles, *index):
    for c, tile in enumerate(tiles):
        ref[(*index, slice(c * LANES, (c + 1) * LANES))] = tile


def load_tiles(ref, at):
    return [ref[c, at, :] for c in range(ref.shape[0])]


def load_field(ref, i, at):
    return [ref[i, c, at, :] for c in range(ref.shape[1])]


def store_field(ref, tiles, i, at):
    for c, tile in enumerate(tiles):
        ref[i, c, at, :] = tile


def add(x, y):
    return [a + b for a, b in zip(x, y)]


def sub(x, y):
    return [a - b for a, b in zip(x, y)]


def dot(x, y):
    return functools.reduce(lambda s, t: s + t, [a * b for a, b in zip(x, y)])


def is_compact(capacity):
    return capacity % 16 == 0 and LANES % capacity == 0


def pack_kernel(
    capacity, owner_hbm, cell_hbm, live_hbm, traces_hbm, p1_hbm, p2_hbm, out_ref, p1_last_ref, p2_last_ref,
    owner_ref, cell_ref, live_ref, traces_ref, sems,
):
    held, samples = traces_ref.shape
    slots = lax.axis_size("inl") * lax.axis_size("xl") * capacity
    rows, cols, _ = p1_hbm.shape
    pairs = (
        (owner_hbm, owner_ref), (cell_hbm, cell_ref), (live_hbm, live_ref), (traces_hbm, traces_ref),
        (p1_hbm.at[rows - 1], p1_last_ref), (p2_hbm.at[:, pl.ds(cols - SUBLANES, SUBLANES)], p2_last_ref),
    )
    copies = [pltpu.make_async_copy(src, dst, sems.at[k]) for k, (src, dst) in enumerate(pairs)]
    for copy in copies:
        copy.start()
    for copy in copies[:3]:
        copy.wait()
    owner = owner_ref[...].astype(jnp.float32)
    row, col = iota((held, held), 0), iota((held, held), 1)
    owner_down = jnp.sum(jnp.where(row == col, owner, 0.0), axis=1, keepdims=True)
    earlier_same = (owner_down == owner) & (row < col)
    rank = jnp.sum(jnp.where(earlier_same, 1.0, 0.0), axis=0, keepdims=True)
    slot = jnp.where(live_ref[...] > 0, owner * capacity + rank, -1.0).astype(jnp.int32)
    chosen = (iota((slots, held), 0) == slot).astype(jnp.float32).astype(jnp.bfloat16)
    cell = cell_ref[...]
    kind = iota((LANES, held), 0)
    upper = (lax.shift_right_logical(cell, 6) + 1).astype(jnp.float32)
    lower = (cell & 63).astype(jnp.float32)
    codes = jnp.where(kind == 0, upper, jnp.where(kind == 1, lower, 0.0)).astype(jnp.bfloat16)
    if not is_compact(capacity):
        sent = lax.dot_general(chosen, codes, (((1,), (1,)), ((), ())), preferred_element_type=jnp.float32)
        out_ref[:, samples:] = sent.astype(jnp.bfloat16)
        copies[3].wait()
        packed = jnp.dot(chosen, traces_ref[...], preferred_element_type=jnp.float32)
        out_ref[:, :samples] = packed.astype(jnp.bfloat16)
    else:
        sent = lax.dot_general(codes[:16], chosen, (((1,), (1,)), ((), ())), preferred_element_type=jnp.float32)
        per = LANES // capacity
        here = lax.rem(lax.axis_index("inl") * lax.axis_size("xl") + lax.axis_index("xl"), per)
        mine = lax.div(iota((SUBLANES, LANES), 1), capacity) == here
        moves = [lax.rem(here - j + per, per) * capacity for j in range(per)]
        copies[3].wait()
        packed = jnp.dot(chosen, traces_ref[...], preferred_element_type=jnp.float32)
        for d in range(slots // capacity):
            at = slice(d * capacity, (d + 1) * capacity)
            tile = slice(d // per * LANES, (d // per + 1) * LANES)
            code = jnp.where(mine, pltpu.roll(sent[:SUBLANES, tile], moves[d % per], 1), 0.0)
            parts = [packed[at, c : c + LANES] for c in range(0, samples, LANES)]
            out_ref[d] = jnp.concatenate(parts + [code], axis=0).astype(jnp.bfloat16)
    for copy in copies[4:]:
        copy.wait()


def unpack(capacity, samples, got_ref):
    if not is_compact(capacity):
        kind = iota((SUBLANES, LANES), 1)
        weight = jnp.where(kind == 0, 64.0, jnp.where(kind == 1, 1.0, 0.0)).astype(jnp.bfloat16)
        value = lax.dot_general(
            weight, got_ref[:, samples:], (((1,), (1,)), ((), ())), preferred_element_type=jnp.float32
        )
        return got_ref[:, :samples], value[:1].astype(jnp.int32) - 64
    sources, per = got_ref.shape[0], LANES // capacity
    blocks = [got_ref[d].astype(jnp.float32) for d in range(sources)]
    tiles = samples // LANES
    values = []
    for first in range(0, sources, per):
        code = functools.reduce(lambda s, t: s + t, [blocks[d][tiles * capacity :] for d in range(first, first + per)])
        values.append(64.0 * code[:1] + code[1:2] - 64.0)
    columns = [
        jnp.concatenate([blocks[d][c * capacity : (c + 1) * capacity] for d in range(sources)], axis=0)
        for c in range(tiles)
    ]
    got = jnp.concatenate([column.astype(jnp.bfloat16) for column in columns], axis=1)
    return got, jnp.concatenate(values, axis=1).astype(jnp.int32)


def bin_kernel(capacity, got_ref, p1_ref, p2_ref, b_ref, diag_ref, *edge_refs):
    rows, tiles, cols, _ = b_ref.shape
    got, bin_of = unpack(capacity, tiles * LANES, got_ref)
    slots = got.shape[0]
    not_first_row = (lax.axis_index("inl") > 0).astype(jnp.float32)
    not_first_col = (lax.axis_index("xl") > 0).astype(jnp.float32)
    ones = jnp.ones((slots, LANES), jnp.bfloat16)
    first_col = jnp.where(iota((cols, LANES), 0) == 0, not_first_col, 0.0) - SHIFT
    for i in range(rows):
        place = (iota((cols, slots), 0) + i * cols == bin_of).astype(jnp.float32).astype(jnp.bfloat16)
        total = jnp.dot(place, got, preferred_element_type=jnp.float32)
        for c in range(tiles):
            b_ref[i, c] = total[:, c * LANES : (c + 1) * LANES]
        hits = jnp.dot(place, ones, preferred_element_type=jnp.float32)
        diag = 2.0 * hits + first_col
        diag_ref[i] = diag + not_first_row if i == 0 else diag
    write_edges(
        b_ref, lambda at: load(p1_ref, at), lambda i: load(p2_ref, i, slice(None)), *edge_refs
    )


def write_edges(v_ref, p1_last_row, p2_last_cols, row0_ref, row7_ref, col0_ref, col7_ref):
    rows, _, cols, _ = v_ref.shape
    for x in range(0, cols, SUBLANES):
        at = slice(x, x + SUBLANES)
        store(row0_ref, load_field(v_ref, 0, at), at)
        v = load_field(v_ref, rows - 1, at)
        store(row7_ref, add(v, dip_part(p1_last_row(at), *stencil(v))), at)
    for i in range(rows):
        store(col0_ref, load_field(v_ref, i, slice(0, 1)), slice(i, i + 1))
        v = load_field(v_ref, i, slice(cols - SUBLANES, cols))
        moved = add(v, dip_part(p2_last_cols(i), *stencil(v)))
        store(col7_ref, [t[SUBLANES - 1 :] for t in moved], slice(i, i + 1))


def apply_kernel(v_ref, p1_ref, p2_ref, diag_ref, out_ref, sums_ref, edge_ref):
    rows, tiles, cols, _ = v_ref.shape
    sub_index = iota((SUBLANES, LANES), 0)
    zero = [jnp.zeros((SUBLANES, LANES), jnp.float32)] * tiles
    edge_ref[...] = jnp.zeros_like(edge_ref)

    def roll_tiles(values, steps):
        return [pltpu.roll(t, steps, 0) for t in values]

    def filters(i, x, v, right, shifted_v, above, below, down_before):
        at = slice(x, x + SUBLANES)
        odd, even = shifted_v
        p1, p2 = load(p1_ref.at[i], at), load(p2_ref.at[i], at)
        first = sub(sub(below, v), dip_part(p1, odd, even))
        second = sub(sub(right, v), dip_part(p2, odd, even))
        down = roll_tiles(second, 1)
        left = [jnp.where(sub_index == 0, e, t) for e, t in zip(down_before, down)]
        a1, b1 = adjoint_terms(p1, first)
        a2, b2 = adjoint_terms(p2, second)
        a, b = add(a1, a2), add(b1, b2)
        diag = diag_ref.at[i][at, :]
        rest = [
            (diag * c + (f + s)) - ((f1 + s1) - (y + y))
            for c, f, s, f1, s1, y in zip(v, above, left, first, second, b)
        ]
        return first, (rest, add(a, b), sub(b, a)), down

    def adjoint(i, x, pending):
        at = slice(x, x + SUBLANES)
        rest, up, down = pending
        out = [r - (u + d) for r, u, d in zip(rest, later(up), earlier(down))]
        out_row = out_ref.at[i]
        for c in range(tiles):
            out_row[c, at, :] = out[c]
        return dot(load_tiles(v_ref.at[i], at), out)

    vout, vv = zero[0], zero[0]
    for x in range(0, cols, GROUP):
        chunks = range(x, x + GROUP, SUBLANES)

        def fetch(i):
            below = [load_tiles(v_ref.at[i], slice(k, k + SUBLANES)) for k in chunks]
            return below, [stencil(tiles_of) for tiles_of in below]

        def all_filters(i, v, shifted_v, first, below):
            leads = [roll_tiles(tiles_of, SUBLANES - 1) for tiles_of in v]
            if x + GROUP < cols:
                following = load_tiles(v_ref.at[i], slice(x + GROUP, x + GROUP + SUBLANES))
                leads.append(roll_tiles(following, SUBLANES - 1))
            else:
                leads.append(zero)
            edge_row = edge_ref.at[i]
            down = load_tiles(edge_row, slice(None))
            firsts, pending = [], []
            for n, k in enumerate(chunks):
                right = [jnp.where(sub_index == SUBLANES - 1, e, t) for e, t in zip(leads[n + 1], leads[n])]
                made, waiting, down = filters(i, k, v[n], right, shifted_v[n], first[n], below[n], down)
                firsts.append(made)
                pending.append(waiting)
            for c in range(tiles):
                edge_row[c, :, :] = down[c]
            return firsts, pending

        def all_adjoint(i, own, pending):
            for k, waiting in zip(chunks, pending):
                own = own + adjoint(i, k, waiting)
            return own

        def norms(norm, v):
            for tiles_of in v:
                norm = norm + dot(tiles_of, tiles_of)
            return norm

        nothing = [zero] * len(chunks)
        v, shifted_v = fetch(0)
        below, below_shifted = fetch(1)
        first, pending = all_filters(0, v, shifted_v, nothing, below)

        def body(i, carry):
            v, shifted_v, first, pending, own, norm = carry
            below, below_shifted = fetch(i + 1)
            first, fresh = all_filters(i, v, shifted_v, first, below)
            own = all_adjoint(i - 1, own, pending)
            return below, below_shifted, first, fresh, own, norms(norm, v)

        carry = (below, below_shifted, first, pending, zero[0], norms(zero[0], v))
        v, shifted_v, first, pending, own, norm = lax.fori_loop(1, rows - 1, body, carry)
        first, fresh = all_filters(rows - 1, v, shifted_v, first, nothing)
        own = all_adjoint(rows - 1, all_adjoint(rows - 2, own, pending), fresh)
        vout, vv = vout + own, vv + norms(norm, v)
    sums_ref[0], sums_ref[1] = vout, vv


def halo_corrections(out_ref, p1_ref, p2_ref, below_ref, above_ref, right_ref, left_ref):
    rows, _, cols, _ = out_ref.shape
    last = rows - 1
    sub_index = iota((SUBLANES, LANES), 0)
    for x in range(0, cols, SUBLANES):
        at = slice(x, x + SUBLANES)
        store_field(out_ref, sub(load_field(out_ref, 0, at), load(above_ref, at)), 0, at)
        r = load(below_ref, at)
        moved = adjoint_finish(r, *adjoint_terms(load(p1_ref, last, at), r))
        store_field(out_ref, sub(load_field(out_ref, last, at), moved), last, at)
    for i in range(rows):
        at = slice(0, SUBLANES)
        r = [jnp.where(sub_index == 0, t, 0.0) for t in load(left_ref, slice(i, i + 1))]
        store_field(out_ref, sub(load_field(out_ref, i, at), r), i, at)
        at = slice(cols - SUBLANES, cols)
        r = [jnp.where(sub_index == SUBLANES - 1, t, 0.0) for t in load(right_ref, slice(i, i + 1))]
        moved = adjoint_finish(r, *adjoint_terms(load(p2_ref, i, at), r))
        store_field(out_ref, sub(load_field(out_ref, i, at), moved), i, at)


def settle(image_ref, p1_ref, p2_ref, below_ref, above_ref, right_ref, left_ref, row7_ref, col7_ref, out_ref):
    across = jnp.zeros((SUBLANES, LANES), jnp.float32)
    for mine, theirs in ((row7_ref, below_ref), (col7_ref, right_ref)):
        for x in range(0, mine.shape[0], SUBLANES):
            at = slice(x, x + SUBLANES)
            across = across + dot(load(mine, at), load(theirs, at))
    halo_corrections(out_ref, p1_ref, p2_ref, below_ref, above_ref, right_ref, left_ref)
    return across


def correct_kernel(
    image_ref, p1_ref, p2_ref, below_ref, above_ref, right_ref, left_ref, row7_ref, col7_ref,
    out_ref, across_ref, *edge_refs,
):
    across_ref[...] = settle(
        image_ref, p1_ref, p2_ref, below_ref, above_ref, right_ref, left_ref, row7_ref, col7_ref, out_ref
    )
    rows, _, cols, _ = out_ref.shape
    write_edges(
        out_ref,
        lambda at: load(p1_ref, rows - 1, at),
        lambda i: load(p2_ref, i, slice(cols - SUBLANES, cols)),
        *edge_refs,
    )


def moments_kernel(
    image_ref, p1_ref, p2_ref, below_ref, above_ref, right_ref, left_ref, row7_ref, col7_ref, *refs
):
    sums_refs, across_refs = refs[:ITERS], refs[ITERS : 2 * ITERS - 1]
    out_ref, message_ref = refs[2 * ITERS - 1 :]
    final = settle(
        image_ref, p1_ref, p2_ref, below_ref, above_ref, right_ref, left_ref, row7_ref, col7_ref, out_ref
    )
    m = []
    for sums_ref, across in zip(sums_refs, [ref[...] for ref in across_refs] + [final]):
        m.append(sums_ref[1])
        m.append(sums_ref[0] - 2.0 * across)
    sub_index, lane = iota((SUBLANES, LANES), 0), iota((SUBLANES, LANES), 1)
    block = jnp.zeros((SUBLANES, LANES), jnp.float32)
    for k, part in enumerate(m):
        block = jnp.where(sub_index == k, jnp.sum(part, axis=0, keepdims=True), block)
    total = jnp.sum(block, axis=1, keepdims=True)
    line = jnp.sum(jnp.where(sub_index == lane, total, 0.0), axis=0, keepdims=True)
    message_ref[...] = jnp.broadcast_to(line[None], message_ref.shape)


def coefficients(m):
    zero = jnp.zeros_like(m[0])
    model = [zero] * ITERS
    residual = [zero + 1.0] + [zero] * ITERS
    direction = [zero + 1.0] + [zero] * (ITERS - 1)
    norm_now = m[0]

    def inner(x, y, count):
        total = zero
        for i in range(count):
            for j in range(len(y)):
                if i + j < len(m):
                    total = total + x[i] * y[j] * m[i + j]
        return total

    for sweep in range(ITERS):
        image = [SHIFT * d for d in direction] + [zero]
        image = [image[0]] + [s + d for s, d in zip(image[1:], direction)]
        alpha = norm_now / inner(direction, image[: sweep + 2], sweep + 1)
        model = [s + alpha * d for s, d in zip(model, direction)]
        residual = [r - alpha * d for r, d in zip(residual, image)]
        if sweep + 1 < ITERS:
            norm_next = inner(residual, residual[: sweep + 2], sweep + 2)
            beta = norm_next / norm_now
            direction = [r + beta * d for r, d in zip(residual, direction)]
            norm_now = norm_next
    return [2.0 * s for s in model] + residual


def finish_kernel(parts_ref, b_ref, v1_ref, v2_ref, v3_ref, model_hbm, residual_hbm, model_ref, residual_ref, sems):
    rows, _, cols, _ = b_ref.shape
    line = jnp.sum(parts_ref[...], axis=0)
    sub_index, lane = iota((SUBLANES, LANES), 0), iota((SUBLANES, LANES), 1)
    total = jnp.sum(jnp.where(sub_index == lane, line, 0.0), axis=1, keepdims=True)
    total = jnp.broadcast_to(total, (SUBLANES, LANES))
    m = [jnp.broadcast_to(total[k : k + 1], (SUBLANES, LANES)) for k in range(2 * ITERS)]
    weights = coefficients(m)
    model, residual = weights[:ITERS], weights[ITERS:]

    def copies(i):
        return (
            pltpu.make_async_copy(model_ref.at[i], model_hbm.at[i], sems.at[0, i]),
            pltpu.make_async_copy(residual_ref.at[i], residual_hbm.at[i], sems.at[1, i]),
        )

    def body(i, carry):
        for x in range(0, cols, SUBLANES):
            at = slice(x, x + SUBLANES)
            b, v1, v2, v3 = (load_field(ref, i, at) for ref in (b_ref, v1_ref, v2_ref, v3_ref))
            store(model_ref, [model[0] * s + model[1] * t + model[2] * u for s, t, u in zip(b, v1, v2)], i, at)
            store(
                residual_ref,
                [(residual[0] * s + residual[1] * t) + (residual[2] * u + residual[3] * w) for s, t, u, w in zip(b, v1, v2, v3)],
                i, at,
            )
        for copy in copies(i):
            copy.start()
        return carry

    lax.fori_loop(0, rows, body, 0)
    for i in range(rows):
        for copy in copies(i):
            copy.wait()


def f32(*shape):
    return pltpu.VMEM(shape, jnp.float32)


def call(kernel, outs, *args, name, scratch=(), aliases=None, cost=None, ins=None, places=None):
    return pl.pallas_call(
        kernel,
        out_shape=outs,
        in_specs=ins or [IN_VMEM] * len(args),
        out_specs=places or [IN_VMEM] * len(outs),
        scratch_shapes=list(scratch),
        input_output_aliases=aliases or {},
        compiler_params=PARAMS,
        cost_estimate=cost,
        name=name,
    )(*args)


def in_hbm(array):
    return pltpu.with_memory_space_constraint(array, pltpu.HBM)


def per_device(traces, trace_owner, trace_cell, acquired, inline_dip, cross_dip):
    rows, cols, samples = inline_dip.shape
    devices = lax.axis_size("inl") * lax.axis_size("xl")
    held = traces.shape[0]
    capacity = max(2, 2 * held // devices)
    slots = devices * capacity
    message = (slots, samples + LANES)
    if is_compact(capacity):
        message = (devices, samples // LANES * capacity + SUBLANES, LANES)
    small = pltpu.VMEM((1, held), jnp.int32)
    inputs = (trace_owner.reshape(1, held), trace_cell[None], acquired[None], traces, inline_dip, cross_dip)
    sent, p1_last, p2_last = call(
        functools.partial(pack_kernel, capacity),
        [
            jax.ShapeDtypeStruct(message, jnp.bfloat16),
            f32(cols, samples),
            f32(rows, SUBLANES, samples),
        ],
        *(in_hbm(x) for x in inputs),
        name="pack", ins=[IN_HBM] * len(inputs),
        scratch=[small, small, small, pltpu.VMEM((held, samples), jnp.bfloat16), pltpu.SemaphoreType.DMA((6,))],
    )
    got = lax.all_to_all(sent, ("inl", "xl"), split_axis=0, concat_axis=0, tiled=True)
    edge_shapes = [f32(cols, samples), f32(cols, samples), f32(rows, samples), f32(rows, samples)]
    tile = f32(rows, samples // LANES, cols, LANES)
    b, diag, *edges = call(
        functools.partial(bin_kernel, capacity), [tile, f32(rows, cols, LANES)] + edge_shapes, got, p1_last, p2_last,
        name="bin",
    )
    fields, sums, products = [b], [], []
    cost = pl.CostEstimate(
        flops=60 * rows * cols * samples, bytes_accessed=16 * rows * cols * samples, transcendentals=0
    )
    for step in range(ITERS):
        row0, row7, col0, col7 = edges
        below = shifted(row0, "inl", -1)
        above = shifted(row7, "inl", 1)
        right = shifted(col0, "xl", -1)
        left = shifted(col7, "xl", 1)
        image, partial = call(
            apply_kernel,
            [tile, f32(2, SUBLANES, LANES)],
            fields[-1], inline_dip, cross_dip, diag,
            name="apply",
            scratch=[pltpu.VMEM((rows, samples // LANES, SUBLANES, LANES), jnp.float32)],
            cost=cost,
        )
        sums.append(partial)
        args = [image, inline_dip, cross_dip, below, above, right, left, row7, col7]
        if step + 1 < ITERS:
            image, across, *edges = call(
                correct_kernel, [tile, f32(SUBLANES, LANES)] + edge_shapes, *args, name="correct", aliases={0: 0}
            )
            products.append(across)
        else:
            image, message = call(
                moments_kernel, [tile, f32(devices, 1, LANES)], *args, *sums, *products,
                name="moments", aliases={0: 0},
            )
        fields.append(image)
    parts = lax.all_to_all(message, ("inl", "xl"), split_axis=0, concat_axis=0, tiled=True)
    out = jax.ShapeDtypeStruct((rows, cols, samples), jnp.float32)
    return tuple(
        call(
            finish_kernel, [out, out], parts, *fields,
            name="finish", places=[pl.BlockSpec(memory_space=pl.ANY)] * 2,
            scratch=[
                pltpu.VMEM((rows, cols, samples), jnp.float32),
                pltpu.VMEM((rows, cols, samples), jnp.float32),
                pltpu.SemaphoreType.DMA((2, rows)),
            ],
        )
    )


def solution(mesh):
    placed = (
        P(("inl", "xl"), None),
        P(("inl", "xl"), None),
        P(("inl", "xl")),
        P(("inl", "xl")),
        P("inl", "xl", None),
        P("inl", "xl", None),
    )
    return jax.shard_map(
        per_device,
        mesh=mesh,
        in_specs=placed,
        out_specs=(P("inl", "xl", None), P("inl", "xl", None)),
        check_vma=False,
    )
```
